32 devices in a mesh: dp: 32 (over z, y, x, core).
Axes of the slice: x: 2, y: 2, z: 4, core: 2. Of those that a mesh axis runs over, the one named last changes fastest.
Arguments:
- frames: bfloat16 [16384, 768], P('dp'), may hold values from -6 to 6
- ln1_gain: bfloat16 [768], P('dp'), may hold values from 0.5 to 1.5
- ln1_shift: bfloat16 [768], P('dp'), may hold values from -1.75 to 1.75
- w_query: bfloat16 [768, 768], P('dp'), may hold values from -0.21875 to 0.21875
- b_query: bfloat16 [768], P('dp'), may hold values from -3 to 3
- w_key: bfloat16 [768, 768], P('dp'), may hold values from -0.21875 to 0.21875
- w_value: bfloat16 [768, 768], P('dp'), may hold values from -0.21875 to 0.21875
- b_value: bfloat16 [768], P('dp'), may hold values from -1.75 to 1.75
- w_out: bfloat16 [768, 768], P('dp'), may hold values from -2.5 to 2.5
- b_out: bfloat16 [768], P('dp'), may hold values from -1.75 to 1.75
- ln2_gain: bfloat16 [768], P('dp'), may hold values from 0.5 to 1.5
- ln2_shift: bfloat16 [768], P('dp'), may hold values from -1.75 to 1.75
- w_inner: bfloat16 [768, 3072], P('dp'), may hold values from -0.21875 to 0.21875
- b_inner: bfloat16 [3072], P('dp'), may hold values from -3 to 3
- w_outer: bfloat16 [3072, 768], P('dp'), may hold values from -0.109375 to 0.109375
- b_outer: bfloat16 [768], P('dp'), may hold values from -1.75 to 1.75
- bias_table: bfloat16 [3840], P('dp'), may hold values from -6 to 6
- layout: int32 [32], P('dp'), may hold values from 0 to 3, as said below
- valid: int32 [32, 4], P('dp'), may hold values from 65 to 384, as said below
- rel_index: int32 [1023], replicated, may hold values from 0 to 319
- cotangent: bfloat16 [16384, 768], P('dp'), may hold values from -6 to 6
Outputs:
- mixed: bfloat16 [16384, 768], P('dp')
- frames_grad: bfloat16 [16384, 768], P('dp')
- grad_ln1_gain: float32 [768], P('dp')
- grad_ln1_shift: float32 [768], P('dp')
- grad_w_query: float32 [768, 768], P('dp')
- grad_b_query: float32 [768], P('dp')
- grad_w_key: float32 [768, 768], P('dp')
- grad_w_value: float32 [768, 768], P('dp')
- grad_b_value: float32 [768], P('dp')
- grad_w_out: float32 [768, 768], P('dp')
- grad_b_out: float32 [768], P('dp')
- grad_ln2_gain: float32 [768], P('dp')
- grad_ln2_shift: float32 [768], P('dp')
- grad_w_inner: float32 [768, 3072], P('dp')
- grad_b_inner: float32 [3072], P('dp')
- grad_w_outer: float32 [3072, 768], P('dp')
- grad_b_outer: float32 [768], P('dp')
- grad_bias_table: float32 [3840], P('dp')
The draws below stay inside these ranges and needn't reach their ends.
Inputs may be any that keep to these rules, and one draw needn't show every extreme that they name: `layout`: every code 0 to 3 is taken by some group in every draw. For the s-th sequence of a group, valid holds more than half of its length and at most its length; entries of slots past a group's last sequence are ignored. Some sequence of 384 frames is valid in full in every draw.
All inputs are finite; a program needn't handle non-finite values.
Results may differ from the reference program's by a relative error of at most 0.013.
Values may be sent and summed in bfloat16 or wider, within the bound.
No kernel may reach another device: no remote copies, remote signals or barrier semaphores. Data moves between devices by JAX's collectives and lax.ppermute only.
A program may use at most 192 MiB of HBM per device.

```python
import jax
import jax.numpy as jnp
import numpy as np
from jax import lax

D = 768
HEADS = 12
FF = 3072
NBUCK = 320
UNIT = 128
SLOTS = 4
GROUPS = 32
TOKENS = 16384
SPAN = 1023


def device_codes(key):
    keys = jax.random.split(key, 2)
    roll = jax.random.randint(keys[0], (GROUPS,), 0, 20)
    codes = jnp.where(roll < 1, 0, jnp.where(roll < 3, 1, jnp.where(roll < 8, 2, 3)))
    first = jax.random.randint(keys[1], (), 0, GROUPS)
    place = (jnp.arange(GROUPS, dtype=jnp.int32) - first) % GROUPS
    codes = jnp.where(place < 4, place, codes).astype(jnp.int32)
    return (codes, place)


def draw_layout(key, part):
    codes, place = device_codes(key)
    return codes


def draw_valid(key, part):
    codes, place = device_codes(key)
    key = jax.random.fold_in(key, 5)
    unit_table = jnp.array([[3, 1, 1, 1], [2, 2, 1, 1], [2, 1, 1, 1], [1, 1, 1, 1]], dtype=jnp.int32)
    lengths = unit_table[codes] * UNIT
    cut = jax.random.randint(key, (GROUPS, SLOTS), 0, lengths // 2)
    counts = lengths - cut
    first_slot = (place[:, None] == 0) & (jnp.arange(SLOTS, dtype=jnp.int32)[None, :] == 0)
    return jnp.where(first_slot, lengths, counts).astype(jnp.int32)


def set_ends(values, own_key, least, largest):
    spot = [jax.random.randint(jax.random.fold_in(own_key, axis), (), 0, length) for axis, length in enumerate(values.shape)]
    widest = values.shape.index(max(values.shape))
    neighbour = spot[:widest] + [(spot[widest] + 1) % values.shape[widest]] + spot[widest + 1:]
    return values.at[tuple(spot)].set(least).at[tuple(neighbour)].set(largest)


def steps_of(key, extent, pieces, least, largest):
    loudness = 1.0
    for axis_at, parts in pieces:
        draws = jax.random.uniform(jax.random.fold_in(jax.random.fold_in(key, 6), axis_at), (parts,), jnp.float32, least / len(pieces), largest / len(pieces))
        loudness = loudness * jnp.repeat(jnp.exp(draws), extent[axis_at] // parts).reshape((-1,) + (1,) * (len(extent) - 1 - axis_at))
    return loudness


def bell_draw(key, extent, scale, most, shards=(), held_as=jnp.bfloat16):
    drawn = scale * jax.random.normal(key, extent, jnp.float32)
    if shards:
        drawn = drawn * steps_of(key, extent, shards, -0.22, 0.18)
    return jnp.clip(drawn, -most, most).astype(held_as)


def setup_inputs(seed: int = 0) -> dict:
    key_of = jax.random.split(jax.random.key(seed), 22)
    frames = bell_draw(key_of[0], (TOKENS, D), 1.0, 6.0, ((0, 32),))
    ln1_gain = jnp.clip(1.0 + 0.1 * jax.random.normal(key_of[1], (D,), jnp.float32), 0.5, 1.5).astype(jnp.bfloat16)
    ln1_shift = bell_draw(key_of[2], (D,), 0.3, 1.75, ((0, 32),))
    w_query = bell_draw(key_of[3], (D, D), D ** -0.5, 0.21875, ((0, 32),))
    b_query = bell_draw(key_of[4], (D,), 0.5, 3.0, ((0, 32),))
    w_key = bell_draw(key_of[5], (D, D), D ** -0.5, 0.21875, ((0, 32),))
    w_value = bell_draw(key_of[6], (D, D), D ** -0.5, 0.21875, ((0, 32),))
    b_value = bell_draw(key_of[7], (D,), 0.3, 1.75, ((0, 32),))
    w_out = bell_draw(key_of[8], (D, D), (D // 128) ** -0.5, 2.5, ((0, 32),))
    b_out = bell_draw(key_of[9], (D,), 0.3, 1.75, ((0, 32),))
    ln2_gain = jnp.clip(1.0 + 0.1 * jax.random.normal(key_of[10], (D,), jnp.float32), 0.5, 1.5).astype(jnp.bfloat16)
    ln2_shift = bell_draw(key_of[11], (D,), 0.3, 1.75, ((0, 32),))
    w_inner = bell_draw(key_of[12], (D, FF), D ** -0.5, 0.21875, ((0, 32),))
    b_inner = bell_draw(key_of[13], (FF,), 0.5, 3.0, ((0, 32),))
    w_outer = bell_draw(key_of[14], (FF, D), FF ** -0.5, 0.109375, ((0, 32),))
    b_outer = bell_draw(key_of[15], (D,), 0.3, 1.75, ((0, 32),))
    bias_table = bell_draw(key_of[16], (NBUCK * HEADS,), 1.0, 6.0, ((0, 32),))
    layout = draw_layout(jax.random.fold_in(key_of[21], 71), 0)
    valid = draw_valid(jax.random.fold_in(key_of[21], 71), 0)
    rel_index = set_ends(jax.random.randint(key_of[19], (SPAN,), 0, NBUCK), jax.random.fold_in(key_of[19], 1), 0, NBUCK - 1).astype(jnp.int32)
    cotangent = bell_draw(key_of[20], (TOKENS, D), 1.0, 6.0, ((0, 32),))
    return dict(frames=frames, ln1_gain=ln1_gain, ln1_shift=ln1_shift, w_query=w_query, b_query=b_query, w_key=w_key, w_value=w_value, b_value=b_value, w_out=w_out, b_out=b_out, ln2_gain=ln2_gain, ln2_shift=ln2_shift, w_inner=w_inner, b_inner=b_inner, w_outer=w_outer, b_outer=b_outer, bias_table=bias_table, layout=layout, valid=valid, rel_index=rel_index, cotangent=cotangent)


@jax.custom_vjp
def low(v):
    return lax.optimization_barrier(v.astype(jnp.bfloat16)).astype(jnp.float32)

@jax.custom_vjp
def low_back(v):
    return v

def low_keep(v):
    return (low(v), None)

def low_pass(kept, grad):
    return (grad,)

def back_keep(v):
    return (v, None)

def back_low(kept, grad):
    return (low(grad),)
low.defvjp(low_keep, low_pass)
low_back.defvjp(back_keep, back_low)
segment_units = np.array([[0, 0, 0, 1], [0, 0, 1, 1], [0, 0, 1, 2], [0, 1, 2, 3]], dtype=np.int32)
start_units = np.array([[0, 0, 0, 3], [0, 0, 2, 2], [0, 0, 2, 3], [0, 1, 2, 3]], dtype=np.int32)
masked_score = -1e+30

def layer_norm(inputs, gain, shift):
    centred = inputs - lax.optimization_barrier(jnp.mean(inputs, axis=-1, keepdims=True))
    spread = lax.optimization_barrier(jnp.mean(centred * centred, axis=-1, keepdims=True))
    return centred * lax.rsqrt(spread + 1e-05) * gain + shift

def toeplitz(vector, length):
    tiled = jnp.tile(vector, length)
    window = lax.slice_in_dim(tiled, length - 1, length - 1 + length * (2 * length - 2))
    return window.reshape(length, 2 * length - 2)[:, :length]

def allowed_pairs(layout_code, slot_valid, unit_rows):
    choose = jnp.arange(4, dtype=jnp.int32)[:, None] == layout_code
    seg_of_unit = lax.optimization_barrier(jnp.sum(jnp.where(choose, jnp.asarray(segment_units), 0), axis=0)).astype(jnp.int32)
    start_of_unit = lax.optimization_barrier(jnp.sum(jnp.where(choose, jnp.asarray(start_units), 0), axis=0)).astype(jnp.int32)
    segment = jnp.repeat(seg_of_unit, unit_rows)
    place = jnp.arange(4 * unit_rows, dtype=jnp.int32) - jnp.repeat(start_of_unit, unit_rows) * unit_rows
    slot_ids = jnp.arange(4, dtype=jnp.int32)
    limit = lax.optimization_barrier(jnp.sum(jnp.where(segment[:, None] == slot_ids[None, :], slot_valid[None, :], 0), axis=1))
    return (segment[:, None] == segment[None, :]) & (place < limit)[None, :]

def matmul(left, right):
    return jnp.dot(left, right, precision=lax.Precision.HIGHEST, preferred_element_type=jnp.float32)

def reference(frames, ln1_gain, ln1_shift, w_query, b_query, w_key, w_value, b_value, w_out, b_out, ln2_gain, ln2_shift, w_inner, b_inner, w_outer, b_outer, bias_table, layout, valid, rel_index, cotangent):
    row_count = 4 * UNIT
    head_size = D // HEADS
    scale = float(head_size) ** (-0.5)
    parameters = tuple((tensor.astype(jnp.float32) for tensor in (ln1_gain, ln1_shift, w_query, b_query, w_key, w_value, b_value, w_out, b_out, ln2_gain, ln2_shift, w_inner, b_inner, w_outer, b_outer, bias_table)))
    one_hot = (rel_index[:, None] == jnp.arange(NBUCK, dtype=jnp.int32)[None, :]).astype(jnp.float32)
    split_shape = (row_count, HEADS, head_size)

    def forward(parameters, inputs):
        first_gain, first_shift, query_weight, query_bias, key_weight, value_weight, value_bias, out_weight, out_bias, second_gain, second_shift, inner_weight, inner_bias, outer_weight, outer_bias, bias_grid = parameters
        bias_rows = matmul(one_hot, bias_grid.reshape(NBUCK, HEADS)).T
        relative = jax.vmap(lambda vector: toeplitz(vector, row_count))(bias_rows)

        def group_step(block, layout_code, slot_valid):
            allowed = allowed_pairs(layout_code, slot_valid, UNIT)
            normed_in = low(layer_norm(block, first_gain, first_shift))
            queries = low(low_back((matmul(normed_in, query_weight) + query_bias) * scale))
            key_rows = low(low_back(matmul(normed_in, key_weight)))
            values = low(low_back(matmul(normed_in, value_weight) + value_bias))
            scores = jnp.einsum('ihd,jhd->hij', queries.reshape(split_shape), key_rows.reshape(split_shape), precision=lax.Precision.HIGHEST)
            scores = low_back(scores + relative)
            scores = jnp.where(allowed[None], scores, masked_score)
            weights = low(jax.nn.softmax(scores, axis=-1))
            context = jnp.einsum('hij,jhd->ihd', weights, values.reshape(split_shape), precision=lax.Precision.HIGHEST)
            context = low(low_back(context.reshape(row_count, D)))
            attended = block + low_back(matmul(context, out_weight) + out_bias)
            normed_mid = low(layer_norm(attended, second_gain, second_shift))
            inner_sum = low_back(matmul(normed_mid, inner_weight) + inner_bias)
            activated = low(jax.nn.gelu(inner_sum, approximate=False))
            return attended + matmul(activated, outer_weight) + outer_bias
        checked = jax.checkpoint(group_step)

        def scan_step(carry, scan_item):
            return (carry, checked(*scan_item))
        blocks = inputs.reshape(GROUPS, row_count, D)
        _, outputs = lax.scan(scan_step, None, (blocks, layout, valid))
        return outputs.reshape(TOKENS, D)
    result, pull_back = jax.vjp(forward, parameters, frames.astype(jnp.float32))
    grads, frames_grad = pull_back(cotangent.astype(jnp.float32))
    return (result.astype(jnp.bfloat16), frames_grad.astype(jnp.bfloat16), grads[0], grads[1], grads[2], grads[3], grads[4], grads[5], grads[6], grads[7], grads[8], grads[9], grads[10], grads[11], grads[12], grads[13], grads[14], grads[15])
```

```python
import functools

import jax
import jax.numpy as jnp
import numpy as np
from jax import lax
from jax.experimental import pallas as pl
from jax.experimental.pallas import tpu as pltpu
from jax.sharding import PartitionSpec as P

HEADS = 12
LANES = 128
UNITS = 4
MASKED = -1e30
F32 = jnp.float32
BF16 = jnp.bfloat16
SEGMENT = ((0, 0, 0, 1), (0, 0, 1, 1), (0, 0, 1, 2), (0, 1, 2, 3))
START = ((0, 0, 0, 3), (0, 0, 2, 2), (0, 0, 2, 3), (0, 1, 2, 3))
VMEM_LIMIT = 56 * 1024 * 1024


def bit_orders(n):
    chip = [1 << k for k in range(1, n.bit_length() - 1)]
    low, high = chip[:2], chip[2:][::-1]
    return (high + low, high + low[::-1])


def gather_masks(bits):
    masks = [0]
    for bit in bits:
        masks = masks + [bit ^ m for m in masks]
    return masks


def scatter_masks(bits):
    masks = [0]
    for bit in bits:
        masks = [bit ^ m for m in masks] + masks
    return masks


def pairs(n, by_core):
    return [(i, i ^ by_core[i & 1]) for i in range(n)]


def gather(part, n):
    orders = bit_orders(n)
    held = part[None]
    for step, by_core in enumerate(zip(*orders)):
        got = lax.ppermute(held, "dp", pairs(n, by_core))
        if step < len(orders[0]) - 1:
            held = jnp.concatenate([held, got], axis=0)
    return (held, got, lax.ppermute(held, "dp", pairs(n, (1, 1))), lax.ppermute(got, "dp", pairs(n, (1, 1))))


def scatter(send, keep, n):
    orders = bit_orders(n)
    terms = [(keep, 0), (lax.ppermute(send, "dp", pairs(n, (1, 1))), 0)]
    half = n // 4

    def total(count):
        return sum(lax.slice_in_dim(t, at, at + count).astype(F32) for t, at in terms)

    for by_core in reversed(list(zip(*orders))):
        out = total(half).astype(BF16)
        terms = [(t, at + half) for t, at in terms]
        terms.append((lax.ppermute(out, "dp", pairs(n, by_core)), 0))
        half //= 2
    return total(1)[0]


def plan_tables(n):
    orders = bit_orders(n)
    me = lax.axis_index("dp")
    core = me & 1
    g = np.array([gather_masks(o) for o in orders], np.int32)
    s = np.array([scatter_masks(o) for o in orders], np.int32)
    other = np.array([[list(g[1 - c]).index(m) for m in g[c]] for c in (0, 1)], np.int32)
    inverse = np.zeros((2, n), np.int32)
    for c in (0, 1):
        for i, m in enumerate(s[c]):
            inverse[c, m] = i
    devices = jnp.arange(n, dtype=jnp.int32)
    chip_of = (me ^ jnp.asarray(g)[core]) >> 1
    other_place = jnp.asarray(other)[core]
    plane = devices & 1
    mask = (devices ^ me) & ~1
    scatter_place = jnp.asarray(inverse)[plane, mask]
    return me, core, chip_of, other_place, scatter_place


def assemble_kernel(meta, own0, own1, oth0, oth1, out, *, half):
    core = meta[0]
    i = pl.program_id(0)
    for place in range(2 * half):

        @pl.when(i == place)
        def _(place=place):
            mine = (own0 if place < half else own1)[place % half]
            j = meta[1 + 2 * half + place]
            pick0 = oth0[jnp.minimum(j, half - 1)]
            pick1 = oth1[jnp.maximum(j - half, 0)]
            theirs = jnp.where(j < half, pick0, pick1)
            first = jnp.where(core == 0, mine, theirs)
            second = jnp.where(core == 0, theirs, mine)
            out[0] = jnp.concatenate([first, second], axis=0)


def assemble(parts, plan, n):
    me, core, chip_of, other_place, _ = plan
    own0, own1, oth0, oth1 = parts
    half, rows, cols = own0.shape
    if rows % 8:
        mine = jnp.concatenate([own0, own1])
        theirs = jnp.concatenate([oth0, oth1])[other_place]
        both = jnp.where(core == 0, jnp.stack([mine, theirs], 1), jnp.stack([theirs, mine], 1))
        back = jnp.argsort(chip_of)
        return both[back].reshape(n * rows, cols)
    meta = jnp.concatenate([core[None], chip_of, other_place]).astype(jnp.int32)
    whole = pl.BlockSpec((half, rows, cols), lambda i, m: (0, 0, 0))
    out = pl.pallas_call(
        functools.partial(assemble_kernel, half=half),
        grid_spec=pltpu.PrefetchScalarGridSpec(
            num_scalar_prefetch=1,
            grid=(2 * half,),
            in_specs=[whole] * 4,
            out_specs=pl.BlockSpec((1, 2 * rows, cols), lambda i, m: (m[1 + i], 0, 0)),
        ),
        out_shape=jax.ShapeDtypeStruct((2 * half, 2 * rows, cols), BF16),
        compiler_params=pltpu.CompilerParams(vmem_limit_bytes=VMEM_LIMIT),
        name="assemble",
    )(meta, own0, own1, oth0, oth1)
    return out.reshape(n * rows, cols)


def split_natural(grad, plan, n):
    me, core, _, _, place = plan
    rows = grad.shape[0] // n
    blocks = grad.reshape(n // 2, 2, rows, grad.shape[1])
    mine = jnp.where(core == 0, blocks[:, 0], blocks[:, 1])
    theirs = jnp.where(core == 0, blocks[:, 1], blocks[:, 0])
    both = place.reshape(n // 2, 2)
    my_place = jnp.where(core == 0, both[:, 0], both[:, 1])
    their_place = jnp.where(core == 0, both[:, 1], both[:, 0])
    return theirs[jnp.argsort(their_place)], mine[jnp.argsort(my_place)]


def nn(a, b):
    return jnp.dot(a, b, preferred_element_type=F32)


def nt(a, b):
    return lax.dot_general(a, b, (((1,), (1,)), ((), ())), preferred_element_type=F32)


def tn(a, b):
    return lax.dot_general(a, b, (((0,), (0,)), ((), ())), preferred_element_type=F32)


def normalise(v):
    centred = v - jnp.mean(v, axis=-1, keepdims=True)
    r = lax.rsqrt(jnp.mean(centred * centred, axis=-1, keepdims=True) + 1e-05)
    return centred * r, r


def norm_backward(n, r, gain, e):
    eg = e * gain
    return r * (eg - jnp.mean(eg, axis=-1, keepdims=True) - n * jnp.mean(eg * n, axis=-1, keepdims=True))


def pick(table, code, u):
    out = jnp.int32(table[0][u])
    for c in range(1, 4):
        out = jnp.where(code == c, jnp.int32(table[c][u]), out)
    return out


def unit_range(meta, u, unit):
    code = meta[0]
    segment = pick(SEGMENT, code, u)
    start = pick(START, code, u)
    count = meta[1]
    for s in range(1, 4):
        count = jnp.where(segment == s, meta[1 + s], count)
    window = jnp.minimum(start, 1) * unit
    return start * unit, start * unit + count, window


def skewed(row, unit):
    wide = jnp.broadcast_to(row, (unit, row.shape[1]))
    return pltpu.roll(wide, row.shape[1] - (unit - 1), 1, stride=1, stride_axis=0)


def unskewed_sum(block, unit):
    width = block.shape[1]
    total = None
    for a in range(unit // 8):
        part = block[8 * a : 8 * a + 8]
        shift = (unit - 1 - 8 * a) % width
        part = pltpu.roll(part, shift, 1) if shift else part
        total = part if total is None else total + part
    out = total[0:1]
    for s in range(1, 8):
        out = out + pltpu.roll(total[s : s + 1], width - s, 1)
    return out


def put_blocks(place, core, send, keep, value, first, rows, columns):
    for at in range(value.shape[0] // rows):
        part = value[at * rows : (at + 1) * rows].astype(BF16)
        where = place[first + at]

        @pl.when(core == at % 2)
        def _(part=part, where=where):
            keep[where, :, columns] = part

        @pl.when(core != at % 2)
        def _(part=part, where=where):
            send[where, :, columns] = part


def attend_kernel(meta, frames, wqkv, vec, bias, q_out, k_out, v_out, nin_out, ctx_out, lse_out, base):
    rows, width = frames.shape
    unit = rows // UNITS
    window = rows - unit
    head = width // HEADS
    n, _ = normalise(frames[...].astype(F32))
    nin = (n * vec[0:1, :] + vec[1:2, :]).astype(BF16)
    nin_out[...] = nin
    q_out[...] = ((nn(nin, wqkv[:, 0:width]) + vec[2:3, :]) * (head ** -0.5)).astype(BF16)
    k_out[...] = nn(nin, wqkv[:, width : 2 * width]).astype(BF16)
    v_out[...] = (nn(nin, wqkv[:, 2 * width : 3 * width]) + vec[3:4, :]).astype(BF16)
    ranges = [unit_range(meta, u, unit) for u in range(UNITS)]
    column = lax.broadcasted_iota(jnp.int32, (1, window), 1)
    masks = [
        jnp.where((column + ws >= lo) & (column + ws < hi), 0.0, MASKED).astype(F32) for lo, hi, ws in ranges
    ]
    lane = lax.broadcasted_iota(jnp.int32, (unit, LANES), 1)
    lse_out[...] = jnp.zeros_like(lse_out)

    def pair(hp, carry):
        cols = pl.ds(pl.multiple_of(hp * LANES, LANES), LANES)
        for sub in range(2):
            h = 2 * hp + sub
            base[sub] = skewed(bias[pl.ds(h, 1), :], unit)
        for u in range(UNITS):
            lo, hi, ws = ranges[u]
            win = pl.ds(pl.multiple_of(ws, LANES), window)
            shift = pl.ds(pl.multiple_of(ws + (rows - unit) - u * unit, LANES), window)
            urows = slice(u * unit, (u + 1) * unit)
            kk = k_out[win, cols]
            vv = v_out[win, cols]
            qu = q_out[urows, cols]
            parts = []
            lses = lse_out[urows, :]
            for sub in range(2):
                qs = jnp.where((lane >= head) == bool(sub), qu, jnp.zeros_like(qu))
                s = nt(qs, kk) + (base[sub, :, shift] + masks[u])
                top = jnp.max(s, axis=1, keepdims=True)
                e = jnp.exp(s - top)
                tot = jnp.sum(e, axis=1, keepdims=True)
                parts.append(nn(e.astype(BF16), vv) * (1.0 / tot))
                lses = jnp.where(lane == 2 * hp + sub, top + jnp.log(tot), lses)
            lse_out[urows, :] = lses
            ctx_out[urows, cols] = jnp.where(lane < head, parts[0], parts[1]).astype(BF16)
        return carry

    lax.fori_loop(0, HEADS // 2, pair, 0)


def inner_kernel(
    place, frames, ctx, w_out, w_inner, vec, b_inner, cot, att_out, nmid_out, act_out, slope_out, send, keep, *, rows_ff, direct
):
    width = frames.shape[1]
    attended = frames[...].astype(F32) + nn(ctx[...], w_out[...]) + vec[4:5, :]
    att_out[...] = attended
    n, _ = normalise(attended)
    nmid_out[...] = (n * vec[5:6, :] + vec[6:7, :]).astype(BF16)
    core = place[0]

    def tile(t, carry):
        cols = pl.ds(pl.multiple_of(t * width, LANES), width)
        v = nn(nmid_out[...], w_inner[:, cols]) + b_inner[:, cols]
        phi = 0.5 * (1.0 + lax.erf(v * (0.5**0.5)))
        act = (v * phi).astype(BF16)
        act_out[:, cols] = act
        slope_out[:, cols] = (phi + v * jnp.exp(-0.5 * v * v) * 0.3989422804014327).astype(BF16)
        g = tn(act, cot[...])
        if direct:
            per = width // rows_ff
            for at in range(per):
                part = g[at * rows_ff : (at + 1) * rows_ff].astype(BF16)
                where = place[1 + t * per + at]

                @pl.when(core == at % 2)
                def _(part=part, where=where):
                    keep[where] = part

                @pl.when(core != at % 2)
                def _(part=part, where=where):
                    send[where] = part
        else:
            keep[cols, :] = g.astype(BF16)
        return carry

    lax.fori_loop(0, w_inner.shape[1] // width, tile, 0)


def outer_kernel(
    place, act, slope, nmid, attended, cot, w_outer, w_inner, w_out, ctx, vec,
    mixed_out, gatt_out, gctx_out, send, keep, gb_out, gvec_out, acc, gmid, *, rows, direct,
):
    width = nmid.shape[1]
    core = place[0]
    acc[...] = attended[...] + vec[7:8, :]
    gmid[...] = jnp.zeros_like(gmid)
    nblocks = width // rows

    def blocks(value, cols):
        if not direct:
            keep[:, cols] = value.astype(BF16)
            return
        for at in range(nblocks):
            part = value[at * rows : (at + 1) * rows].astype(BF16)
            where = place[1 + at]

            @pl.when(core == at % 2)
            def _(part=part, where=where):
                keep[where, :, cols] = part

            @pl.when(core != at % 2)
            def _(part=part, where=where):
                send[where, :, cols] = part

    def tile(t, carry):
        cols = pl.ds(pl.multiple_of(t * width, LANES), width)
        wo = w_outer[cols, :]
        acc[...] += nn(act[:, cols], wo)
        gi = (slope[:, cols].astype(F32) * nt(cot[...], wo)).astype(BF16)
        gb_out[:, cols] = jnp.sum(gi.astype(F32), axis=0, keepdims=True)
        gmid[...] += nt(gi, w_inner[:, cols])
        blocks(tn(nmid[...], gi), cols)
        return carry

    lax.fori_loop(0, w_inner.shape[1] // width, tile, 0)
    mixed_out[...] = acc[...].astype(BF16)
    n, r = normalise(attended[...])
    e = gmid[...]
    c32 = cot[...].astype(F32)
    gatt = c32 + norm_backward(n, r, vec[5:6, :], e)
    gatt_out[...] = gatt
    gbr = gatt.astype(BF16)
    gctx_out[...] = nt(gbr, w_out[...]).astype(BF16)
    blocks(tn(ctx[...], gbr), slice(w_inner.shape[1], w_inner.shape[1] + width))
    gvec_out[0:1, :] = jnp.sum(gbr.astype(F32), axis=0, keepdims=True)
    gvec_out[1:2, :] = jnp.sum(e * n, axis=0, keepdims=True)
    gvec_out[2:3, :] = jnp.sum(e, axis=0, keepdims=True)
    gvec_out[3:4, :] = jnp.sum(c32, axis=0, keepdims=True)
    gvec_out[4:8, :] = jnp.zeros_like(gvec_out[4:8, :])


def attend_back_kernel(
    meta, place, q, k, v, lse, ctx, gctx, bias_rev, nin, frames, gatt, wqkv, vec,
    fgrad_out, send, keep, gvec_out, grow_out,
    base, gbase, lse_t, delta_t, kt, dqkv, gk, gv, *, rows_d, direct,
):
    rows, width = frames.shape
    unit = rows // UNITS
    window = rows - unit
    head = width // HEADS
    core = place[0]
    lses = jnp.transpose(lse[...])
    for h in range(HEADS):
        lse_t[h] = lses[h : h + 1]
    prod = gctx[...].astype(F32) * ctx[...].astype(F32)
    sel_row = lax.broadcasted_iota(jnp.int32, (16, width), 0)
    sel_col = lax.broadcasted_iota(jnp.int32, (16, width), 1)
    sel = jnp.where((sel_col >= sel_row * head) & (sel_col < (sel_row + 1) * head), 1.0, 0.0).astype(BF16)
    high = prod.astype(BF16)
    low = (prod - high.astype(F32)).astype(BF16)
    deltas = nt(sel, high) + nt(sel, low)
    for h in range(HEADS):
        delta_t[h] = deltas[h : h + 1]
    ranges = [unit_range(meta, u, unit) for u in range(UNITS)]
    row_at = lax.broadcasted_iota(jnp.int32, (window, LANES), 0)
    lane = lax.broadcasted_iota(jnp.int32, (unit, LANES), 1)
    sub_lane = lax.broadcasted_iota(jnp.int32, (LANES, unit), 0)

    def pair(hp, carry):
        at = pl.multiple_of(hp * LANES, LANES)
        cols = pl.ds(at, LANES)
        kt[...] = jnp.transpose(k[:, cols])
        gk[...] = jnp.zeros_like(gk)
        gv[...] = jnp.zeros_like(gv)
        gbase[...] = jnp.zeros_like(gbase)
        for sub in range(2):
            base[sub] = skewed(bias_rev[pl.ds(2 * hp + sub, 1), :], unit)
        for u in range(UNITS):
            lo, hi, ws = ranges[u]
            ws = pl.multiple_of(ws, LANES)
            win = pl.ds(ws, window)
            urows = slice(u * unit, (u + 1) * unit)
            mask = jnp.where((row_at + ws >= lo) & (row_at + ws < hi), 0.0, MASKED).astype(F32)
            kk = k[win, cols]
            vv = v[win, cols]
            qu = q[urows, cols]
            gu = gctx[urows, cols]
            gk_win = gk[win, :]
            gv_win = gv[win, :]
            gq = []
            for sub in range(2):
                h = 2 * hp + sub
                mine = (lane >= head) == bool(sub)
                qs = jnp.where(mine, qu, jnp.zeros_like(qu))
                gs = jnp.where(mine, gu, jnp.zeros_like(gu))
                offsets = [
                    pl.ds(pl.multiple_of((rows - unit) + u * unit - ws - jb * unit, LANES), unit)
                    for jb in range(UNITS - 1)
                ]
                rel = jnp.concatenate([base[sub, :, o] for o in offsets], axis=0)
                s = nt(kk, qs) + rel + mask
                p = jnp.exp(s - lse_t[h, :, urows])
                gp = nt(vv, gs)
                ds = (p * (gp - delta_t[h, :, urows])).astype(BF16)
                gv_win = gv_win + nn(p.astype(BF16), gs)
                gk_win = gk_win + nn(ds, qs)
                gq.append(nn(kt[:, win], ds))
                d32 = ds.astype(F32)
                for jb, o in enumerate(offsets):
                    gbase[sub, :, o] += d32[jb * unit : (jb + 1) * unit]
            gk[win, :] = gk_win
            gv[win, :] = gv_win
            gq_t = jnp.where(sub_lane < head, gq[0], gq[1])
            dqkv[urows, cols] = jnp.transpose(gq_t).astype(BF16) * BF16(head ** -0.5)
        dqkv[:, pl.ds(width + at, LANES)] = gk[...].astype(BF16)
        dqkv[:, pl.ds(2 * width + at, LANES)] = gv[...].astype(BF16)
        for sub in range(2):
            grow_out[pl.ds(2 * hp + sub, 1), :] = unskewed_sum(gbase[sub], unit)
        return carry

    lax.fori_loop(0, HEADS // 2, pair, 0)
    grad_in = jnp.zeros((rows, width), F32)
    for part in range(3):
        cols = slice(part * width, (part + 1) * width)
        d = dqkv[:, cols]
        grad_in = grad_in + nt(d, wqkv[:, cols])
        g = tn(nin[...], d)
        if direct:
            for at in range(width // rows_d):
                block = g[at * rows_d : (at + 1) * rows_d].astype(BF16)
                where = place[1 + at]

                @pl.when(core == at % 2)
                def _(block=block, where=where):
                    keep[where, :, cols] = block

                @pl.when(core != at % 2)
                def _(block=block, where=where):
                    send[where, :, cols] = block
        else:
            keep[:, cols] = g.astype(BF16)
    n, r = normalise(frames[...].astype(F32))
    fgrad_out[...] = (gatt[...] + norm_backward(n, r, vec[0:1, :], grad_in)).astype(BF16)
    gvec_out[0:1, :] = jnp.sum(grad_in * n, axis=0, keepdims=True)
    gvec_out[1:2, :] = jnp.sum(grad_in, axis=0, keepdims=True)
    gvec_out[2:3, :] = jnp.sum(dqkv[:, 0:width].astype(F32), axis=0, keepdims=True)
    gvec_out[3:4, :] = jnp.sum(dqkv[:, 2 * width :].astype(F32), axis=0, keepdims=True)
    gvec_out[4:8, :] = jnp.zeros_like(gvec_out[4:8, :])


def run_kernel(kernel, name, scalars, arrays, outs, scratch=()):
    spec = pl.BlockSpec(memory_space=pltpu.VMEM)
    smem = pl.BlockSpec(memory_space=pltpu.SMEM)
    return pl.pallas_call(
        kernel,
        in_specs=[smem] * len(scalars) + [spec] * len(arrays),
        out_specs=[spec] * len(outs),
        out_shape=[jax.ShapeDtypeStruct(s, d) for s, d in outs],
        scratch_shapes=list(scratch),
        compiler_params=pltpu.CompilerParams(vmem_limit_bytes=VMEM_LIMIT),
        name=name,
    )(*scalars, *arrays)


def on_device(
    frames, ln1_gain, ln1_shift, w_query, b_query, w_key, w_value, b_value, w_out, b_out, ln2_gain, ln2_shift,
    w_inner, b_inner, w_outer, b_outer, bias_table, layout, valid, rel_index, cotangent, *, n,
):
    rows, width = frames.shape
    rows_d = w_query.shape[0]
    rows_ff = w_outer.shape[0]
    ff = w_inner.shape[1]
    span = rel_index.shape[0]
    plan = plan_tables(n)
    me, core, chip_of, other_place, scatter_place = plan
    direct = rows_d % 8 == 0 and rows_ff % 16 == 0
    place = jnp.concatenate([core[None], scatter_place]).astype(jnp.int32)
    meta = jnp.concatenate([layout, valid.reshape(-1)]).astype(jnp.int32)

    small_d = jnp.stack([ln1_gain, ln1_shift, b_query, b_value, b_out, ln2_gain, ln2_shift, b_outer])
    flat = jnp.concatenate([small_d.reshape(-1), b_inner, bias_table])
    per = flat.shape[0] // rows_d
    small = jnp.pad(flat.reshape(rows_d, per), ((0, 0), (0, LANES - per)))
    first = assemble(gather(jnp.concatenate([w_query, w_key, w_value, small], axis=1), n), plan, n)
    second = assemble(gather(jnp.concatenate([w_inner, w_out], axis=1), n), plan, n)
    third = assemble(gather(w_outer, n), plan, n)
    flats = first[:, 3 * width : 3 * width + per].reshape(n, rows_d * per)
    vec = flats[:, : 8 * rows_d].reshape(n, 8, rows_d).transpose(1, 0, 2).reshape(8, width).astype(F32)
    inner_bias = flats[:, 8 * rows_d : 8 * rows_d + rows_ff].reshape(1, ff).astype(F32)
    table = flats[:, 8 * rows_d + rows_ff :].reshape(-1, HEADS)
    buckets = table.shape[0]
    index = jnp.pad(rel_index, (0, 1), constant_values=-1)
    index_rev = jnp.pad(rel_index[::-1], (0, 1), constant_values=-1)
    ids = jnp.arange(buckets, dtype=jnp.int32)
    hot = (ids[:, None] == index[None, :]).astype(BF16)
    hot_rev = (ids[:, None] == index_rev[None, :]).astype(BF16)
    wide = jnp.pad(table, ((0, 0), (0, 16 - HEADS)))
    bias = tn(wide, hot)
    bias_rev = tn(wide, hot_rev)

    q, k, v, nin, ctx, lse = run_kernel(
        attend_kernel, "attend", [meta], [frames, first, vec, bias],
        [((rows, width), BF16)] * 5 + [((rows, LANES), F32)],
        [pltpu.VMEM((2, rows // UNITS, span + 1), F32)],
    )
    if direct:
        part_ff = [((n // 2, rows_ff, width), BF16)] * 2
        part_io = [((n // 2, rows_d, ff + width), BF16)] * 2
        part_qkv = [((n // 2, rows_d, 3 * width), BF16)] * 2
    else:
        part_ff = [((8, LANES), BF16), ((ff, width), BF16)]
        part_io = [((8, LANES), BF16), ((width, ff + width), BF16)]
        part_qkv = [((8, LANES), BF16), ((width, 3 * width), BF16)]

    def split(send, keep):
        return (send, keep) if direct else split_natural(keep, plan, n)

    w_out_all = second[:, ff:]
    w_inner_all = second[:, :ff]
    attended, nmid, act, slope, ff_send, ff_keep = run_kernel(
        functools.partial(inner_kernel, rows_ff=rows_ff, direct=direct), "inner", [place],
        [frames, ctx, w_out_all, w_inner_all, vec, inner_bias, cotangent],
        [((rows, width), F32), ((rows, width), BF16), ((rows, ff), BF16), ((rows, ff), BF16)] + part_ff,
    )
    sum_outer = scatter(*split(ff_send, ff_keep), n)
    mixed, gatt, gctx, io_send, io_keep, gb_inner, gvec2 = run_kernel(
        functools.partial(outer_kernel, rows=rows_d, direct=direct), "outer", [place],
        [act, slope, nmid, attended, cotangent, third, w_inner_all, w_out_all, ctx, vec],
        [((rows, width), BF16), ((rows, width), F32), ((rows, width), BF16)] + part_io
        + [((1, ff), F32), ((8, width), F32)],
        [pltpu.VMEM((rows, width), F32), pltpu.VMEM((rows, width), F32)],
    )
    sum_io = scatter(*split(io_send, io_keep), n)
    unit = rows // UNITS
    fgrad, qkv_send, qkv_keep, gvec1, grow = run_kernel(
        functools.partial(attend_back_kernel, rows_d=rows_d, direct=direct), "attend_back", [meta, place],
        [q, k, v, lse, ctx, gctx, bias_rev, nin, frames, gatt, first, vec],
        [((rows, width), BF16)] + part_qkv + [((8, width), F32), ((16, span + 1), F32)],
        [
            pltpu.VMEM((2, unit, span + 1), F32),
            pltpu.VMEM((2, unit, span + 1), F32),
            pltpu.VMEM((HEADS, 1, rows), F32),
            pltpu.VMEM((HEADS, 1, rows), F32),
            pltpu.VMEM((LANES, rows), BF16),
            pltpu.VMEM((rows, 3 * width), BF16),
            pltpu.VMEM((rows, LANES), F32),
            pltpu.VMEM((rows, LANES), F32),
        ],
    )
    sum_qkv = scatter(*split(qkv_send, qkv_keep), n)
    gtable = lax.dot_general(
        hot_rev.astype(F32), grow, (((1,), (1,)), ((), ())), precision=lax.Precision.HIGHEST, preferred_element_type=F32
    )[:, :HEADS]
    gsmall = jnp.stack([gvec1[0], gvec1[1], gvec1[2], gvec1[3], gvec2[0], gvec2[1], gvec2[2], gvec2[3]])
    gsmall = gsmall.reshape(8, n, rows_d).transpose(1, 0, 2).reshape(n, 8 * rows_d)
    gflat = jnp.concatenate([gsmall, gb_inner.reshape(n, rows_ff), gtable.reshape(n, -1)], axis=1)
    gflat = jnp.pad(gflat, ((0, 0), (0, -gflat.shape[1] % LANES))).astype(BF16)
    sum_flat = scatter(*split_natural(gflat, plan, n), n)[0]
    vecs = sum_flat[: 8 * rows_d].reshape(8, rows_d)
    sum_b_inner = sum_flat[8 * rows_d : 8 * rows_d + rows_ff]
    sum_table = sum_flat[8 * rows_d + rows_ff : 8 * rows_d + rows_ff + bias_table.shape[0]]
    return (
        mixed, fgrad, vecs[0], vecs[1],
        sum_qkv[:, :width], vecs[2], sum_qkv[:, width : 2 * width], sum_qkv[:, 2 * width :], vecs[3],
        sum_io[:, ff:], vecs[4], vecs[5], vecs[6],
        sum_io[:, :ff], sum_b_inner, sum_outer, vecs[7], sum_table,
    )


def solution(mesh):
    row, two = P("dp"), P("dp", None)
    in_specs = (two, row, row, two, row, two, two, row, two, row, row, row, two, row, two, row, row, row, two, P(), two)
    out_specs = (two, two, row, row, two, row, two, two, row, two, row, row, row, two, row, two, row, row)
    return jax.shard_map(
        functools.partial(on_device, n=mesh.shape["dp"]),
        mesh=mesh, in_specs=in_specs, out_specs=out_specs, check_vma=False,
    )
```

```python
import functools
import math

import jax
import jax.numpy as jnp
import numpy as np
from jax import lax
from jax.experimental import pallas as pl
from jax.experimental.pallas import tpu as pltpu
from jax.sharding import PartitionSpec as P

HEADS = 12
LANES = 128
UNITS = 4
MASKED = -1e30
F32 = jnp.float32
BF16 = jnp.bfloat16
SEGMENT = ((0, 0, 0, 1), (0, 0, 1, 1), (0, 0, 1, 2), (0, 1, 2, 3))
START = ((0, 0, 0, 3), (0, 0, 2, 2), (0, 0, 2, 3), (0, 1, 2, 3))
MIB = 1024 * 1024


def bit_orders(n):
    chip = [1 << k for k in range(1, n.bit_length() - 1)]
    low, high = chip[:2], chip[2:][::-1]
    return (high + low, high + low[::-1])


def gather_masks(bits):
    masks = [0]
    for bit in bits:
        masks = masks + [bit ^ m for m in masks]
    return masks


def scatter_masks(bits):
    masks = [0]
    for bit in bits:
        masks = [bit ^ m for m in masks] + masks
    return masks


def pairs(n, by_core):
    return [(i, i ^ by_core[i & 1]) for i in range(n)]


class Order:
    def __init__(self):
        self.last = None

    def after(self, *arrays):
        if self.last is None:
            return arrays
        return lax.optimization_barrier((*arrays, self.last))[:-1]

    def did(self, array):
        self.last = array


class Gather:
    def __init__(self, part, n, order):
        self.n = n
        self.order = order
        self.steps = list(zip(*bit_orders(n)))
        self.held = part[None]
        self.got = lax.ppermute(self.held, "dp", pairs(n, self.steps.pop(0)))

    def step(self):
        pair = self.order.after(self.held, self.got)
        self.held = jnp.concatenate(pair, axis=0)
        self.order.did(self.held)
        self.got = lax.ppermute(self.held, "dp", pairs(self.n, self.steps.pop(0)))
        return self

    def finish(self):
        while self.steps:
            self.step()
        swap = pairs(self.n, (1, 1))
        return (self.held, self.got, lax.ppermute(self.held, "dp", swap), lax.ppermute(self.got, "dp", swap))


class Scatter:
    def __init__(self, n, order):
        self.n = n
        self.order = order
        self.parts = []
        self.terms = []
        self.at = 0
        self.steps = list(reversed(list(zip(*bit_orders(n)))))
        self.half = n // 4

    def add(self, send, keep):
        self.parts.append((keep, lax.ppermute(send, "dp", pairs(self.n, (1, 1)))))
        return self

    def total(self, count, dtype):
        flat = [t for part in self.parts for t in part] + [t for t, _ in self.terms]
        flat = list(self.order.after(*flat))
        at = self.at
        cut = [lax.slice_in_dim(t, at, at + count).astype(F32) for t in flat[: 2 * len(self.parts)]]
        out = [cut[2 * i] + cut[2 * i + 1] for i in range(len(self.parts))]
        out = out[0] if len(out) == 1 else jnp.concatenate(out, axis=-1)
        for t, (_, first) in zip(flat[2 * len(self.parts) :], self.terms):
            out = out + lax.slice_in_dim(t, at - first, at - first + count).astype(F32)
        out = out.astype(dtype)
        self.order.did(out)
        return out

    def step(self):
        by_core = self.steps.pop(0)
        out = self.total(self.half, BF16)
        self.at += self.half
        self.terms.append((lax.ppermute(out, "dp", pairs(self.n, by_core)), self.at))
        self.half //= 2

    def finish(self):
        while self.steps:
            self.step()
        return self.total(1, F32)[0]


def plan_tables(n):
    orders = bit_orders(n)
    me = lax.axis_index("dp")
    core = me & 1
    g = np.array([gather_masks(o) for o in orders], np.int32)
    s = np.array([scatter_masks(o) for o in orders], np.int32)
    inverse = np.zeros((2, n), np.int32)
    for c in (0, 1):
        for i, m in enumerate(s[c]):
            inverse[c, m] = i
    devices = jnp.arange(n, dtype=jnp.int32)
    chips = (me ^ jnp.where(core == 0, jnp.asarray(g[0]), jnp.asarray(g[1]))) >> 1
    mask = (devices ^ me) & ~1
    place = jnp.sum(jnp.where(mask[:, None] == devices[None, :], jnp.asarray(inverse)[np.arange(n) % 2], 0), axis=1)
    return core, chips, place


def crossed_places(n):
    first, second = (gather_masks(o) for o in bit_orders(n))
    places = [second.index(m) for m in first]
    assert places == [first.index(m) for m in second]
    return places


def gathered(parts, plan, n):
    core, chips, _ = plan
    mine = jnp.concatenate(parts[:2])
    theirs = jnp.concatenate(parts[2:])[np.array(crossed_places(n))]
    both = jnp.where(core == 0, jnp.stack([mine, theirs], 1), jnp.stack([theirs, mine], 1))
    return both[jnp.argsort(chips)].reshape(n * mine.shape[1], mine.shape[2])


def split_natural(grad, plan, n):
    core, _, place = plan
    rows = grad.shape[0] // n
    blocks = grad.reshape(n // 2, 2, rows, grad.shape[1])
    mine = jnp.where(core == 0, blocks[:, 0], blocks[:, 1])
    theirs = jnp.where(core == 0, blocks[:, 1], blocks[:, 0])
    both = place.reshape(n // 2, 2)
    my_place = jnp.where(core == 0, both[:, 0], both[:, 1])
    their_place = jnp.where(core == 0, both[:, 1], both[:, 0])
    return theirs[jnp.argsort(their_place)], mine[jnp.argsort(my_place)]


def nn(a, b):
    return jnp.dot(a, b, preferred_element_type=F32)


def nt(a, b):
    return lax.dot_general(a, b, (((1,), (1,)), ((), ())), preferred_element_type=F32)


def tn(a, b):
    return lax.dot_general(a, b, (((0,), (0,)), ((), ())), preferred_element_type=F32)


def normalise(v):
    centred = v - jnp.mean(v, axis=-1, keepdims=True)
    r = lax.rsqrt(jnp.mean(centred * centred, axis=-1, keepdims=True) + 1e-05)
    return centred * r, r


def norm_backward(n, r, gain, e):
    eg = e * gain
    return r * (eg - jnp.mean(eg, axis=-1, keepdims=True) - n * jnp.mean(eg * n, axis=-1, keepdims=True))


def pick(table, code, u):
    out = jnp.int32(table[0][u])
    for c in range(1, 4):
        out = jnp.where(code == c, jnp.int32(table[c][u]), out)
    return out


def unit_range(meta, u, unit):
    code = meta[0]
    segment = pick(SEGMENT, code, u)
    start = pick(START, code, u)
    count = meta[1]
    for s in range(1, 4):
        count = jnp.where(segment == s, meta[1 + s], count)
    window = jnp.minimum(start, 1) * unit
    return start * unit, start * unit + count, window


def skewed(row, unit):
    wide = jnp.broadcast_to(row, (unit, row.shape[1]))
    return pltpu.roll(wide, row.shape[1] - (unit - 1), 1, stride=1, stride_axis=0)


def unskewed_sum(block, unit):
    width = block.shape[1]
    total = None
    for a in range(unit // 8):
        part = block[8 * a : 8 * a + 8]
        shift = (unit - 1 - 8 * a) % width
        part = pltpu.roll(part, shift, 1) if shift else part
        total = part if total is None else total + part
    out = total[0:1]
    for s in range(1, 8):
        out = out + pltpu.roll(total[s : s + 1], width - s, 1)
    return out


def unpack(core, chips, parts, crossed, out, columns):
    half = parts[0].shape[0]
    for i, j in enumerate(crossed):
        mine = parts[i // half][i % half, :, columns]
        theirs = parts[2 + j // half][j % half, :, columns]
        first = jnp.where(core == 0, mine, theirs)
        second = jnp.where(core == 0, theirs, mine)
        out[chips[i]] = jnp.concatenate([first, second], axis=0)


def weight(ref, columns):
    value = ref[..., columns]
    return value.reshape(-1, value.shape[-1])


def put_blocks(core, place, first, value, send, keep, rows, columns):
    for at in range(value.shape[0] // rows):
        part = value[at * rows : (at + 1) * rows].astype(BF16)
        where = place[first + at]

        @pl.when(core == at % 2)
        def _(part=part, where=where):
            keep[where, :, columns] = part

        @pl.when(core != at % 2)
        def _(part=part, where=where):
            send[where, :, columns] = part


def project_body(meta, frames, w, vec, q_out, k_out, v_out, nin_out):
    width = frames.shape[1]
    head = width // HEADS
    n, _ = normalise(frames[...].astype(F32))
    nin = (n * vec[0:1, :] + vec[1:2, :]).astype(BF16)
    nin_out[...] = nin
    q_out[...] = ((nn(nin, weight(w, slice(0, width))) + vec[2:3, :]) * (head**-0.5)).astype(BF16)
    k_out[...] = nn(nin, weight(w, slice(width, 2 * width))).astype(BF16)
    v_out[...] = (nn(nin, weight(w, slice(2 * width, 3 * width))) + vec[3:4, :]).astype(BF16)


def attend_kernel(meta, q_out, k_out, v_out, bias, ctx_out, lse_out, base):
    rows, width = q_out.shape
    unit = rows // UNITS
    window = rows - unit
    head = width // HEADS
    ranges = [unit_range(meta, u, unit) for u in range(UNITS)]
    column = lax.broadcasted_iota(jnp.int32, (1, window), 1)
    masks = [
        jnp.where((column + ws >= lo) & (column + ws < hi), 0.0, MASKED).astype(F32) for lo, hi, ws in ranges
    ]
    lane = lax.broadcasted_iota(jnp.int32, (unit, LANES), 1)
    lse_out[...] = jnp.zeros_like(lse_out)

    def pair(hp, carry):
        cols = pl.ds(pl.multiple_of(hp * LANES, LANES), LANES)
        for sub in range(2):
            base[sub] = skewed(bias[pl.ds(2 * hp + sub, 1), :], unit)
        for u in range(UNITS):
            ws = ranges[u][2]
            win = pl.ds(pl.multiple_of(ws, LANES), window)
            shift = pl.ds(pl.multiple_of(ws + (rows - unit) - u * unit, LANES), window)
            urows = slice(u * unit, (u + 1) * unit)
            kk = k_out[win, cols]
            vv = v_out[win, cols]
            qu = q_out[urows, cols]
            parts = []
            lses = lse_out[urows, :]
            for sub in range(2):
                qs = jnp.where((lane >= head) == bool(sub), qu, jnp.zeros_like(qu))
                s = nt(qs, kk) + (base[sub, :, shift] + masks[u])
                top = jnp.max(s, axis=1, keepdims=True)
                e = jnp.exp(s - top)
                tot = jnp.sum(e, axis=1, keepdims=True)
                parts.append(nn(e.astype(BF16), vv) * (1.0 / tot))
                lses = jnp.where(lane == 2 * hp + sub, top + jnp.log(tot), lses)
            lse_out[urows, :] = lses
            ctx_out[urows, cols] = jnp.where(lane < head, parts[0], parts[1]).astype(BF16)
        return carry

    lax.fori_loop(0, HEADS // 2, pair, 0)


def small_vectors(core, chips, parts, crossed, at, rows_d, rows_ff, vec3, inner3, table):
    half = parts[0].shape[0]
    lane = lax.broadcasted_iota(jnp.int32, (8, LANES), 1)
    vec3[...] = jnp.zeros_like(vec3)
    inner3[...] = jnp.zeros_like(inner3)
    for i, j in enumerate(crossed):
        mine = parts[i // half][i % half, :, at : at + LANES].astype(F32)
        theirs = parts[2 + j // half][j % half, :, at : at + LANES].astype(F32)
        for plane in range(2):
            block = jnp.where(core == plane, mine, theirs)
            d = 2 * chips[i] + plane
            for rows, part, out in ((rows_d, block[0:8], vec3), (rows_ff, block[8:16], inner3)):
                tile = (d * rows) >> 7
                shift = (d * rows) & (LANES - 1)
                rolled = pltpu.roll(part, shift, 1)
                out[tile] += jnp.where(lane >= shift, rolled, 0.0)
                out[tile + 1] += jnp.where(lane < shift, rolled, 0.0)
            table[pl.ds(d, 1), :] = block[9:10]


def relative_rows(bucket, table, out):
    devices = lax.broadcasted_iota(jnp.int32, (table.shape[0], bucket.shape[1]), 0)
    hot = jnp.where(devices == bucket[0:1, :], 1.0, 0.0).astype(BF16)
    rows = tn(table[...].astype(BF16), hot)
    total = jnp.zeros((HEADS, bucket.shape[1]), F32)
    for m in range(LANES // HEADS):
        total = total + jnp.where(bucket[1:2, :] == m, rows[m * HEADS : (m + 1) * HEADS], 0.0)
    out[0:HEADS, :] = total
    out[HEADS:, :] = jnp.zeros_like(out[HEADS:, :])


def project_kernel(
    meta, frames, p0, p1, p2, p3, bucket, bucket_rev,
    q_out, k_out, v_out, nin_out, w, vec, b_inner, bias, bias_rev,
    vec3, inner3, table, *, crossed, rows_d, rows_ff,
):
    width = frames.shape[1]
    core = meta[5]
    chips = [meta[6 + i] for i in range(len(crossed))]
    parts = (p0, p1, p2, p3)
    small_vectors(core, chips, parts, crossed, 3 * width, rows_d, rows_ff, vec3, inner3, table)
    for a in range(width // LANES):
        vec[:, a * LANES : (a + 1) * LANES] = vec3[a]
    for a in range(b_inner.shape[1] // LANES):
        b_inner[:, a * LANES : (a + 1) * LANES] = inner3[a, 0:1]
    relative_rows(bucket, table, bias)
    relative_rows(bucket_rev, table, bias_rev)
    unpack(core, chips, parts, crossed, w, slice(0, 3 * width))
    project_body(meta, frames, w, vec, q_out, k_out, v_out, nin_out)


def inner_kernel(meta, frames, ctx, *refs, crossed, rows_ff):
    if crossed:
        p0, p1, p2, p3, vec, b_inner, cot, att_out, nmid_out, act_out, slope_out, send, keep, w = refs
        core = meta[5]
        chips = [meta[6 + i] for i in range(len(crossed))]
        place = [meta[6 + len(crossed) + i] for i in range(2 * len(crossed))]
        unpack(core, chips, (p0, p1, p2, p3), crossed, w, slice(None))
    else:
        w, vec, b_inner, cot, att_out, nmid_out, act_out, slope_out, send, keep = refs
    width = frames.shape[1]
    ff = b_inner.shape[1]
    attended = frames[...].astype(F32) + nn(ctx[...], weight(w, slice(ff, ff + width))) + vec[4:5, :]
    att_out[...] = attended
    n, _ = normalise(attended)
    nmid_out[...] = (n * vec[5:6, :] + vec[6:7, :]).astype(BF16)
    for t in range(ff // width):
        cols = slice(t * width, (t + 1) * width)
        v = nn(nmid_out[...], weight(w, cols)) + b_inner[:, cols]
        phi = 0.5 * (1.0 + lax.erf(v * (0.5**0.5)))
        act = (v * phi).astype(BF16)
        act_out[:, cols] = act
        slope_out[:, cols] = (phi + v * jnp.exp(-0.5 * v * v) * 0.3989422804014327).astype(BF16)
        g = tn(act, cot[...])
        if crossed:
            put_blocks(core, place, t * (width // rows_ff), g, send, keep, rows_ff, slice(None))
        else:
            keep[cols, :] = g.astype(BF16)


def outer_kernel(meta, act, slope, attended, cot, *refs, crossed):
    if crossed:
        p0, p1, p2, p3, w, ctx, vec, mixed_out, gatt_out, gctx_out, gi_out, gvec_out, acc, gmid, w_outer = refs
        core = meta[5]
        chips = [meta[6 + i] for i in range(len(crossed))]
        unpack(core, chips, (p0, p1, p2, p3), crossed, w_outer, slice(None))
        w_outer = w_outer.reshape(act.shape[1], attended.shape[1])
    else:
        w_outer, w, ctx, vec, mixed_out, gatt_out, gctx_out, gi_out, gvec_out, acc, gmid = refs
    width = attended.shape[1]
    ff = act.shape[1]
    acc[...] = attended[...] + vec[7:8, :]
    gmid[...] = jnp.zeros_like(gmid)
    for t in range(ff // width):
        cols = slice(t * width, (t + 1) * width)
        wo = w_outer[cols, :]
        acc[...] += nn(act[:, cols], wo)
        gi = (slope[:, cols].astype(F32) * nt(cot[...], wo)).astype(BF16)
        gi_out[:, cols] = gi
        gmid[...] += nt(gi, weight(w, cols))
    mixed_out[...] = acc[...].astype(BF16)
    n, r = normalise(attended[...])
    e = gmid[...]
    c32 = cot[...].astype(F32)
    gatt = c32 + norm_backward(n, r, vec[5:6, :], e)
    gatt_out[...] = gatt
    gbr = gatt.astype(BF16)
    gctx_out[...] = nt(gbr, weight(w, slice(ff, ff + width))).astype(BF16)
    gvec_out[0:1, :] = jnp.sum(gbr.astype(F32), axis=0, keepdims=True)
    gvec_out[1:2, :] = jnp.sum(e * n, axis=0, keepdims=True)
    gvec_out[2:3, :] = jnp.sum(e, axis=0, keepdims=True)
    gvec_out[3:4, :] = jnp.sum(c32, axis=0, keepdims=True)
    gvec_out[4:8, :] = jnp.zeros_like(gvec_out[4:8, :])


def outer_weights_kernel(meta, nmid, gi, ctx, gatt, send, keep, gb_out, *, crossed, rows_d):
    width = nmid.shape[1]
    ff = gi.shape[1]
    core = meta[5]
    place = [meta[6 + len(crossed) + i] for i in range(2 * len(crossed))]
    for t in range(ff // width + 1):
        cols = slice(t * width, (t + 1) * width)
        if t < ff // width:
            d = gi[:, cols]
            gb_out[:, cols] = jnp.sum(d.astype(F32), axis=0, keepdims=True)
            g = tn(nmid[...], d)
        else:
            g = tn(ctx[...], gatt[...].astype(BF16))
        if crossed:
            put_blocks(core, place, 0, g, send, keep, rows_d, cols)
        else:
            keep[:, cols] = g.astype(BF16)


def small_blocks(core, place, vecs, inner, grows, bucket_rev, send, keep, columns, rows_d, rows_ff):
    n = len(place)
    span = bucket_rev.shape[1]
    row = lax.broadcasted_iota(jnp.int32, (8, LANES), 0)
    lane = lax.broadcasted_iota(jnp.int32, (8, LANES), 1)
    each = LANES // HEADS
    big = [jnp.where(bucket_rev[1:2, :] == m, grows, 0.0) for m in range(each)]
    big = jnp.concatenate(big + [jnp.zeros((LANES - each * HEADS, span), F32)], axis=0)
    high = big.astype(BF16)
    low = (big - high.astype(F32)).astype(BF16)
    hot = jnp.where(lax.broadcasted_iota(jnp.int32, (n, span), 0) == bucket_rev[0:1, :], 1.0, 0.0).astype(BF16)
    table = nt(hot, high) + nt(hot, low)

    def cut(value, at, count):
        tile, shift = at // LANES, at % LANES
        out = value[:, tile * LANES : (tile + 1) * LANES]
        if shift:
            out = pltpu.roll(out, LANES - shift, 1)
            if shift + count > LANES:
                more = pltpu.roll(value[:, (tile + 1) * LANES : (tile + 2) * LANES], LANES - shift, 1)
                out = jnp.where(lane < LANES - shift, out, more)
        return jnp.where(lane < count, out, 0.0)

    for d in range(n):
        low_rows = jnp.where(row == 0, cut(inner, d * rows_ff, rows_ff), 0.0)
        low_rows = jnp.where(row == 1, table[d : d + 1], low_rows)
        block = [cut(vecs, d * rows_d, rows_d), low_rows]
        block = jnp.concatenate(block + [jnp.zeros((rows_d - 16, LANES), F32)], axis=0).astype(BF16)
        where = place[d]

        @pl.when(core == d % 2)
        def _(block=block, where=where):
            keep[where, :, columns] = block

        @pl.when(core != d % 2)
        def _(block=block, where=where):
            send[where, :, columns] = block


def attend_back_kernel(
    meta, q, k, v, lse, ctx, gctx, bias_rev, nin, frames, gatt, gin, w, vec, *refs, crossed, rows_d, first, count,
):
    last = first + 2 * count == HEADS
    if last and crossed:
        gvec2, gb_inner, bucket_rev, *refs = refs
        earlier = first // (2 * count)
        before = [(refs[2 * i], refs[2 * i + 1]) for i in range(earlier)]
        refs = refs[2 * earlier :]
    send, keep, gin_out, gvec_out, grow_out, base, gbase, lse_t, delta_t, kt, dqkv, gk, gv = refs
    rows, width = frames.shape
    unit = rows // UNITS
    window = rows - unit
    head = width // HEADS
    core = meta[5]
    place = [meta[6 + len(crossed) + i] for i in range(2 * len(crossed))]
    lses = jnp.transpose(lse[...])
    prod = gctx[...].astype(F32) * ctx[...].astype(F32)
    sel_row = lax.broadcasted_iota(jnp.int32, (16, width), 0)
    sel_col = lax.broadcasted_iota(jnp.int32, (16, width), 1)
    sel = jnp.where((sel_col >= sel_row * head) & (sel_col < (sel_row + 1) * head), 1.0, 0.0).astype(BF16)
    high = prod.astype(BF16)
    low = (prod - high.astype(F32)).astype(BF16)
    deltas = nt(sel, high) + nt(sel, low)
    for h in range(HEADS):
        lse_t[h] = lses[h : h + 1]
        delta_t[h] = deltas[h : h + 1]
    ranges = [unit_range(meta, u, unit) for u in range(UNITS)]
    row_at = lax.broadcasted_iota(jnp.int32, (window, LANES), 0)
    lane = lax.broadcasted_iota(jnp.int32, (unit, LANES), 1)
    sub_lane = lax.broadcasted_iota(jnp.int32, (LANES, unit), 0)
    span = count * LANES

    def pair(step, carry):
        hp = first // 2 + step
        cols = pl.ds(pl.multiple_of(hp * LANES, LANES), LANES)
        here = pl.multiple_of(step * LANES, LANES)
        kt[...] = jnp.transpose(k[:, cols])
        gk[...] = jnp.zeros_like(gk)
        gv[...] = jnp.zeros_like(gv)
        gbase[...] = jnp.zeros_like(gbase)
        for sub in range(2):
            base[sub] = skewed(bias_rev[pl.ds(2 * hp + sub, 1), :], unit)
        for u in range(UNITS):
            lo, hi, ws = ranges[u]
            ws = pl.multiple_of(ws, LANES)
            win = pl.ds(ws, window)
            urows = slice(u * unit, (u + 1) * unit)
            mask = jnp.where((row_at + ws >= lo) & (row_at + ws < hi), 0.0, MASKED).astype(F32)
            kk = k[win, cols]
            vv = v[win, cols]
            qu = q[urows, cols]
            gu = gctx[urows, cols]
            gk_win = gk[win, :]
            gv_win = gv[win, :]
            gq = []
            offsets = [
                pl.ds(pl.multiple_of((rows - unit) + u * unit - ws - jb * unit, LANES), unit) for jb in range(UNITS - 1)
            ]
            for sub in range(2):
                h = 2 * hp + sub
                mine = (lane >= head) == bool(sub)
                qs = jnp.where(mine, qu, jnp.zeros_like(qu))
                gs = jnp.where(mine, gu, jnp.zeros_like(gu))
                rel = jnp.concatenate([base[sub, :, o] for o in offsets], axis=0)
                s = nt(kk, qs) + rel + mask
                p = jnp.exp(s - lse_t[h, :, urows])
                gp = nt(vv, gs)
                ds = (p * (gp - delta_t[h, :, urows])).astype(BF16)
                gv_win = gv_win + nn(p.astype(BF16), gs)
                gk_win = gk_win + nn(ds, qs)
                gq.append(nn(kt[:, win], ds))
                d32 = ds.astype(F32)
                for jb, o in enumerate(offsets):
                    gbase[sub, :, o] += d32[jb * unit : (jb + 1) * unit]
            gk[win, :] = gk_win
            gv[win, :] = gv_win
            gq_t = jnp.where(sub_lane < head, gq[0], gq[1])
            dqkv[urows, pl.ds(here, LANES)] = jnp.transpose(gq_t).astype(BF16) * BF16(head**-0.5)
        dqkv[:, pl.ds(span + here, LANES)] = gk[...].astype(BF16)
        dqkv[:, pl.ds(2 * span + here, LANES)] = gv[...].astype(BF16)
        for sub in range(2):
            grow_out[pl.ds(2 * step + sub, 1), :] = unskewed_sum(gbase[sub], unit)
        return carry

    grow_out[...] = jnp.zeros_like(grow_out)
    lax.fori_loop(0, count, pair, 0)
    at_columns = first * head
    grad_in = gin[...] if first else jnp.zeros((rows, width), F32)
    for part in range(3):
        d = dqkv[:, part * span : (part + 1) * span]
        grad_in = grad_in + nt(d, weight(w, slice(part * width + at_columns, part * width + at_columns + span)))
    g = tn(nin[...], dqkv[...])
    if crossed:
        put_blocks(core, place, 0, g, send, keep, rows_d, slice(0, 3 * span))
    else:
        keep[:, 0 : 3 * span] = g.astype(BF16)
    sums = [jnp.sum(dqkv[:, at : at + span].astype(F32), axis=0, keepdims=True) for at in (0, 2 * span)]
    gvec_out[...] = jnp.zeros_like(gvec_out)
    gvec_out[2:4, 0:span] = jnp.concatenate(sums, axis=0)
    if not last:
        gin_out[...] = grad_in
        return
    n, r = normalise(frames[...].astype(F32))
    gin_out[...] = (gatt[...] + norm_backward(n, r, vec[0:1, :], grad_in)).astype(BF16)
    gvec_out[0:1, :] = jnp.sum(grad_in * n, axis=0, keepdims=True)
    gvec_out[1:2, :] = jnp.sum(grad_in, axis=0, keepdims=True)
    if crossed:
        for i, (vectors, _) in enumerate(before):
            gvec_out[2:4, i * span : (i + 1) * span] = vectors[2:4, 0:span]
        gvec_out[2:4, at_columns : at_columns + span] = jnp.concatenate(sums, axis=0)
        gvec_out[4:8, :] = gvec2[0:4, :]
        grows = jnp.concatenate([grow[0 : 2 * count, :] for _, grow in before] + [grow_out[0 : 2 * count, :]], axis=0)
        small_blocks(
            core, place, gvec_out[...], jnp.broadcast_to(gb_inner[...], (8, gb_inner.shape[1])), grows, bucket_rev,
            send, keep, slice(3 * span, 3 * span + LANES), rows_d, gb_inner.shape[1] // len(place),
        )


def run_kernel(order, kernel, name, scalars, arrays, outs, scratch=(), spare=10):
    spec = pl.BlockSpec(memory_space=pltpu.VMEM)
    smem = pl.BlockSpec(memory_space=pltpu.SMEM)
    arrays = order.after(*arrays)
    arrays = [pltpu.with_memory_space_constraint(a, pltpu.VMEM) for a in arrays]
    limit = spare * MIB + sum(math.prod(b.shape) * jnp.dtype(b.dtype).itemsize for b in scratch)
    out = pl.pallas_call(
        kernel,
        in_specs=[smem] * len(scalars) + [spec] * len(arrays),
        out_specs=[spec] * len(outs),
        out_shape=[pltpu.VMEM(s, d) for s, d in outs],
        scratch_shapes=list(scratch),
        compiler_params=pltpu.CompilerParams(vmem_limit_bytes=limit),
        cost_estimate=pl.CostEstimate(flops=100_000_000_000, bytes_accessed=100_000_000, transcendentals=0),
        name=name,
    )(*scalars, *arrays)
    order.did(out[0])
    return out


def on_device(
    frames, ln1_gain, ln1_shift, w_query, b_query, w_key, w_value, b_value, w_out, b_out, ln2_gain, ln2_shift,
    w_inner, b_inner, w_outer, b_outer, bias_table, layout, valid, rel_index, cotangent, *, n,
):
    rows, width = frames.shape
    rows_d = w_query.shape[0]
    rows_ff = w_outer.shape[0]
    ff = w_inner.shape[1]
    span = rel_index.shape[0] + 1
    unit = rows // UNITS
    per_table = bias_table.shape[0]
    plan = plan_tables(n)
    core, chips, place = plan
    order = Order()
    direct = (
        rows_d % 8 == 0 and rows_ff % 16 == 0 and max(rows_d, rows_ff, per_table) <= LANES and per_table % HEADS == 0
    )
    crossed = tuple(crossed_places(n)) if direct else ()
    meta = jnp.concatenate([layout, valid.reshape(-1), core[None]] + [chips, place] * direct).astype(jnp.int32)
    small_d = jnp.stack([ln1_gain, ln1_shift, b_query, b_value, b_out, ln2_gain, ln2_shift, b_outer])

    base = pltpu.VMEM((2, unit, span), F32)
    if direct:
        wide = [jnp.pad(small_d, ((0, 0), (0, LANES - rows_d))), jnp.pad(b_inner, (0, LANES - rows_ff))[None]]
        wide.append(jnp.pad(bias_table, (0, LANES - per_table))[None])
        small = jnp.pad(jnp.concatenate(wide), ((0, rows_d - 10), (0, 0)))
        g1 = Gather(jnp.concatenate([w_query, w_key, w_value, small], axis=1), n, order)
        (part2,) = lax.optimization_barrier((jnp.concatenate([w_inner, w_out], axis=1), g1.got))[:1]
        g2 = Gather(part2, n, order)
        (part3,) = lax.optimization_barrier((w_outer, g2.got))[:1]
        g3 = Gather(part3, n, order)
        for g in (g1, g1, g2, g1, g2, g3, g2):
            g.step()
        first = g1.finish()
        each = per_table // HEADS
        index = jnp.stack([rel_index // each, rel_index % each])
        bucket = jnp.pad(index, ((0, 6), (0, 1)), constant_values=-1)
        bucket_rev = jnp.pad(index[:, ::-1], ((0, 6), (0, 1)), constant_values=-1)
        q, k, v, nin, w1, vec, inner_bias, bias, bias_rev = run_kernel(
            order, functools.partial(project_kernel, crossed=crossed, rows_d=rows_d, rows_ff=rows_ff), "project", [meta],
            [frames, *first, bucket, bucket_rev],
            [((rows, width), BF16)] * 4
            + [((n // 2, 2 * rows_d, 3 * width), BF16), ((8, width), F32), ((1, ff), F32), ((16, span), F32), ((16, span), F32)],
            [
                pltpu.VMEM((width // LANES + 1, 8, LANES), F32),
                pltpu.VMEM((ff // LANES + 1, 8, LANES), F32),
                pltpu.VMEM((n, LANES), F32),
            ],
        )
        g3.step()
        w2 = g2.finish()
        part_ff = [((n // 2, rows_ff, width), BF16)] * 2
        part_io = [((n // 2, rows_d, ff + width), BF16)] * 2
        w2_out = [((n // 2, 2 * rows_d, ff + width), BF16)]
    else:
        flat = jnp.concatenate([small_d.reshape(-1), b_inner, bias_table])
        per = flat.shape[0] // rows_d
        small = jnp.pad(flat.reshape(rows_d, per), ((0, 0), (0, LANES - per)))
        w1 = gathered(Gather(jnp.concatenate([w_query, w_key, w_value, small], axis=1), n, order).finish(), plan, n)
        w2 = (gathered(Gather(jnp.concatenate([w_inner, w_out], axis=1), n, order).finish(), plan, n),)
        w3 = (gathered(Gather(w_outer, n, order).finish(), plan, n),)
        flats = w1[:, 3 * width : 3 * width + per].reshape(n, rows_d * per)
        vec = flats[:, : 8 * rows_d].reshape(n, 8, rows_d).transpose(1, 0, 2).reshape(8, width).astype(F32)
        inner_bias = flats[:, 8 * rows_d : 8 * rows_d + rows_ff].reshape(1, ff).astype(F32)
        table = jnp.pad(flats[:, 8 * rows_d + rows_ff :].reshape(-1, HEADS), ((0, 0), (0, 16 - HEADS)))
        index = jnp.pad(rel_index, (0, 1), constant_values=-1)
        index_rev = jnp.pad(rel_index[::-1], (0, 1), constant_values=-1)
        ids = jnp.arange(table.shape[0], dtype=jnp.int32)[:, None]
        bias = tn(table, (ids == index[None]).astype(BF16))
        bias_rev = tn(table, (ids == index_rev[None]).astype(BF16))
        q, k, v, nin = run_kernel(
            order, project_body, "project", [meta], [frames, w1, vec], [((rows, width), BF16)] * 4
        )
        part_ff = [((8, LANES), BF16), ((ff, width), BF16)]
        part_io = [((8, LANES), BF16), ((width, ff + width), BF16)]
        w2_out = []

    ctx, lse = run_kernel(
        order, attend_kernel, "attend", [meta], [q, k, v, bias], [((rows, width), BF16), ((rows, LANES), F32)], [base]
    )

    def start(send, keep, scatter=None):
        scatter = scatter or Scatter(n, order)
        return scatter.add(*((send, keep) if direct else split_natural(keep, plan, n)))

    if direct:
        g3.step()
    attended, nmid, act, slope, ff_send, ff_keep, *w2_whole = run_kernel(
        order, functools.partial(inner_kernel, crossed=crossed, rows_ff=rows_ff), "inner", [meta],
        [frames, ctx, *w2, vec, inner_bias, cotangent],
        [((rows, width), F32), ((rows, width), BF16), ((rows, ff), BF16), ((rows, ff), BF16)] + part_ff + w2_out,
    )
    w2_whole = w2_whole[0] if direct else w2[0]
    sum_ff = start(ff_send, ff_keep)
    if direct:
        w3 = g3.finish()
    mixed, gatt, gctx, gi, gvec2 = run_kernel(
        order, functools.partial(outer_kernel, crossed=crossed), "outer", [meta],
        [act, slope, attended, cotangent, *w3, w2_whole, ctx, vec],
        [((rows, width), BF16), ((rows, width), F32), ((rows, width), BF16), ((rows, ff), BF16), ((8, width), F32)],
        [pltpu.VMEM((rows, width), F32)] * 2 + [pltpu.VMEM((n // 2, 2 * rows_ff, width), BF16)] * direct,
    )
    sum_ff.step()
    io_send, io_keep, gb_inner = run_kernel(
        order, functools.partial(outer_weights_kernel, crossed=crossed, rows_d=rows_d), "outer_weights", [meta],
        [nmid, gi, ctx, gatt], part_io + [((1, ff), F32)],
    )
    sum_io = start(io_send, io_keep)

    count = 2
    cols = count * LANES
    passed = gatt
    done, earlier = [], []
    begin = functools.partial(Scatter, n, order)
    sum_early, sum_late = begin(), begin()
    calls = HEADS // (2 * count)
    for call in range(calls):
        last = call == calls - 1
        wide = 3 * cols + LANES * (last and direct)
        part = [((n // 2, rows_d, wide), BF16)] * 2 if direct else [((8, LANES), BF16), ((width, wide), BF16)]
        extra = [gvec2, gb_inner, bucket_rev] + [a for pair in earlier for a in pair] if last and direct else []
        send, keep, passed, gvec1, grow = run_kernel(
            order,
            functools.partial(
                attend_back_kernel, crossed=crossed, rows_d=rows_d, first=call * 2 * count, count=count
            ),
            "attend_back", [meta],
            [q, k, v, lse, ctx, gctx, bias_rev, nin, frames, gatt, passed, w1, vec] + extra,
            part + [((rows, width), BF16 if last else F32), ((8, width), F32), ((8, span), F32)],
            [
                base, base,
                pltpu.VMEM((HEADS, 1, rows), F32),
                pltpu.VMEM((HEADS, 1, rows), F32),
                pltpu.VMEM((LANES, rows), BF16),
                pltpu.VMEM((rows, 3 * cols), BF16),
                pltpu.VMEM((rows, LANES), F32),
                pltpu.VMEM((rows, LANES), F32),
            ],
            spare=10,
        )
        earlier.append((gvec1, grow))
        start(send, keep, sum_late if last else sum_early)
        if call == 0:
            sum_ff.step()
            sum_io.step()
        if call == 1:
            sum_ff.step()
            sum_early.step()
    tail = [sum_io, sum_ff, sum_early, sum_late, sum_io, sum_early, sum_late, sum_io, sum_early, sum_late, sum_late]
    for each_sum in tail:
        if each_sum.steps:
            each_sum.step()
    sum_outer = sum_ff.finish()
    early, sum_io, late = sum_early.finish(), sum_io.finish(), sum_late.finish()
    pieces = [early[:, i * 3 * cols : (i + 1) * 3 * cols] for i in range(calls - 1)] + [late[:, : 3 * cols]]
    sum_q, sum_k, sum_v = (jnp.concatenate([p[:, i * cols : (i + 1) * cols] for p in pieces], axis=1) for i in range(3))
    if direct:
        small = late[:, 3 * cols :]
        vecs = small[:8, :rows_d]
        sum_b_inner = small[8, :rows_ff]
        sum_table = small[9, :per_table]
    else:
        hot_rev = (ids == index_rev[None]).astype(F32)
        grow = jnp.concatenate([g[: 2 * count] for _, g in earlier])
        gtable = lax.dot_general(
            hot_rev, grow, (((1,), (1,)), ((), ())), precision=lax.Precision.HIGHEST, preferred_element_type=F32
        )
        gbias = jnp.concatenate([g[2:4, :cols] for g, _ in earlier], axis=1)
        gsmall = jnp.concatenate([gvec1[0:2], gbias, gvec2[0:4]])
        gsmall = gsmall.reshape(8, n, rows_d).transpose(1, 0, 2).reshape(n, 8 * rows_d)
        gflat = jnp.concatenate([gsmall, gb_inner.reshape(n, rows_ff), gtable.reshape(n, -1)], axis=1)
        gflat = jnp.pad(gflat, ((0, 0), (0, -gflat.shape[1] % LANES))).astype(BF16)
        sum_flat = Scatter(n, order).add(*split_natural(gflat, plan, n)).finish()[0]
        vecs = sum_flat[: 8 * rows_d].reshape(8, rows_d)
        sum_b_inner = sum_flat[8 * rows_d : 8 * rows_d + rows_ff]
        sum_table = sum_flat[8 * rows_d + rows_ff : 8 * rows_d + rows_ff + per_table]
    return (
        mixed, passed, vecs[0], vecs[1], sum_q, vecs[2], sum_k, sum_v, vecs[3],
        sum_io[:, ff:], vecs[4], vecs[5], vecs[6], sum_io[:, :ff], sum_b_inner, sum_outer, vecs[7], sum_table,
    )


def solution(mesh):
    row, two = P("dp"), P("dp", None)
    in_specs = (two, row, row, two, row, two, two, row, two, row, row, row, two, row, two, row, row, row, two, P(), two)
    out_specs = (two, two, row, row, two, row, two, two, row, two, row, row, row, two, row, two, row, row)
    return jax.shard_map(
        functools.partial(on_device, n=mesh.shape["dp"]),
        mesh=mesh, in_specs=in_specs, out_specs=out_specs, check_vma=False,
    )
```

```python
import functools
import math

import jax
import jax.numpy as jnp
import numpy as np
from jax import lax
from jax.experimental import pallas as pl
from jax.experimental.pallas import tpu as pltpu
from jax.sharding import PartitionSpec as P

HEADS = 12
LANES = 128
UNITS = 4
MASKED = -1e30
F32 = jnp.float32
BF16 = jnp.bfloat16
SEGMENT = ((0, 0, 0, 1), (0, 0, 1, 1), (0, 0, 1, 2), (0, 1, 2, 3))
START = ((0, 0, 0, 3), (0, 0, 2, 2), (0, 0, 2, 3), (0, 1, 2, 3))
MIB = 1024 * 1024


def bit_orders(n, kind):
    chip = [1 << k for k in range(1, n.bit_length() - 1)]
    low, high = chip[:2], chip[2:][::-1]
    if kind == "outer":
        return (low[:1] + high + low[1:], low[1:] + high + low[:1])
    return (high + low, high + low[::-1])


def gather_masks(bits):
    masks = [0]
    for bit in bits:
        masks = masks + [bit ^ m for m in masks]
    return masks


def scatter_masks(bits):
    masks = [0]
    for bit in bits:
        masks = [bit ^ m for m in masks] + masks
    return masks


def pairs(n, by_core):
    return [(i, i ^ by_core[i & 1]) for i in range(n)]


class Order:
    def __init__(self):
        self.last = None

    def after(self, *arrays):
        if self.last is None:
            return arrays
        return lax.optimization_barrier((*arrays, self.last))[:-1]

    def did(self, array):
        self.last = array


class Gather:
    def __init__(self, part, n, order, kind="inner"):
        self.n = n
        self.order = order
        self.steps = list(zip(*bit_orders(n, kind)))
        self.held = part[None]
        self.got = lax.ppermute(self.held, "dp", pairs(n, self.steps.pop(0)))

    def step(self):
        pair = self.order.after(self.held, self.got)
        self.held = jnp.concatenate(pair, axis=0)
        self.order.did(self.held)
        self.got = lax.ppermute(self.held, "dp", pairs(self.n, self.steps.pop(0)))
        return self

    def finish(self):
        while self.steps:
            self.step()
        (self.got,) = self.order.after(self.got)
        swap = pairs(self.n, (1, 1))
        return (self.held, self.got, lax.ppermute(self.held, "dp", swap), lax.ppermute(self.got, "dp", swap))


class Scatter:
    def __init__(self, n, order, kind="inner"):
        self.n = n
        self.order = order
        self.parts = []
        self.terms = []
        self.at = 0
        self.steps = list(reversed(list(zip(*bit_orders(n, kind)))))
        self.half = n // 4

    def add(self, send, keep):
        self.parts.append((keep, lax.ppermute(send, "dp", pairs(self.n, (1, 1)))))
        return self

    def total(self, count, dtype):
        flat = [t for part in self.parts for t in part] + [t for t, _ in self.terms]
        flat = list(self.order.after(*flat))
        at = self.at
        cut = [lax.slice_in_dim(t, at, at + count).astype(F32) for t in flat[: 2 * len(self.parts)]]
        out = [cut[2 * i] + cut[2 * i + 1] for i in range(len(self.parts))]
        out = out[0] if len(out) == 1 else jnp.concatenate(out, axis=-1)
        for t, (_, first) in zip(flat[2 * len(self.parts) :], self.terms):
            out = out + lax.slice_in_dim(t, at - first, at - first + count).astype(F32)
        out = out.astype(dtype)
        self.order.did(out)
        return out

    def step(self):
        by_core = self.steps.pop(0)
        out = self.total(self.half, BF16)
        self.at += self.half
        self.terms.append((lax.ppermute(out, "dp", pairs(self.n, by_core)), self.at))
        self.half //= 2

    def finish(self):
        while self.steps:
            self.step()
        return self.total(1, F32)[0]


def plan_tables(n, kind="inner"):
    orders = bit_orders(n, kind)
    me = lax.axis_index("dp")
    core = me & 1
    g = np.array([gather_masks(o) for o in orders], np.int32)
    s = np.array([scatter_masks(o) for o in orders], np.int32)
    inverse = np.zeros((2, n), np.int32)
    for c in (0, 1):
        for i, m in enumerate(s[c]):
            inverse[c, m] = i
    devices = jnp.arange(n, dtype=jnp.int32)
    chips = (me ^ jnp.where(core == 0, jnp.asarray(g[0]), jnp.asarray(g[1]))) >> 1
    mask = (devices ^ me) & ~1
    place = jnp.sum(jnp.where(mask[:, None] == devices[None, :], jnp.asarray(inverse)[np.arange(n) % 2], 0), axis=1)
    return core, chips, place


def crossed_places(n, kind="inner"):
    first, second = (gather_masks(o) for o in bit_orders(n, kind))
    places = [second.index(m) for m in first]
    assert places == [first.index(m) for m in second]
    return places


def gathered(parts, plan, n):
    core, chips, _ = plan
    mine = jnp.concatenate(parts[:2])
    theirs = jnp.concatenate(parts[2:])[np.array(crossed_places(n))]
    both = jnp.where(core == 0, jnp.stack([mine, theirs], 1), jnp.stack([theirs, mine], 1))
    return both[jnp.argsort(chips)].reshape(n * mine.shape[1], mine.shape[2])


def split_natural(grad, plan, n):
    core, _, place = plan
    rows = grad.shape[0] // n
    blocks = grad.reshape(n // 2, 2, rows, grad.shape[1])
    mine = jnp.where(core == 0, blocks[:, 0], blocks[:, 1])
    theirs = jnp.where(core == 0, blocks[:, 1], blocks[:, 0])
    both = place.reshape(n // 2, 2)
    my_place = jnp.where(core == 0, both[:, 0], both[:, 1])
    their_place = jnp.where(core == 0, both[:, 1], both[:, 0])
    return theirs[jnp.argsort(their_place)], mine[jnp.argsort(my_place)]


def nn(a, b):
    return jnp.dot(a, b, preferred_element_type=F32)


def nt(a, b):
    return lax.dot_general(a, b, (((1,), (1,)), ((), ())), preferred_element_type=F32)


def tn(a, b):
    return lax.dot_general(a, b, (((0,), (0,)), ((), ())), preferred_element_type=F32)


def normalise(v):
    centred = v - jnp.mean(v, axis=-1, keepdims=True)
    r = lax.rsqrt(jnp.mean(centred * centred, axis=-1, keepdims=True) + 1e-05)
    return centred * r, r


def norm_backward(n, r, gain, e):
    eg = e * gain
    return r * (eg - jnp.mean(eg, axis=-1, keepdims=True) - n * jnp.mean(eg * n, axis=-1, keepdims=True))


def pick(table, code, u):
    out = jnp.int32(table[0][u])
    for c in range(1, 4):
        out = jnp.where(code == c, jnp.int32(table[c][u]), out)
    return out


def unit_range(meta, u, unit):
    code = meta[0]
    segment = pick(SEGMENT, code, u)
    start = pick(START, code, u)
    count = meta[1]
    for s in range(1, 4):
        count = jnp.where(segment == s, meta[1 + s], count)
    window = jnp.minimum(start, 1) * unit
    return start * unit, start * unit + count, window


def skewed(row, unit):
    wide = jnp.broadcast_to(row, (unit, row.shape[1]))
    return pltpu.roll(wide, row.shape[1] - (unit - 1), 1, stride=1, stride_axis=0)


def unskewed_sum(block, unit):
    width = block.shape[1]
    total = None
    for a in range(unit // 8):
        part = block[8 * a : 8 * a + 8]
        shift = (unit - 1 - 8 * a) % width
        part = pltpu.roll(part, shift, 1) if shift else part
        total = part if total is None else total + part
    out = total[0:1]
    for s in range(1, 8):
        out = out + pltpu.roll(total[s : s + 1], width - s, 1)
    return out


def unpack(core, chips, parts, crossed, out, columns):
    half = parts[0].shape[0]
    for i, j in enumerate(crossed):
        mine = parts[i // half][i % half, :, columns]
        theirs = parts[2 + j // half][j % half, :, columns]
        first = jnp.where(core == 0, mine, theirs)
        second = jnp.where(core == 0, theirs, mine)
        out[chips[i]] = jnp.concatenate([first, second], axis=0)


def weight(ref, columns):
    value = ref[..., columns]
    return value.reshape(-1, value.shape[-1])


def put_blocks(core, place, first, value, send, keep, rows, columns):
    for at in range(value.shape[0] // rows):
        part = value[at * rows : (at + 1) * rows].astype(BF16)
        where = place[first + at]

        @pl.when(core == at % 2)
        def _(part=part, where=where):
            keep[where, :, columns] = part

        @pl.when(core != at % 2)
        def _(part=part, where=where):
            send[where, :, columns] = part


def project_body(meta, frames, w, vec, q_out, k_out, v_out, nin_out):
    width = frames.shape[1]
    head = width // HEADS
    n, _ = normalise(frames[...].astype(F32))
    nin = (n * vec[0:1, :] + vec[1:2, :]).astype(BF16)
    nin_out[...] = nin
    q_out[...] = ((nn(nin, weight(w, slice(0, width))) + vec[2:3, :]) * (head**-0.5)).astype(BF16)
    k_out[...] = nn(nin, weight(w, slice(width, 2 * width))).astype(BF16)
    v_out[...] = (nn(nin, weight(w, slice(2 * width, 3 * width))) + vec[3:4, :]).astype(BF16)


def attend_kernel(meta, q, k, v, bias_rev, ctx_out, lse_out, base, vt):
    rows, width = q.shape
    unit = rows // UNITS
    window = rows - unit
    head = width // HEADS
    ranges = [unit_range(meta, u, unit) for u in range(UNITS)]
    row_at = lax.broadcasted_iota(jnp.int32, (window, unit), 0)
    lane = lax.broadcasted_iota(jnp.int32, (unit, LANES), 1)
    sub_lane = lax.broadcasted_iota(jnp.int32, (LANES, unit), 0)

    def pair(hp, carry):
        cols = pl.ds(pl.multiple_of(hp * LANES, LANES), LANES)
        vt[...] = jnp.transpose(v[:, cols])
        for sub in range(2):
            base[sub] = skewed(bias_rev[pl.ds(2 * hp + sub, 1), :], unit)
        for u in range(UNITS):
            lo, hi, ws = ranges[u]
            ws = pl.multiple_of(ws, LANES)
            win = pl.ds(ws, window)
            urows = slice(u * unit, (u + 1) * unit)
            mask = jnp.where((row_at + ws >= lo) & (row_at + ws < hi), 0.0, MASKED).astype(F32)
            kk = k[win, cols]
            qu = q[urows, cols]
            offsets = [
                pl.ds(pl.multiple_of((rows - unit) + u * unit - ws - jb * unit, LANES), unit) for jb in range(UNITS - 1)
            ]
            parts = []
            for sub in range(2):
                qs = jnp.where((lane >= head) == bool(sub), qu, jnp.zeros_like(qu))
                rel = jnp.concatenate([base[sub, :, o] for o in offsets], axis=0)
                s = nt(kk, qs) + rel + mask
                top = jnp.max(s, axis=0, keepdims=True)
                e = jnp.exp(s - top)
                tot = jnp.sum(e, axis=0, keepdims=True)
                parts.append(nn(vt[:, win], e.astype(BF16)) * (1.0 / tot))
                lse_out[2 * hp + sub, :, urows] = top + jnp.log(tot)
            ctx_out[urows, cols] = jnp.transpose(jnp.where(sub_lane < head, parts[0], parts[1])).astype(BF16)
        return carry

    lax.fori_loop(0, HEADS // 2, pair, 0)


def small_vectors(core, chips, parts, crossed, at, rows_d, rows_ff, vec3, inner3, table):
    half = parts[0].shape[0]
    lane = lax.broadcasted_iota(jnp.int32, (8, LANES), 1)
    vec3[...] = jnp.zeros_like(vec3)
    inner3[...] = jnp.zeros_like(inner3)
    for i, j in enumerate(crossed):
        mine = parts[i // half][i % half, :, at : at + LANES].astype(F32)
        theirs = parts[2 + j // half][j % half, :, at : at + LANES].astype(F32)
        for plane in range(2):
            block = jnp.where(core == plane, mine, theirs)
            d = 2 * chips[i] + plane
            unit_half = rows_ff // 2
            half_at = 2 * half * rows_ff
            for first, rows, part, out in (
                (0, rows_d, block[0:8], vec3),
                (0, unit_half, block[8:16], inner3),
                (half_at, unit_half, block[16:24], inner3),
            ):
                start = first + d * rows
                tile = start >> 7
                shift = start & (LANES - 1)
                rolled = pltpu.roll(part, shift, 1)
                out[tile] += jnp.where(lane >= shift, rolled, 0.0)
                out[tile + 1] += jnp.where(lane < shift, rolled, 0.0)
            table[pl.ds(d, 1), :] = block[9:10]


def relative_rows(bucket, table, out):
    devices = lax.broadcasted_iota(jnp.int32, (table.shape[0], bucket.shape[1]), 0)
    hot = jnp.where(devices == bucket[0:1, :], 1.0, 0.0).astype(BF16)
    rows = tn(table[...].astype(BF16), hot)
    total = jnp.zeros((HEADS, bucket.shape[1]), F32)
    for m in range(LANES // HEADS):
        total = total + jnp.where(bucket[1:2, :] == m, rows[m * HEADS : (m + 1) * HEADS], 0.0)
    out[0:HEADS, :] = total
    out[HEADS:, :] = jnp.zeros_like(out[HEADS:, :])


def project_kernel(
    meta, frames, p0, p1, p2, p3, bucket_rev,
    q_out, k_out, v_out, nin_out, w, vec, b_inner, bias_rev,
    vec3, inner3, table, *, crossed, rows_d, rows_ff,
):
    width = frames.shape[1]
    core = meta[5]
    chips = [meta[6 + i] for i in range(len(crossed))]
    parts = (p0, p1, p2, p3)
    small_vectors(core, chips, parts, crossed, 3 * width, rows_d, rows_ff, vec3, inner3, table)
    for a in range(width // LANES):
        vec[:, a * LANES : (a + 1) * LANES] = vec3[a]
    for a in range(b_inner.shape[1] // LANES):
        b_inner[:, a * LANES : (a + 1) * LANES] = inner3[a, 0:1]
    relative_rows(bucket_rev, table, bias_rev)
    unpack(core, chips, parts, crossed, w, slice(0, 3 * width))
    project_body(meta, frames, w, vec, q_out, k_out, v_out, nin_out)


def unpack_folded(core, chips, parts, crossed, out, at, width):
    half = parts[0].shape[0]
    for i, j in enumerate(crossed):
        mine = parts[i // half][i % half, :, at : at + 2 * width]
        theirs = parts[2 + j // half][j % half, :, at : at + 2 * width]
        first = jnp.where(core == 0, mine, theirs)
        second = jnp.where(core == 0, theirs, mine)
        rows = [first[:, :width], first[:, width:], second[:, :width], second[:, width:]]
        out[chips[i]] = jnp.concatenate(rows, axis=0)


def feed_tiles(meta, kind, crossed, parts, natural, b_inner, cot, first, nmid, acc, gmid, gb_out, send, keep, w_tile, w_rows, rows_d):
    width = nmid.shape[1]
    tiles = b_inner.shape[1] // width // 2
    if crossed:
        half = len(crossed)
        core = meta[5]
        chips_at = 6 + half * (kind == "outer")
        chips = [meta[chips_at + i] for i in range(half)]
        place_at = 6 + 2 * half + 2 * half * (first == 0)
        place = [meta[place_at + i] for i in range(2 * half)]
        unpack_folded(core, chips, parts, crossed, w_rows, tiles * width, width)
        w_outer = w_rows.reshape(tiles * width, width)
    else:
        w, w_outer = natural

    def tile(t, carry):
        here = pl.multiple_of(t * width, LANES)
        cols = pl.ds(here, width)
        all_cols = pl.ds(pl.multiple_of(first + here, LANES), width)
        if crossed:
            unpack(core, chips, parts, crossed, w_tile, cols)
            wi = weight(w_tile, slice(None))
            wo = w_outer[cols, :]
        else:
            wi = w[:, all_cols]
            wo = w_outer[all_cols, :]
        v = nn(nmid[...], wi) + b_inner[:, all_cols]
        phi = 0.5 * (1.0 + lax.erf(v * (0.5**0.5)))
        act = (v * phi).astype(BF16)
        slope = phi + v * jnp.exp(-0.5 * v * v) * 0.3989422804014327
        acc[...] += nn(act, wo)
        gi = (slope * nt(cot[...], wo)).astype(BF16)
        gb_out[:, cols] = jnp.sum(gi.astype(F32), axis=0, keepdims=True)
        gmid[...] += nt(gi, wi)
        g_outer = tn(act, cot[...])
        g_inner = tn(nmid[...], gi)
        if crossed:
            put_blocks(core, place, 0, g_inner, send, keep, rows_d, cols)
            for at in range(width // (2 * rows_d)):
                d = t * (width // (2 * rows_d)) + at
                where = meta[place_at + d]
                rows = g_outer[2 * at * rows_d : 2 * (at + 1) * rows_d].astype(BF16)
                block = jnp.concatenate([rows[:rows_d], rows[rows_d:]], axis=1)
                folded = slice(tiles * width, (tiles + 2) * width)

                @pl.when(core == at % 2)
                def _(block=block, where=where):
                    keep[where, :, folded] = block

                @pl.when(core != at % 2)
                def _(block=block, where=where):
                    send[where, :, folded] = block
        else:
            keep[0, :width, cols] = g_inner.astype(BF16)
            keep[1, cols, :width] = g_outer.astype(BF16)
        return carry

    lax.fori_loop(0, tiles, tile, 0)


def feed_first_kernel(meta, frames, ctx, vec, b_inner, cot, *refs, crossed, rows_d):
    rows, width = frames.shape
    ff = b_inner.shape[1]
    if crossed:
        parts, refs = refs[:4], refs[4:]
        att, nmid, acc, gmid, gb_out, send, keep, w_out, w_tile, w_rows = refs
        chips = [meta[6 + i] for i in range(len(crossed))]
        unpack(meta[5], chips, parts, crossed, w_out, slice(ff, ff + width))
        wo, natural = weight(w_out, slice(None)), None
    else:
        w, w_outer, att, nmid, acc, gmid, gb_out, send, keep = refs
        parts, natural, w_tile, w_rows = None, (w, w_outer), None, None
        wo = w[:, ff : ff + width]
    attended = frames[...].astype(F32) + nn(ctx[...], wo) + vec[4:5, :]
    att[...] = attended
    n, _ = normalise(attended)
    nmid[...] = (n * vec[5:6, :] + vec[6:7, :]).astype(BF16)
    acc[...] = attended + vec[7:8, :]
    gmid[...] = jnp.zeros_like(gmid)
    feed_tiles(
        meta, "inner", crossed, parts, natural, b_inner, cot, 0, nmid, acc, gmid, gb_out, send, keep, w_tile, w_rows, rows_d
    )


def feed_second_kernel(meta, att, nmid, acc_in, gmid_in, ctx, vec, b_inner, cot, *refs, crossed, rows_d):
    rows, width = att.shape
    ff = b_inner.shape[1]
    if crossed:
        w_out, parts, refs = refs[0], refs[1:5], refs[5:]
        mixed_out, gatt_out, gctx_out, send, keep, gb_out, gvec_out, acc, gmid, w_tile, w_rows = refs
        wo, natural = weight(w_out, slice(None)), None
    else:
        w, w_outer, mixed_out, gatt_out, gctx_out, send, keep, gb_out, gvec_out, acc, gmid = refs
        parts, natural, w_tile, w_rows = None, (w, w_outer), None, None
        wo = w[:, ff : ff + width]
    acc[...] = acc_in[...]
    gmid[...] = gmid_in[...]
    feed_tiles(
        meta, "outer", crossed, parts, natural, b_inner, cot, ff // 2, nmid, acc, gmid, gb_out, send, keep, w_tile, w_rows, rows_d
    )
    mixed_out[...] = acc[...].astype(BF16)
    n, r = normalise(att[...])
    e = gmid[...]
    c32 = cot[...].astype(F32)
    gatt = c32 + norm_backward(n, r, vec[5:6, :], e)
    gatt_out[...] = gatt
    gbr = gatt.astype(BF16)
    gctx_out[...] = nt(gbr, wo).astype(BF16)
    g = tn(ctx[...], gbr)
    if crossed:
        core = meta[5]
        place = [meta[6 + 2 * len(crossed) + i] for i in range(2 * len(crossed))]
        put_blocks(core, place, 0, g, send, keep, rows_d, slice(ff, ff + width))
    else:
        keep[2, :width, :width] = g.astype(BF16)
    gvec_out[0:1, :] = jnp.sum(gbr.astype(F32), axis=0, keepdims=True)
    gvec_out[1:2, :] = jnp.sum(e * n, axis=0, keepdims=True)
    gvec_out[2:3, :] = jnp.sum(e, axis=0, keepdims=True)
    gvec_out[3:4, :] = jnp.sum(c32, axis=0, keepdims=True)
    gvec_out[4:8, :] = jnp.zeros_like(gvec_out[4:8, :])


def moved_lanes(value, moves):
    lane = lax.broadcasted_iota(jnp.int32, (value.shape[0], LANES), 1)
    out = [None] * (value.shape[1] // LANES)
    for source, target, count in moves:
        while count:
            step = min(count, LANES - source % LANES, LANES - target % LANES)
            piece = value[:, source - source % LANES : source - source % LANES + LANES]
            shift = (target - source) % LANES
            piece = pltpu.roll(piece, shift, 1) if shift else piece
            at = target % LANES
            old = out[target // LANES]
            inside = (lane >= at) & (lane < at + step)
            out[target // LANES] = piece if old is None else jnp.where(inside, piece, old)
            source, target, count = source + step, target + step, count - step
    return jnp.concatenate(out, axis=1)


def move_kernel(value, out, *, moves):
    out[...] = moved_lanes(value[...].astype(F32), moves).astype(out.dtype)


def small_blocks(core, place, vecs, inner, grows, bucket_rev, send, keep, columns, rows_d, rows_ff):
    n = len(place)
    span = bucket_rev.shape[1]
    row = lax.broadcasted_iota(jnp.int32, (8, LANES), 0)
    lane = lax.broadcasted_iota(jnp.int32, (8, LANES), 1)
    each = LANES // HEADS
    big = [jnp.where(bucket_rev[1:2, :] == m, grows, 0.0) for m in range(each)]
    big = jnp.concatenate(big + [jnp.zeros((LANES - each * HEADS, span), F32)], axis=0)
    high = big.astype(BF16)
    low = (big - high.astype(F32)).astype(BF16)
    hot = jnp.where(lax.broadcasted_iota(jnp.int32, (n, span), 0) == bucket_rev[0:1, :], 1.0, 0.0).astype(BF16)
    table = nt(hot, high) + nt(hot, low)

    def cut(value, at, count):
        tile, shift = at // LANES, at % LANES
        out = value[:, tile * LANES : (tile + 1) * LANES]
        if shift:
            out = pltpu.roll(out, LANES - shift, 1)
            if shift + count > LANES:
                more = pltpu.roll(value[:, (tile + 1) * LANES : (tile + 2) * LANES], LANES - shift, 1)
                out = jnp.where(lane < LANES - shift, out, more)
        return jnp.where(lane < count, out, 0.0)

    half = rows_ff // 2
    for d in range(n):
        low_rows = jnp.where(row == 0, cut(inner, d * half, half), 0.0)
        low_rows = jnp.where(row == 1, table[d : d + 1], low_rows)
        last_rows = jnp.where(row == 0, cut(inner, (n + d) * half, half), 0.0)
        block = [cut(vecs, d * rows_d, rows_d), low_rows, last_rows]
        block = jnp.concatenate(block + [jnp.zeros((rows_d - 24, LANES), F32)] * (rows_d > 24), axis=0).astype(BF16)
        where = place[d]

        @pl.when(core == d % 2)
        def _(block=block, where=where):
            keep[where, :, columns] = block

        @pl.when(core != d % 2)
        def _(block=block, where=where):
            send[where, :, columns] = block


def attend_back_kernel(
    meta, q, k, v, lse, ctx, gctx, bias_rev, nin, frames, gatt, gin, w, vec, *refs, crossed, rows_d, first, count,
):
    last = first + 2 * count == HEADS
    if last and crossed:
        gvec2, gb_inner, bucket_rev, *refs = refs
        earlier = first // (2 * count)
        before = [(refs[2 * i], refs[2 * i + 1]) for i in range(earlier)]
        refs = refs[2 * earlier :]
    send, keep, gin_out, gvec_out, grow_out, base, gbase, delta_t, kt, dqkv, gk, gv = refs
    rows, width = frames.shape
    unit = rows // UNITS
    window = rows - unit
    head = width // HEADS
    core = meta[5]
    place = [meta[6 + 2 * len(crossed) + i] for i in range(2 * len(crossed))]
    prod = gctx[...].astype(F32) * ctx[...].astype(F32)
    sel_row = lax.broadcasted_iota(jnp.int32, (16, width), 0)
    sel_col = lax.broadcasted_iota(jnp.int32, (16, width), 1)
    sel = jnp.where((sel_col >= sel_row * head) & (sel_col < (sel_row + 1) * head), 1.0, 0.0).astype(BF16)
    high = prod.astype(BF16)
    low = (prod - high.astype(F32)).astype(BF16)
    deltas = nt(sel, high) + nt(sel, low)
    for h in range(HEADS):
        delta_t[h] = deltas[h : h + 1]
    ranges = [unit_range(meta, u, unit) for u in range(UNITS)]
    row_at = lax.broadcasted_iota(jnp.int32, (window, LANES), 0)
    lane = lax.broadcasted_iota(jnp.int32, (unit, LANES), 1)
    sub_lane = lax.broadcasted_iota(jnp.int32, (LANES, unit), 0)
    span = count * LANES

    def pair(step, carry):
        hp = first // 2 + step
        cols = pl.ds(pl.multiple_of(hp * LANES, LANES), LANES)
        here = pl.multiple_of(step * LANES, LANES)
        kt[...] = jnp.transpose(k[:, cols])
        gk[...] = jnp.zeros_like(gk)
        gv[...] = jnp.zeros_like(gv)
        gbase[...] = jnp.zeros_like(gbase)
        for sub in range(2):
            base[sub] = skewed(bias_rev[pl.ds(2 * hp + sub, 1), :], unit)
        for u in range(UNITS):
            lo, hi, ws = ranges[u]
            ws = pl.multiple_of(ws, LANES)
            win = pl.ds(ws, window)
            urows = slice(u * unit, (u + 1) * unit)
            mask = jnp.where((row_at + ws >= lo) & (row_at + ws < hi), 0.0, MASKED).astype(F32)
            kk = k[win, cols]
            vv = v[win, cols]
            qu = q[urows, cols]
            gu = gctx[urows, cols]
            gk_win = gk[win, :]
            gv_win = gv[win, :]
            gq = []
            offsets = [
                pl.ds(pl.multiple_of((rows - unit) + u * unit - ws - jb * unit, LANES), unit) for jb in range(UNITS - 1)
            ]
            for sub in range(2):
                h = 2 * hp + sub
                mine = (lane >= head) == bool(sub)
                qs = jnp.where(mine, qu, jnp.zeros_like(qu))
                gs = jnp.where(mine, gu, jnp.zeros_like(gu))
                rel = jnp.concatenate([base[sub, :, o] for o in offsets], axis=0)
                s = nt(kk, qs) + rel + mask
                p = jnp.exp(s - lse[h, :, urows])
                gp = nt(vv, gs)
                ds = (p * (gp - delta_t[h, :, urows])).astype(BF16)
                gv_win = gv_win + nn(p.astype(BF16), gs)
                gk_win = gk_win + nn(ds, qs)
                gq.append(nn(kt[:, win], ds))
                d32 = ds.astype(F32)
                for jb, o in enumerate(offsets):
                    gbase[sub, :, o] += d32[jb * unit : (jb + 1) * unit]
            gk[win, :] = gk_win
            gv[win, :] = gv_win
            gq_t = jnp.where(sub_lane < head, gq[0], gq[1])
            dqkv[urows, pl.ds(here, LANES)] = jnp.transpose(gq_t).astype(BF16) * BF16(head**-0.5)
        dqkv[:, pl.ds(span + here, LANES)] = gk[...].astype(BF16)
        dqkv[:, pl.ds(2 * span + here, LANES)] = gv[...].astype(BF16)
        for sub in range(2):
            grow_out[pl.ds(2 * step + sub, 1), :] = unskewed_sum(gbase[sub], unit)
        return carry

    grow_out[...] = jnp.zeros_like(grow_out)
    lax.fori_loop(0, count, pair, 0)
    at_columns = first * head
    grad_in = gin[...] if first else jnp.zeros((rows, width), F32)
    for part in range(3):
        d = dqkv[:, part * span : (part + 1) * span]
        grad_in = grad_in + nt(d, weight(w, slice(part * width + at_columns, part * width + at_columns + span)))
    g = tn(nin[...], dqkv[...])
    if crossed:
        put_blocks(core, place, 0, g, send, keep, rows_d, slice(0, 3 * span))
    else:
        keep[:, 0 : 3 * span] = g.astype(BF16)
    sums = [jnp.sum(dqkv[:, at : at + span].astype(F32), axis=0, keepdims=True) for at in (0, 2 * span)]
    gvec_out[...] = jnp.zeros_like(gvec_out)
    gvec_out[2:4, 0:span] = jnp.concatenate(sums, axis=0)
    if not last:
        gin_out[...] = grad_in
        return
    n, r = normalise(frames[...].astype(F32))
    gin_out[...] = (gatt[...] + norm_backward(n, r, vec[0:1, :], grad_in)).astype(BF16)
    gvec_out[0:1, :] = jnp.sum(grad_in * n, axis=0, keepdims=True)
    gvec_out[1:2, :] = jnp.sum(grad_in, axis=0, keepdims=True)
    if crossed:
        for i, (vectors, _) in enumerate(before):
            gvec_out[2:4, i * span : (i + 1) * span] = vectors[2:4, 0:span]
        gvec_out[2:4, at_columns : at_columns + span] = jnp.concatenate(sums, axis=0)
        gvec_out[4:8, :] = gvec2[0:4, :]
        grows = jnp.concatenate([grow[0 : 2 * count, :] for _, grow in before] + [grow_out[0 : 2 * count, :]], axis=0)
        small_blocks(
            core, place, gvec_out[...], jnp.broadcast_to(gb_inner[...], (8, gb_inner.shape[1])), grows, bucket_rev,
            send, keep, slice(3 * span, 3 * span + LANES), rows_d, gb_inner.shape[1] // len(place),
        )


def run_kernel(order, kernel, name, scalars, arrays, outs, scratch=(), spare=10):
    spec = pl.BlockSpec(memory_space=pltpu.VMEM)
    smem = pl.BlockSpec(memory_space=pltpu.SMEM)
    arrays = order.after(*arrays)
    arrays = [pltpu.with_memory_space_constraint(a, pltpu.VMEM) for a in arrays]
    limit = spare * MIB + sum(math.prod(b.shape) * jnp.dtype(b.dtype).itemsize for b in scratch)
    out = pl.pallas_call(
        kernel,
        in_specs=[smem] * len(scalars) + [spec] * len(arrays),
        out_specs=[spec] * len(outs),
        out_shape=[pltpu.VMEM(s, d) for s, d in outs],
        scratch_shapes=list(scratch),
        compiler_params=pltpu.CompilerParams(vmem_limit_bytes=limit),
        cost_estimate=pl.CostEstimate(flops=100_000_000_000, bytes_accessed=100_000_000, transcendentals=0),
        name=name,
    )(*scalars, *arrays)
    order.did(out[0])
    return out


def on_device(
    frames, ln1_gain, ln1_shift, w_query, b_query, w_key, w_value, b_value, w_out, b_out, ln2_gain, ln2_shift,
    w_inner, b_inner, w_outer, b_outer, bias_table, layout, valid, rel_index, cotangent, *, n,
):
    rows, width = frames.shape
    rows_d = w_query.shape[0]
    rows_ff = w_outer.shape[0]
    ff = w_inner.shape[1]
    span = rel_index.shape[0] + 1
    unit = rows // UNITS
    per_table = bias_table.shape[0]
    plan = plan_tables(n)
    core, chips, place = plan
    order = Order()
    direct = (
        rows_d % 8 == 0 and rows_d >= 24 and rows_ff == 4 * rows_d and max(rows_d, rows_ff, per_table) <= LANES and per_table % HEADS == 0
    )
    crossed = tuple(crossed_places(n)) if direct else ()
    crossed_outer = tuple(crossed_places(n, "outer")) if direct else ()
    unit_half = rows_ff // 2
    apart = [(d * rows_ff + h * unit_half, h * ff // 2 + d * unit_half, unit_half) for h in range(2) for d in range(n)]
    together = [(b, a, c) for a, b, c in apart]
    meta = [layout, valid.reshape(-1), core[None]]
    if direct:
        _, chips_outer, place_outer = plan_tables(n, "outer")
        meta += [chips, chips_outer, place, place_outer]
    meta = jnp.concatenate(meta).astype(jnp.int32)
    small_d = jnp.stack([ln1_gain, ln1_shift, b_query, b_value, b_out, ln2_gain, ln2_shift, b_outer])

    base = pltpu.VMEM((2, unit, span), F32)
    if direct:
        wide = [small_d, b_inner[None, :unit_half], bias_table[None], jnp.zeros((6, 1), BF16), b_inner[None, unit_half:]]
        wide = jnp.concatenate([jnp.pad(a, ((0, 0), (0, LANES - a.shape[1]))) for a in wide])
        small = jnp.pad(wide, ((0, rows_d - wide.shape[0]), (0, 0)))
        g1 = Gather(jnp.concatenate([w_query, w_key, w_value, small], axis=1), n, order)
        (halves,) = run_kernel(
            Order(), functools.partial(move_kernel, moves=apart), "apart", [], [w_inner], [((rows_d, ff), BF16)]
        )
        fold = [w_outer[i * rows_d : (i + 1) * rows_d] for i in range(4)]
        part3 = jnp.concatenate([halves[:, ff // 2 :], fold[2], fold[3]], axis=1)
        g3 = Gather(part3, n, order, "outer")
        part2 = jnp.concatenate([halves[:, : ff // 2], fold[0], fold[1], w_out], axis=1)
        (part2,) = lax.optimization_barrier((part2, g1.got, g3.got))[:1]
        g2 = Gather(part2, n, order)
        for g in (g1, g1, g2, g1, g2, g3, g2, g3):
            g.step()
        first = g1.finish()
        each = per_table // HEADS
        index = jnp.stack([rel_index // each, rel_index % each])
        bucket_rev = jnp.pad(index[:, ::-1], ((0, 6), (0, 1)), constant_values=-1)
        q, k, v, nin, w1, vec, inner_bias, bias_rev = run_kernel(
            order, functools.partial(project_kernel, crossed=crossed, rows_d=rows_d, rows_ff=rows_ff), "project", [meta],
            [frames, *first, bucket_rev],
            [((rows, width), BF16)] * 4
            + [((n // 2, 2 * rows_d, 3 * width), BF16), ((8, width), F32), ((1, ff), F32), ((16, span), F32)],
            [
                pltpu.VMEM((width // LANES + 1, 8, LANES), F32),
                pltpu.VMEM((ff // LANES + 1, 8, LANES), F32),
                pltpu.VMEM((n, LANES), F32),
            ],
        )
        chunk = [[((n // 2, rows_d, c), BF16)] * 2 for c in (ff, ff + width)]
        w_out_whole = [((n // 2, 2 * rows_d, width), BF16)]
        unpacked = [pltpu.VMEM((n // 2, 2 * rows_d, width), BF16), pltpu.VMEM((n // 2, rows_ff, width), BF16)]
    else:
        flat = jnp.concatenate([small_d.reshape(-1), b_inner, bias_table])
        per = flat.shape[0] // rows_d
        small = jnp.pad(flat.reshape(rows_d, per), ((0, 0), (0, LANES - per)))
        w1 = gathered(Gather(jnp.concatenate([w_query, w_key, w_value, small], axis=1), n, order).finish(), plan, n)
        w2 = (gathered(Gather(jnp.concatenate([w_inner, w_out], axis=1), n, order).finish(), plan, n),)
        w2 += (gathered(Gather(w_outer, n, order).finish(), plan, n),)
        flats = w1[:, 3 * width : 3 * width + per].reshape(n, rows_d * per)
        vec = flats[:, : 8 * rows_d].reshape(n, 8, rows_d).transpose(1, 0, 2).reshape(8, width).astype(F32)
        inner_bias = flats[:, 8 * rows_d : 8 * rows_d + rows_ff].reshape(1, ff).astype(F32)
        table = jnp.pad(flats[:, 8 * rows_d + rows_ff :].reshape(-1, HEADS), ((0, 0), (0, 16 - HEADS)))
        index_rev = jnp.pad(rel_index[::-1], (0, 1), constant_values=-1)
        ids = jnp.arange(table.shape[0], dtype=jnp.int32)[:, None]
        bias_rev = tn(table, (ids == index_rev[None]).astype(BF16))
        q, k, v, nin = run_kernel(
            order, project_body, "project", [meta], [frames, w1, vec], [((rows, width), BF16)] * 4
        )
        chunk = [[((8, LANES), BF16), ((c, max(width, ff // 2), max(width, ff // 2)), BF16)] for c in (2, 3)]
        w_out_whole = []
        unpacked = []

    ctx, lse = run_kernel(
        order, attend_kernel, "attend", [meta], [q, k, v, bias_rev],
        [((rows, width), BF16), ((HEADS, 1, rows), F32)], [base, pltpu.VMEM((LANES, rows), BF16)], spare=4,
    )

    def start(send, keep, scatter):
        return scatter.add(*((send, keep) if direct else split_natural(keep, plan, n)))

    if direct:
        g3.step()
        w2 = g2.finish()
    att, nmid, acc, gmid, gb1, send1, keep1, *w_out_all = run_kernel(
        order, functools.partial(feed_first_kernel, crossed=crossed, rows_d=rows_d), "feed_first", [meta],
        [frames, ctx, vec, inner_bias, cotangent, *w2],
        [((rows, width), F32), ((rows, width), BF16), ((rows, width), F32), ((rows, width), F32), ((1, ff // 2), F32)]
        + chunk[0] + w_out_whole,
        unpacked, spare=12,
    )
    if direct:
        w3 = g3.finish()
        begin = functools.partial(Scatter, n, order)
        sum_1 = begin("outer").add(send1, keep1)
    else:
        w3 = w2
    mixed, gatt, gctx, send2, keep2, gb2, gvec2 = run_kernel(
        order, functools.partial(feed_second_kernel, crossed=crossed_outer, rows_d=rows_d), "feed_second", [meta],
        [att, nmid, acc, gmid, ctx, vec, inner_bias, cotangent, *w_out_all, *w3],
        [((rows, width), BF16), ((rows, width), F32), ((rows, width), BF16)] + chunk[1]
        + [((1, ff // 2), F32), ((8, width), F32)],
        [pltpu.VMEM((rows, width), F32)] * 2 + unpacked, spare=12,
    )
    gb_inner = jnp.concatenate([gb1, gb2], axis=1)
    if direct:
        sum_1.step()
        sum_2 = begin().add(send2, keep2)
    else:
        whole_inner = jnp.concatenate([keep1[0, :width, : ff // 2], keep2[0, :width, : ff // 2], keep2[2, :width, :width]], axis=1)
        whole_outer = jnp.concatenate([keep1[1, : ff // 2, :width], keep2[1, : ff // 2, :width]], axis=0)
        begin = functools.partial(Scatter, n, order)
        sum_1 = begin().add(*split_natural(whole_outer, plan, n))
        sum_2 = begin().add(*split_natural(whole_inner, plan, n))

    count = 2
    cols = count * LANES
    passed = gatt
    done, earlier = [], []
    sum_early, sum_late = begin(), begin()
    calls = HEADS // (2 * count)
    for call in range(calls):
        last = call == calls - 1
        wide = 3 * cols + LANES * (last and direct)
        part = [((n // 2, rows_d, wide), BF16)] * 2 if direct else [((8, LANES), BF16), ((width, wide), BF16)]
        extra = [gvec2, gb_inner, bucket_rev] + [a for pair in earlier for a in pair] if last and direct else []
        send, keep, passed, gvec1, grow = run_kernel(
            order,
            functools.partial(
                attend_back_kernel, crossed=crossed, rows_d=rows_d, first=call * 2 * count, count=count
            ),
            "attend_back", [meta],
            [q, k, v, lse, ctx, gctx, bias_rev, nin, frames, gatt, passed, w1, vec] + extra,
            part + [((rows, width), BF16 if last else F32), ((8, width), F32), ((8, span), F32)],
            [
                base, base,
                pltpu.VMEM((HEADS, 1, rows), F32),
                pltpu.VMEM((LANES, rows), BF16),
                pltpu.VMEM((rows, 3 * cols), BF16),
                pltpu.VMEM((rows, LANES), F32),
                pltpu.VMEM((rows, LANES), F32),
            ],
            spare=10,
        )
        earlier.append((gvec1, grow))
        start(send, keep, sum_late if last else sum_early)
        if call == 0:
            sum_2.step()
        if call == 1:
            sum_1.step()
    tail = [sum_2, sum_early, sum_1, sum_late, sum_2, sum_early, sum_late, sum_1, sum_2, sum_early, sum_late, sum_early, sum_late]
    for each_sum in tail:
        if each_sum.steps:
            each_sum.step()
    sum_1, sum_2, early, late = sum_1.finish(), sum_2.finish(), sum_early.finish(), sum_late.finish()
    if direct:
        both = jnp.concatenate([sum_1[:, : ff // 2], sum_2[:, : ff // 2]], axis=1)
        (grad_inner,) = run_kernel(
            Order(), functools.partial(move_kernel, moves=together), "together", [], [both], [((rows_d, ff), F32)]
        )
        folded = (sum_1[:, ff // 2 :], sum_2[:, ff // 2 : ff])
        grad_outer = jnp.concatenate([f[:, i * width : (i + 1) * width] for f in folded for i in range(2)], axis=0)
    else:
        grad_inner, grad_outer = sum_2[:, :ff], sum_1
    pieces = [early[:, i * 3 * cols : (i + 1) * 3 * cols] for i in range(calls - 1)] + [late[:, : 3 * cols]]
    sum_q, sum_k, sum_v = (jnp.concatenate([p[:, i * cols : (i + 1) * cols] for p in pieces], axis=1) for i in range(3))
    if direct:
        small = late[:, 3 * cols :]
        vecs = small[:8, :rows_d]
        sum_b_inner = jnp.concatenate([small[8, :unit_half], small[16, :unit_half]])
        sum_table = small[9, :per_table]
    else:
        hot_rev = (ids == index_rev[None]).astype(F32)
        grow = jnp.concatenate([g[: 2 * count] for _, g in earlier])
        gtable = lax.dot_general(
            hot_rev, grow, (((1,), (1,)), ((), ())), precision=lax.Precision.HIGHEST, preferred_element_type=F32
        )
        gbias = jnp.concatenate([g[2:4, :cols] for g, _ in earlier], axis=1)
        gsmall = jnp.concatenate([gvec1[0:2], gbias, gvec2[0:4]])
        gsmall = gsmall.reshape(8, n, rows_d).transpose(1, 0, 2).reshape(n, 8 * rows_d)
        gflat = jnp.concatenate([gsmall, gb_inner.reshape(n, rows_ff), gtable.reshape(n, -1)], axis=1)
        gflat = jnp.pad(gflat, ((0, 0), (0, -gflat.shape[1] % LANES))).astype(BF16)
        sum_flat = Scatter(n, order).add(*split_natural(gflat, plan, n)).finish()[0]
        vecs = sum_flat[: 8 * rows_d].reshape(8, rows_d)
        sum_b_inner = sum_flat[8 * rows_d : 8 * rows_d + rows_ff]
        sum_table = sum_flat[8 * rows_d + rows_ff : 8 * rows_d + rows_ff + per_table]
    return (
        mixed, passed, vecs[0], vecs[1], sum_q, vecs[2], sum_k, sum_v, vecs[3],
        sum_2[:, ff:], vecs[4], vecs[5], vecs[6], grad_inner, sum_b_inner, grad_outer, vecs[7], sum_table,
    )


def solution(mesh):
    row, two = P("dp"), P("dp", None)
    in_specs = (two, row, row, two, row, two, two, row, two, row, row, row, two, row, two, row, row, row, two, P(), two)
    out_specs = (two, two, row, row, two, row, two, two, row, two, row, row, row, two, row, two, row, row)
    return jax.shard_map(
        functools.partial(on_device, n=mesh.shape["dp"]),
        mesh=mesh, in_specs=in_specs, out_specs=out_specs, check_vma=False,
    )
```

```python
import functools
import math

import jax
import jax.numpy as jnp
import numpy as np
from jax import lax
from jax.experimental import pallas as pl
from jax.experimental.pallas import tpu as pltpu
from jax.sharding import PartitionSpec as P

HEADS = 12
LANES = 128
UNITS = 4
MASKED = -1e30
F32 = jnp.float32
BF16 = jnp.bfloat16
SEGMENT = ((0, 0, 0, 1), (0, 0, 1, 1), (0, 0, 1, 2), (0, 1, 2, 3))
START = ((0, 0, 0, 3), (0, 0, 2, 2), (0, 0, 2, 3), (0, 1, 2, 3))
MIB = 1024 * 1024


def bit_orders(n, kind):
    chip = [1 << k for k in range(1, n.bit_length() - 1)]
    low, high = chip[:2], chip[2:][::-1]
    if kind == "outer":
        return (low[:1] + high + low[1:], low[1:] + high + low[:1])
    return (high + low, high + low[::-1])


def gather_masks(bits):
    masks = [0]
    for bit in bits:
        masks = masks + [bit ^ m for m in masks]
    return masks


def scatter_masks(bits):
    masks = [0]
    for bit in bits:
        masks = [bit ^ m for m in masks] + masks
    return masks


def pairs(n, by_core):
    return [(i, i ^ by_core[i & 1]) for i in range(n)]


class Order:
    def __init__(self):
        self.last = None

    def after(self, *arrays):
        if self.last is None:
            return arrays
        return lax.optimization_barrier((*arrays, self.last))[:-1]

    def did(self, array):
        self.last = array


class Gather:
    def __init__(self, part, n, order, kind="inner"):
        self.n = n
        self.order = order
        self.steps = list(zip(*bit_orders(n, kind)))
        self.held = part if part.ndim == 3 else part[None]
        self.got = lax.ppermute(self.held, "dp", pairs(n, self.steps.pop(0)))

    def step(self):
        pair = self.order.after(self.held, self.got)
        self.held = jnp.concatenate(pair, axis=0)
        self.order.did(self.held)
        self.got = lax.ppermute(self.held, "dp", pairs(self.n, self.steps.pop(0)))
        return self

    def finish(self):
        while self.steps:
            self.step()
        (self.got,) = self.order.after(self.got)
        swap = pairs(self.n, (1, 1))
        return (self.held, self.got, lax.ppermute(self.held, "dp", swap), lax.ppermute(self.got, "dp", swap))


class Scatter:
    def __init__(self, n, order, kind="inner"):
        self.n = n
        self.order = order
        self.parts = []
        self.terms = []
        self.late = []
        self.at = 0
        self.steps = list(reversed(list(zip(*bit_orders(n, kind)))))
        self.half = n // 4

    def add(self, send, keep):
        self.parts.append((keep, lax.ppermute(send, "dp", pairs(self.n, (1, 1)))))
        return self

    def total(self, count, dtype):
        flat = [t for part in self.parts for t in part] + [t for t, _ in self.terms]
        flat = list(self.order.after(*flat))
        at = self.at
        cut = [lax.slice_in_dim(t, at, at + count).astype(F32) for t in flat[: 2 * len(self.parts)]]
        out = [cut[2 * i] + cut[2 * i + 1] for i in range(len(self.parts))]
        out = out[0] if len(out) == 1 else jnp.concatenate(out, axis=-1)
        for t, (_, first) in zip(flat[2 * len(self.parts) :], self.terms):
            out = out + lax.slice_in_dim(t, at - first, at - first + count).astype(F32)
        out = out.astype(dtype)
        self.order.did(out)
        return out

    def step(self):
        by_core = self.steps.pop(0)
        out = self.total(self.half, BF16)
        self.at += self.half
        self.terms.append((lax.ppermute(out, "dp", pairs(self.n, by_core)), self.at))
        self.half //= 2

    def last_steps(self):
        masks = scatter_masks([by_core[0] for by_core in self.steps[::-1]])
        self.steps = []
        for mask in masks[:-1]:
            out = self.total(1, BF16)
            self.at += 1
            self.late.append(lax.ppermute(out, "dp", pairs(self.n, (mask, mask))))

    def finish(self):
        while self.steps:
            self.step()
        self.terms += [(t, self.at) for t in self.late]
        return self.total(1, F32)[0]


def plan_tables(n, kind="inner"):
    orders = bit_orders(n, kind)
    me = lax.axis_index("dp")
    core = me & 1
    g = np.array([gather_masks(o) for o in orders], np.int32)
    s = np.array([scatter_masks(o) for o in orders], np.int32)
    inverse = np.zeros((2, n), np.int32)
    for c in (0, 1):
        for i, m in enumerate(s[c]):
            inverse[c, m] = i
    devices = jnp.arange(n, dtype=jnp.int32)
    chips = (me ^ jnp.where(core == 0, jnp.asarray(g[0]), jnp.asarray(g[1]))) >> 1
    mask = (devices ^ me) & ~1
    place = jnp.sum(jnp.where(mask[:, None] == devices[None, :], jnp.asarray(inverse)[np.arange(n) % 2], 0), axis=1)
    return core, chips, place


def crossed_places(n, kind="inner"):
    first, second = (gather_masks(o) for o in bit_orders(n, kind))
    places = [second.index(m) for m in first]
    assert places == [first.index(m) for m in second]
    return places


def gathered(parts, plan, n):
    core, chips, _ = plan
    mine = jnp.concatenate(parts[:2])
    theirs = jnp.concatenate(parts[2:])[np.array(crossed_places(n))]
    both = jnp.where(core == 0, jnp.stack([mine, theirs], 1), jnp.stack([theirs, mine], 1))
    return both[jnp.argsort(chips)].reshape(n * mine.shape[1], mine.shape[2])


def split_natural(grad, plan, n):
    core, _, place = plan
    rows = grad.shape[0] // n
    blocks = grad.reshape(n // 2, 2, rows, grad.shape[1])
    mine = jnp.where(core == 0, blocks[:, 0], blocks[:, 1])
    theirs = jnp.where(core == 0, blocks[:, 1], blocks[:, 0])
    both = place.reshape(n // 2, 2)
    my_place = jnp.where(core == 0, both[:, 0], both[:, 1])
    their_place = jnp.where(core == 0, both[:, 1], both[:, 0])
    return theirs[jnp.argsort(their_place)], mine[jnp.argsort(my_place)]


def nn(a, b):
    return jnp.dot(a, b, preferred_element_type=F32)


def nt(a, b):
    return lax.dot_general(a, b, (((1,), (1,)), ((), ())), preferred_element_type=F32)


def tn(a, b):
    return lax.dot_general(a, b, (((0,), (0,)), ((), ())), preferred_element_type=F32)


def normalise(v):
    centred = v - jnp.mean(v, axis=-1, keepdims=True)
    r = lax.rsqrt(jnp.mean(centred * centred, axis=-1, keepdims=True) + 1e-05)
    return centred * r, r


def norm_backward(n, r, gain, e):
    eg = e * gain
    return r * (eg - jnp.mean(eg, axis=-1, keepdims=True) - n * jnp.mean(eg * n, axis=-1, keepdims=True))


def pick(table, code, u):
    out = jnp.int32(table[0][u])
    for c in range(1, 4):
        out = jnp.where(code == c, jnp.int32(table[c][u]), out)
    return out


def unit_range(meta, u, unit):
    code = meta[0]
    segment = pick(SEGMENT, code, u)
    start = pick(START, code, u)
    count = meta[1]
    for s in range(1, 4):
        count = jnp.where(segment == s, meta[1 + s], count)
    window = jnp.minimum(start, 1) * unit
    return start * unit, start * unit + count, window


def put_masks(meta, masks):
    units, window, unit = masks.shape
    row_at = lax.broadcasted_iota(jnp.int32, (window, unit), 0)
    starts = []
    for u in range(units):
        first, end, start = unit_range(meta, u, unit)
        masks[u] = jnp.where((row_at + start >= first) & (row_at + start < end), 0.0, MASKED)
        starts.append(start)
    return starts


def skewed(row, unit):
    wide = jnp.broadcast_to(row, (unit, row.shape[1]))
    return pltpu.roll(wide, row.shape[1] - (unit - 1), 1, stride=1, stride_axis=0)


def unskewed_sum(block, unit):
    width = block.shape[1]
    total = None
    for a in range(unit // 8):
        part = block[8 * a : 8 * a + 8]
        shift = (unit - 1 - 8 * a) % width
        part = pltpu.roll(part, shift, 1) if shift else part
        total = part if total is None else total + part
    out = total[0:1]
    for s in range(1, 8):
        out = out + pltpu.roll(total[s : s + 1], width - s, 1)
    return out


def unpack(core, chips, parts, crossed, out, columns):
    half = parts[0].shape[0]
    for i, j in enumerate(crossed):
        mine = parts[i // half][i % half, :, columns]
        theirs = parts[2 + j // half][j % half, :, columns]
        first = jnp.where(core == 0, mine, theirs)
        second = jnp.where(core == 0, theirs, mine)
        out[chips[i]] = jnp.concatenate([first, second], axis=0)


def weight(ref, columns):
    value = ref[..., columns]
    return value.reshape(-1, value.shape[-1])


def put_blocks(core, places, blocks, send, keep, columns):
    for plane in range(2):

        @pl.when(core == plane)
        def _(plane=plane):
            for at, (place, block) in enumerate(zip(places, blocks)):
                (keep if at % 2 == plane else send)[place, :, columns] = block.astype(BF16)


def row_blocks(value, rows):
    return [value[at : at + rows] for at in range(0, value.shape[0], rows)]


def project_body(meta, frames, w, vec, q_out, k_out, v_out, nin_out):
    width = frames.shape[1]
    head = width // HEADS
    n, _ = normalise(frames[...].astype(F32))
    nin = (n * vec[0:1, :] + vec[1:2, :]).astype(BF16)
    nin_out[...] = nin
    q_out[...] = ((nn(nin, weight(w, slice(0, width))) + vec[2:3, :]) * (head**-0.5)).astype(BF16)
    k_out[...] = nn(nin, weight(w, slice(width, 2 * width))).astype(BF16)
    v_out[...] = (nn(nin, weight(w, slice(2 * width, 3 * width))) + vec[3:4, :]).astype(BF16)


def apart_heads(rows, lane, head):
    zero = jnp.zeros_like(rows)
    return jnp.concatenate([jnp.where(lane < head, rows, zero), jnp.where(lane < head, zero, rows)], axis=0)


def attend_kernel(meta, q, k, v, bias_rev, ctx_out, lse_out, base, vt, masks):
    rows, width = q.shape
    unit = rows // UNITS
    window = rows - unit
    head = width // HEADS
    ranges = put_masks(meta, masks)
    lane = lax.broadcasted_iota(jnp.int32, (unit, LANES), 1)
    sub_lane = lax.broadcasted_iota(jnp.int32, (LANES, unit), 0)

    def pair(hp, carry):
        cols = pl.ds(pl.multiple_of(hp * LANES, LANES), LANES)
        vt[...] = jnp.transpose(v[:, cols])
        for sub in range(2):
            base[sub] = skewed(bias_rev[pl.ds(2 * hp + sub, 1), :], unit)
        for u in range(UNITS):
            ws = pl.multiple_of(ranges[u], LANES)
            win = pl.ds(ws, window)
            urows = slice(u * unit, (u + 1) * unit)
            kk = k[win, cols]
            qu = q[urows, cols]
            offsets = [
                pl.ds(pl.multiple_of((rows - unit) + u * unit - ws - jb * unit, LANES), unit) for jb in range(UNITS - 1)
            ]
            parts = []
            for sub in range(2):
                qs = jnp.where((lane >= head) == bool(sub), qu, jnp.zeros_like(qu))
                rel = jnp.concatenate([base[sub, :, o] for o in offsets], axis=0)
                s = nt(kk, qs) + rel + masks[u]
                top = jnp.max(s, axis=0, keepdims=True)
                e = jnp.exp(s - top)
                tot = jnp.sum(e, axis=0, keepdims=True)
                parts.append(nn(vt[:, win], e.astype(BF16)) * (1.0 / tot))
                lse_out[2 * hp + sub, :, urows] = top + jnp.log(tot)
            ctx_out[urows, cols] = jnp.transpose(jnp.where(sub_lane < head, parts[0], parts[1])).astype(BF16)
        return carry

    lax.fori_loop(0, HEADS // 2, pair, 0)


def small_vectors(core, chips, parts, crossed, at, rows_d, rows_ff, vec3, inner3, table):
    half = parts[0].shape[0]
    lane = lax.broadcasted_iota(jnp.int32, (8, LANES), 1)
    vec3[...] = jnp.zeros_like(vec3)
    inner3[...] = jnp.zeros_like(inner3)
    for i, j in enumerate(crossed):
        mine = parts[i // half][i % half, :, at : at + LANES].astype(F32)
        theirs = parts[2 + j // half][j % half, :, at : at + LANES].astype(F32)
        for plane in range(2):
            block = jnp.where(core == plane, mine, theirs)
            d = 2 * chips[i] + plane
            unit_half = rows_ff // 2
            half_at = 2 * half * rows_ff
            for first, rows, part, out in (
                (0, rows_d, block[0:8], vec3),
                (0, unit_half, block[8:16], inner3),
                (half_at, unit_half, block[16:24], inner3),
            ):
                start = first + d * rows
                tile = start >> 7
                shift = start & (LANES - 1)
                rolled = pltpu.roll(part, shift, 1)
                out[tile] += jnp.where(lane >= shift, rolled, 0.0)
                out[tile + 1] += jnp.where(lane < shift, rolled, 0.0)
            table[pl.ds(d, 1), :] = block[9:10]


def relative_rows(bucket, table, out):
    devices = lax.broadcasted_iota(jnp.int32, (table.shape[0], bucket.shape[1]), 0)
    hot = jnp.where(devices == bucket[0:1, :], 1.0, 0.0).astype(BF16)
    rows = tn(table[...].astype(BF16), hot)
    total = jnp.zeros((HEADS, bucket.shape[1]), F32)
    for m in range(LANES // HEADS):
        total = total + jnp.where(bucket[1:2, :] == m, rows[m * HEADS : (m + 1) * HEADS], 0.0)
    out[0:HEADS, :] = total
    out[HEADS:, :] = jnp.zeros_like(out[HEADS:, :])


def project_kernel(
    meta, frames, p0, p1, p2, p3, bucket_rev,
    q_out, k_out, v_out, nin_out, w, vec, b_inner, bias_rev,
    vec3, inner3, table, *, crossed, rows_d, rows_ff,
):
    width = frames.shape[1]
    core = meta[5]
    chips = [meta[6 + i] for i in range(len(crossed))]
    parts = (p0, p1, p2, p3)
    small_vectors(core, chips, parts, crossed, 3 * width, rows_d, rows_ff, vec3, inner3, table)
    for a in range(width // LANES):
        vec[:, a * LANES : (a + 1) * LANES] = vec3[a]
    for a in range(b_inner.shape[1] // LANES):
        b_inner[:, a * LANES : (a + 1) * LANES] = inner3[a, 0:1]
    relative_rows(bucket_rev, table, bias_rev)
    unpack(core, chips, parts, crossed, w, slice(0, 3 * width))
    project_body(meta, frames, w, vec, q_out, k_out, v_out, nin_out)


def unpack_folded(core, chips, parts, crossed, out, at, width):
    half = parts[0].shape[0]
    for i, j in enumerate(crossed):
        mine = parts[i // half][i % half, :, at : at + 2 * width]
        theirs = parts[2 + j // half][j % half, :, at : at + 2 * width]
        first = jnp.where(core == 0, mine, theirs)
        second = jnp.where(core == 0, theirs, mine)
        rows = [first[:, :width], first[:, width:], second[:, :width], second[:, width:]]
        out[chips[i]] = jnp.concatenate(rows, axis=0)


def feed_tiles(meta, kind, crossed, parts, natural, b_inner, cot, first, nmid, acc, gmid, gb_out, send, keep, w_tile, w_rows, rows_d):
    width = nmid.shape[1]
    tiles = b_inner.shape[1] // width // 2
    if crossed:
        half = len(crossed)
        core = meta[5]
        chips_at = 6 + half * (kind == "outer")
        chips = [meta[chips_at + i] for i in range(half)]
        place_at = 6 + 2 * half + 2 * half * (first == 0)
        place = [meta[place_at + i] for i in range(2 * half)]
        unpack_folded(core, chips, parts, crossed, w_rows, tiles * width, width)
        w_outer = w_rows.reshape(tiles * width, width)
    else:
        w, w_outer = natural

    def tile(t, carry):
        here = pl.multiple_of(t * width, LANES)
        cols = pl.ds(here, width)
        all_cols = pl.ds(pl.multiple_of(first + here, LANES), width)
        if crossed:
            unpack(core, chips, parts, crossed, w_tile, cols)
            wi = weight(w_tile, slice(None))
            wo = w_outer[cols, :]
        else:
            wi = w[:, all_cols]
            wo = w_outer[all_cols, :]
        v = nn(nmid[...], wi) + b_inner[:, all_cols]
        phi = 0.5 * (1.0 + lax.erf(v * (0.5**0.5)))
        act = (v * phi).astype(BF16)
        slope = phi + v * jnp.exp(-0.5 * v * v) * 0.3989422804014327
        acc[...] += nn(act, wo)
        gi = (slope * nt(cot[...], wo)).astype(BF16)
        gb_out[:, cols] = jnp.sum(gi.astype(F32), axis=0, keepdims=True)
        gmid[...] += nt(gi, wi)
        g_outer = tn(act, cot[...])
        g_inner = tn(nmid[...], gi)
        if crossed:
            put_blocks(core, place, row_blocks(g_inner, rows_d), send, keep, cols)
            per = width // (2 * rows_d)
            places = [meta[place_at + t * per + at] for at in range(per)]
            rows = row_blocks(g_outer, rows_d)
            blocks = [jnp.concatenate(rows[2 * at : 2 * at + 2], axis=1) for at in range(per)]
            put_blocks(core, places, blocks, send, keep, slice(tiles * width, (tiles + 2) * width))
        else:
            keep[0, :width, cols] = g_inner.astype(BF16)
            keep[1, cols, :width] = g_outer.astype(BF16)
        return carry

    lax.fori_loop(0, tiles, tile, 0)


def feed_first_kernel(meta, frames, ctx, vec, b_inner, cot, *refs, crossed, rows_d):
    rows, width = frames.shape
    ff = b_inner.shape[1]
    if crossed:
        parts, refs = refs[:4], refs[4:]
        att, nmid, acc, gmid, gb_out, send, keep, w_out, w_tile, w_rows = refs
        chips = [meta[6 + i] for i in range(len(crossed))]
        unpack(meta[5], chips, parts, crossed, w_out, slice(ff, ff + width))
        wo, natural = weight(w_out, slice(None)), None
    else:
        w, w_outer, att, nmid, acc, gmid, gb_out, send, keep = refs
        parts, natural, w_tile, w_rows = None, (w, w_outer), None, None
        wo = w[:, ff : ff + width]
    attended = frames[...].astype(F32) + nn(ctx[...], wo) + vec[4:5, :]
    att[...] = attended
    n, _ = normalise(attended)
    nmid[...] = (n * vec[5:6, :] + vec[6:7, :]).astype(BF16)
    acc[...] = attended + vec[7:8, :]
    gmid[...] = jnp.zeros_like(gmid)
    feed_tiles(
        meta, "inner", crossed, parts, natural, b_inner, cot, 0, nmid, acc, gmid, gb_out, send, keep, w_tile, w_rows, rows_d
    )


def feed_second_kernel(meta, att, nmid, acc_in, gmid_in, ctx, vec, b_inner, cot, *refs, crossed, rows_d):
    rows, width = att.shape
    ff = b_inner.shape[1]
    if crossed:
        w_out, parts, refs = refs[0], refs[1:5], refs[5:]
        mixed_out, gatt_out, gctx_out, send, keep, gb_out, gvec_out, acc, gmid, w_tile, w_rows = refs
        wo, natural = weight(w_out, slice(None)), None
    else:
        w, w_outer, mixed_out, gatt_out, gctx_out, send, keep, gb_out, gvec_out, acc, gmid = refs
        parts, natural, w_tile, w_rows = None, (w, w_outer), None, None
        wo = w[:, ff : ff + width]
    acc[...] = acc_in[...]
    gmid[...] = gmid_in[...]
    feed_tiles(
        meta, "outer", crossed, parts, natural, b_inner, cot, ff // 2, nmid, acc, gmid, gb_out, send, keep, w_tile, w_rows, rows_d
    )
    mixed_out[...] = acc[...].astype(BF16)
    n, r = normalise(att[...])
    e = gmid[...]
    c32 = cot[...].astype(F32)
    gatt = c32 + norm_backward(n, r, vec[5:6, :], e)
    gatt_out[...] = gatt
    gbr = gatt.astype(BF16)
    gctx_out[...] = nt(gbr, wo).astype(BF16)
    gvec_out[0:1, :] = jnp.sum(gbr.astype(F32), axis=0, keepdims=True)
    gvec_out[1:2, :] = jnp.sum(e * n, axis=0, keepdims=True)
    gvec_out[2:3, :] = jnp.sum(e, axis=0, keepdims=True)
    gvec_out[3:4, :] = jnp.sum(c32, axis=0, keepdims=True)
    gvec_out[4:8, :] = jnp.zeros_like(gvec_out[4:8, :])


def moved_lanes(value, moves):
    lane = lax.broadcasted_iota(jnp.int32, (value.shape[0], LANES), 1)
    out = [None] * (value.shape[1] // LANES)
    for source, target, count in moves:
        while count:
            step = min(count, LANES - source % LANES, LANES - target % LANES)
            piece = value[:, source - source % LANES : source - source % LANES + LANES]
            shift = (target - source) % LANES
            piece = pltpu.roll(piece, shift, 1) if shift else piece
            at = target % LANES
            old = out[target // LANES]
            inside = (lane >= at) & (lane < at + step)
            out[target // LANES] = piece if old is None else jnp.where(inside, piece, old)
            source, target, count = source + step, target + step, count - step
    return jnp.concatenate(out, axis=1)


def pack_first_kernel(*refs, rows_ff):
    w_query, w_key, w_value, *vectors, b_inner, table, out, small = refs
    rows, width = w_query.shape
    for i, part in enumerate((w_query, w_key, w_value)):
        out[0, :, i * width : (i + 1) * width] = part[...]
    half = rows_ff // 2
    small[...] = jnp.zeros_like(small)
    for i, vector in enumerate(vectors):
        small[i : i + 1, 0:rows] = vector[...].astype(F32)
    small[8:9, 0:half] = b_inner[:, 0:half].astype(F32)
    small[9:10, 0 : table.shape[1]] = table[...].astype(F32)
    small[16:17, 0:half] = b_inner[:, half:].astype(F32)
    out[0, :, 3 * width :] = small[...].astype(BF16)


def pack_feed_kernel(w_inner, w_outer, w_out, second, third, *, moves):
    rows, width = w_out.shape
    half = w_inner.shape[1] // 2
    inner = moved_lanes(w_inner[...].astype(F32), moves).astype(BF16)
    for part, out in enumerate((second, third)):
        out[0, :, 0:half] = inner[:, part * half : (part + 1) * half]
        for i in range(2):
            at = (2 * part + i) * rows
            out[0, :, half + i * width : half + (i + 1) * width] = w_outer[at : at + rows, :]
    second[0, :, 2 * half :] = w_out[...]


def columns_kernel(*refs, count):
    *pieces, q_out, k_out, v_out = refs
    at = 0
    for piece in pieces:
        for first in range(0, piece.shape[1] // (3 * count) * 3 * count, 3 * count):
            for i, out in enumerate((q_out, k_out, v_out)):
                out[:, at : at + count] = piece[:, first + i * count : first + (i + 1) * count]
            at += count


def move_kernel(value, out, *, moves):
    out[...] = moved_lanes(value[...].astype(F32), moves).astype(out.dtype)


def small_blocks(core, place, vecs, inner, grows, bucket_rev, send, keep, columns, rows_d, rows_ff):
    n = len(place)
    span = bucket_rev.shape[1]
    row = lax.broadcasted_iota(jnp.int32, (8, LANES), 0)
    lane = lax.broadcasted_iota(jnp.int32, (8, LANES), 1)
    each = LANES // HEADS
    big = [jnp.where(bucket_rev[1:2, :] == m, grows, 0.0) for m in range(each)]
    big = jnp.concatenate(big + [jnp.zeros((LANES - each * HEADS, span), F32)], axis=0)
    high = big.astype(BF16)
    low = (big - high.astype(F32)).astype(BF16)
    hot = jnp.where(lax.broadcasted_iota(jnp.int32, (n, span), 0) == bucket_rev[0:1, :], 1.0, 0.0).astype(BF16)
    table = nt(hot, high) + nt(hot, low)

    def cut(value, at, count):
        tile, shift = at // LANES, at % LANES
        out = value[:, tile * LANES : (tile + 1) * LANES]
        if shift:
            out = pltpu.roll(out, LANES - shift, 1)
            if shift + count > LANES:
                more = pltpu.roll(value[:, (tile + 1) * LANES : (tile + 2) * LANES], LANES - shift, 1)
                out = jnp.where(lane < LANES - shift, out, more)
        return jnp.where(lane < count, out, 0.0)

    half = rows_ff // 2
    blocks = []
    for d in range(n):
        low_rows = jnp.where(row == 0, cut(inner, d * half, half), 0.0)
        low_rows = jnp.where(row == 1, table[d : d + 1], low_rows)
        last_rows = jnp.where(row == 0, cut(inner, (n + d) * half, half), 0.0)
        block = [cut(vecs, d * rows_d, rows_d), low_rows, last_rows]
        block += [jnp.zeros((rows_d - 24, LANES), F32)] * (rows_d > 24)
        blocks.append(jnp.concatenate(block, axis=0))
    put_blocks(core, place, blocks, send, keep, columns)


def attend_back_kernel(
    meta, q, k, v, lse, ctx, gctx, bias_rev, nin, frames, gatt, gin, w, vec, *refs, crossed, rows_d, first, count,
):
    last = first + 2 * count == HEADS
    if last and crossed:
        gvec2, gb_inner, bucket_rev, *refs = refs
        earlier = first // (2 * count)
        before = [(refs[2 * i], refs[2 * i + 1]) for i in range(earlier)]
        refs = refs[2 * earlier :]
    send, keep, gin_out, gvec_out, grow_out, base, gbase, delta_t, kt, dqkv, gk, gv, masks = refs
    rows, width = frames.shape
    unit = rows // UNITS
    window = rows - unit
    head = width // HEADS
    core = meta[5]
    place = [meta[6 + 2 * len(crossed) + i] for i in range(2 * len(crossed))]
    prod = gctx[...].astype(F32) * ctx[...].astype(F32)
    sel_row = lax.broadcasted_iota(jnp.int32, (16, width), 0)
    sel_col = lax.broadcasted_iota(jnp.int32, (16, width), 1)
    sel = jnp.where((sel_col >= sel_row * head) & (sel_col < (sel_row + 1) * head), 1.0, 0.0).astype(BF16)
    high = prod.astype(BF16)
    low = (prod - high.astype(F32)).astype(BF16)
    deltas = nt(sel, high) + nt(sel, low)
    for h in range(HEADS):
        delta_t[h] = deltas[h : h + 1]
    ranges = put_masks(meta, masks)
    lane = lax.broadcasted_iota(jnp.int32, (unit, LANES), 1)
    sub_lane = lax.broadcasted_iota(jnp.int32, (LANES, unit), 0)
    span = count * LANES

    def pair(step, carry):
        hp = first // 2 + step
        cols = pl.ds(pl.multiple_of(hp * LANES, LANES), LANES)
        here = pl.multiple_of(step * LANES, LANES)
        kt[...] = jnp.transpose(k[:, cols])
        gk[...] = jnp.zeros_like(gk)
        gv[...] = jnp.zeros_like(gv)
        gbase[...] = jnp.zeros_like(gbase)
        for sub in range(2):
            base[sub] = skewed(bias_rev[pl.ds(2 * hp + sub, 1), :], unit)
        for u in range(UNITS):
            ws = pl.multiple_of(ranges[u], LANES)
            win = pl.ds(ws, window)
            urows = slice(u * unit, (u + 1) * unit)
            mask = jnp.concatenate([masks[u], masks[u]], axis=1)
            kk = k[win, cols]
            vv = v[win, cols]
            qu = q[urows, cols]
            gu = gctx[urows, cols]
            offsets = [
                pl.ds(pl.multiple_of((rows - unit) + u * unit - ws - jb * unit, LANES), unit) for jb in range(UNITS - 1)
            ]
            qs = apart_heads(qu, lane, head)
            gs = apart_heads(gu, lane, head)
            rel = jnp.concatenate([jnp.concatenate([base[sub, :, o] for o in offsets], axis=0) for sub in range(2)], axis=1)
            lses = jnp.concatenate([lse[2 * hp + sub, :, urows] for sub in range(2)], axis=1)
            deltas = jnp.concatenate([delta_t[2 * hp + sub, :, urows] for sub in range(2)], axis=1)
            p = jnp.exp(nt(kk, qs) + rel + mask - lses)
            ds = (p * (nt(vv, gs) - deltas)).astype(BF16)
            gv[win, :] += nn(p.astype(BF16), gs)
            gk[win, :] += nn(ds, qs)
            gq = nn(kt[:, win], ds)
            d32 = ds.astype(F32)
            for sub in range(2):
                for jb, o in enumerate(offsets):
                    gbase[sub, :, o] += d32[jb * unit : (jb + 1) * unit, sub * unit : (sub + 1) * unit]
            gq_t = jnp.where(sub_lane < head, gq[:, :unit], gq[:, unit:])
            dqkv[urows, pl.ds(here, LANES)] = jnp.transpose(gq_t).astype(BF16) * BF16(head**-0.5)
        dqkv[:, pl.ds(span + here, LANES)] = gk[...].astype(BF16)
        dqkv[:, pl.ds(2 * span + here, LANES)] = gv[...].astype(BF16)
        for sub in range(2):
            grow_out[pl.ds(2 * step + sub, 1), :] = unskewed_sum(gbase[sub], unit)
        return carry

    grow_out[...] = jnp.zeros_like(grow_out)
    lax.fori_loop(0, count, pair, 0)
    at_columns = first * head
    grad_in = gin[...] if first else jnp.zeros((rows, width), F32)
    for part in range(3):
        d = dqkv[:, part * span : (part + 1) * span]
        grad_in = grad_in + nt(d, weight(w, slice(part * width + at_columns, part * width + at_columns + span)))
    grads = [(tn(nin[...], dqkv[...]), slice(0, 3 * span))]
    if first == 0:
        grads.append((tn(ctx[...], gatt[...].astype(BF16)), slice(3 * span, 3 * span + width)))
    for g, columns in grads:
        if crossed:
            put_blocks(core, place, row_blocks(g, rows_d), send, keep, columns)
        else:
            keep[:, columns] = g.astype(BF16)
    sums = [jnp.sum(dqkv[:, at : at + span].astype(F32), axis=0, keepdims=True) for at in (0, 2 * span)]
    gvec_out[...] = jnp.zeros_like(gvec_out)
    gvec_out[2:4, 0:span] = jnp.concatenate(sums, axis=0)
    if not last:
        gin_out[...] = grad_in
        return
    n, r = normalise(frames[...].astype(F32))
    gin_out[...] = (gatt[...] + norm_backward(n, r, vec[0:1, :], grad_in)).astype(BF16)
    gvec_out[0:1, :] = jnp.sum(grad_in * n, axis=0, keepdims=True)
    gvec_out[1:2, :] = jnp.sum(grad_in, axis=0, keepdims=True)
    if crossed:
        for i, (vectors, _) in enumerate(before):
            gvec_out[2:4, i * span : (i + 1) * span] = vectors[2:4, 0:span]
        gvec_out[2:4, at_columns : at_columns + span] = jnp.concatenate(sums, axis=0)
        gvec_out[4:8, :] = gvec2[0:4, :]
        grows = jnp.concatenate([grow[0 : 2 * count, :] for _, grow in before] + [grow_out[0 : 2 * count, :]], axis=0)
        small_blocks(
            core, place, gvec_out[...], jnp.broadcast_to(gb_inner[...], (8, gb_inner.shape[1])), grows, bucket_rev,
            send, keep, slice(3 * span, 3 * span + LANES), rows_d, gb_inner.shape[1] // len(place),
        )


def run_kernel(order, kernel, name, scalars, arrays, outs, scratch=(), spare=10, us=100, pin_in=True, pin_out=True):
    spec = pl.BlockSpec(memory_space=pltpu.VMEM)
    smem = pl.BlockSpec(memory_space=pltpu.SMEM)
    arrays = order.after(*arrays)
    arrays = [pltpu.with_memory_space_constraint(a, pltpu.VMEM if pin_in else pltpu.HBM) for a in arrays]
    limit = spare * MIB + sum(math.prod(b.shape) * jnp.dtype(b.dtype).itemsize for b in scratch)
    out = pl.pallas_call(
        kernel,
        in_specs=[smem] * len(scalars) + [spec] * len(arrays),
        out_specs=[spec] * len(outs),
        out_shape=[(pltpu.VMEM if pin_out else jax.ShapeDtypeStruct)(s, d) for s, d in outs],
        scratch_shapes=list(scratch),
        compiler_params=pltpu.CompilerParams(vmem_limit_bytes=limit),
        cost_estimate=pl.CostEstimate(flops=us * 1_000_000_000, bytes_accessed=us * 1_000_000, transcendentals=0),
        name=name,
    )(*scalars, *arrays)
    order.did(out[0])
    return out


def on_device(
    frames, ln1_gain, ln1_shift, w_query, b_query, w_key, w_value, b_value, w_out, b_out, ln2_gain, ln2_shift,
    w_inner, b_inner, w_outer, b_outer, bias_table, layout, valid, rel_index, cotangent, *, n,
):
    rows, width = frames.shape
    rows_d = w_query.shape[0]
    rows_ff = w_outer.shape[0]
    ff = w_inner.shape[1]
    span = rel_index.shape[0] + 1
    unit = rows // UNITS
    per_table = bias_table.shape[0]
    plan = plan_tables(n)
    core, chips, place = plan
    order = Order()
    direct = (
        rows_d % 8 == 0 and rows_d >= 24 and rows_ff == 4 * rows_d and max(rows_d, rows_ff, per_table) <= LANES and per_table % HEADS == 0
    )
    crossed = tuple(crossed_places(n)) if direct else ()
    crossed_outer = tuple(crossed_places(n, "outer")) if direct else ()
    unit_half = rows_ff // 2
    apart = [(d * rows_ff + h * unit_half, h * ff // 2 + d * unit_half, unit_half) for h in range(2) for d in range(n)]
    together = [(b, a, c) for a, b, c in apart]
    meta = [layout, valid.reshape(-1), core[None]]
    if direct:
        _, chips_outer, place_outer = plan_tables(n, "outer")
        meta += [chips, chips_outer, place, place_outer]
    meta = jnp.concatenate(meta).astype(jnp.int32)
    small_d = jnp.stack([ln1_gain, ln1_shift, b_query, b_value, b_out, ln2_gain, ln2_shift, b_outer])

    base = pltpu.VMEM((2, unit, span), F32)
    masks = pltpu.VMEM((UNITS, rows - unit, unit), F32)
    if direct:
        vectors = (ln1_gain, ln1_shift, b_query, b_value, b_out, ln2_gain, ln2_shift, b_outer, b_inner, bias_table)
        (part1,) = run_kernel(
            Order(), functools.partial(pack_first_kernel, rows_ff=rows_ff), "pack_first", [],
            [w_query, w_key, w_value, *(v[None] for v in vectors)], [((1, rows_d, 3 * width + LANES), BF16)],
            [pltpu.VMEM((rows_d, LANES), F32)], spare=4, pin_in=False,
        )
        g1 = Gather(part1, n, order)
        part2, part3 = run_kernel(
            order, functools.partial(pack_feed_kernel, moves=apart), "pack_feed", [], [w_inner, w_outer, w_out],
            [((1, rows_d, ff + width), BF16), ((1, rows_d, ff), BF16)], spare=4, pin_in=False,
        )
        g3 = Gather(part3, n, order, "outer")
        (part2,) = lax.optimization_barrier((part2, g1.got))[:1]
        g2 = Gather(part2, n, order)
        (g2.got,) = lax.optimization_barrier((g2.got, g3.got))[:1]
        for g in (g1, g1, g2, g1, g2, g3, g2, g3):
            g.step()
        first = g1.finish()
        each = per_table // HEADS
        index = jnp.stack([rel_index // each, rel_index % each])
        bucket_rev = jnp.pad(index[:, ::-1], ((0, 6), (0, 1)), constant_values=-1)
        q, k, v, nin, w1, vec, inner_bias, bias_rev = run_kernel(
            order, functools.partial(project_kernel, crossed=crossed, rows_d=rows_d, rows_ff=rows_ff), "project", [meta],
            [frames, *first, bucket_rev],
            [((rows, width), BF16)] * 4
            + [((n // 2, 2 * rows_d, 3 * width), BF16), ((8, width), F32), ((1, ff), F32), ((16, span), F32)],
            [
                pltpu.VMEM((width // LANES + 1, 8, LANES), F32),
                pltpu.VMEM((ff // LANES + 1, 8, LANES), F32),
                pltpu.VMEM((n, LANES), F32),
            ],
            us=1,
        )
        chunk = [[((n // 2, rows_d, c), BF16)] * 2 for c in (ff, ff)]
        w_out_whole = [((n // 2, 2 * rows_d, width), BF16)]
        unpacked = [pltpu.VMEM((n // 2, 2 * rows_d, width), BF16), pltpu.VMEM((n // 2, rows_ff, width), BF16)]
    else:
        flat = jnp.concatenate([small_d.reshape(-1), b_inner, bias_table])
        per = flat.shape[0] // rows_d
        small = jnp.pad(flat.reshape(rows_d, per), ((0, 0), (0, LANES - per)))
        w1 = gathered(Gather(jnp.concatenate([w_query, w_key, w_value, small], axis=1), n, order).finish(), plan, n)
        w2 = (gathered(Gather(jnp.concatenate([w_inner, w_out], axis=1), n, order).finish(), plan, n),)
        w2 += (gathered(Gather(w_outer, n, order).finish(), plan, n),)
        flats = w1[:, 3 * width : 3 * width + per].reshape(n, rows_d * per)
        vec = flats[:, : 8 * rows_d].reshape(n, 8, rows_d).transpose(1, 0, 2).reshape(8, width).astype(F32)
        inner_bias = flats[:, 8 * rows_d : 8 * rows_d + rows_ff].reshape(1, ff).astype(F32)
        table = jnp.pad(flats[:, 8 * rows_d + rows_ff :].reshape(-1, HEADS), ((0, 0), (0, 16 - HEADS)))
        index_rev = jnp.pad(rel_index[::-1], (0, 1), constant_values=-1)
        ids = jnp.arange(table.shape[0], dtype=jnp.int32)[:, None]
        bias_rev = tn(table, (ids == index_rev[None]).astype(BF16))
        q, k, v, nin = run_kernel(
            order, project_body, "project", [meta], [frames, w1, vec], [((rows, width), BF16)] * 4
        )
        chunk = [[((8, LANES), BF16), ((c, max(width, ff // 2), max(width, ff // 2)), BF16)] for c in (2, 2)]
        w_out_whole = []
        unpacked = []

    ctx, lse = run_kernel(
        order, attend_kernel, "attend", [meta], [q, k, v, bias_rev],
        [((rows, width), BF16), ((HEADS, 1, rows), F32)], [base, pltpu.VMEM((LANES, rows), BF16), masks], spare=4, us=1,
    )

    def start(send, keep, scatter):
        return scatter.add(*((send, keep) if direct else split_natural(keep, plan, n)))

    if direct:
        g3.step()
        w2 = g2.finish()
    att, nmid, acc, gmid, gb1, send1, keep1, *w_out_all = run_kernel(
        order, functools.partial(feed_first_kernel, crossed=crossed, rows_d=rows_d), "feed_first", [meta],
        [frames, ctx, vec, inner_bias, cotangent, *w2],
        [((rows, width), F32), ((rows, width), BF16), ((rows, width), F32), ((rows, width), F32), ((1, ff // 2), F32)]
        + chunk[0] + w_out_whole,
        unpacked, spare=12,
    )
    if direct:
        w3 = g3.finish()
        begin = functools.partial(Scatter, n, order)
        sum_1 = begin("outer").add(send1, keep1)
    else:
        w3 = w2
    mixed, gatt, gctx, send2, keep2, gb2, gvec2 = run_kernel(
        order, functools.partial(feed_second_kernel, crossed=crossed_outer, rows_d=rows_d), "feed_second", [meta],
        [att, nmid, acc, gmid, ctx, vec, inner_bias, cotangent, *w_out_all, *w3],
        [((rows, width), BF16), ((rows, width), F32), ((rows, width), BF16)] + chunk[1]
        + [((1, ff // 2), F32), ((8, width), F32)],
        [pltpu.VMEM((rows, width), F32)] * 2 + unpacked, spare=12,
    )
    gb_inner = jnp.concatenate([gb1, gb2], axis=1)
    if direct:
        sum_1.step()
        sum_2 = begin().add(send2, keep2)
    else:
        whole_inner = jnp.concatenate([keep1[0, :width, : ff // 2], keep2[0, :width, : ff // 2]], axis=1)
        whole_outer = jnp.concatenate([keep1[1, : ff // 2, :width], keep2[1, : ff // 2, :width]], axis=0)
        begin = functools.partial(Scatter, n, order)
        sum_1 = begin().add(*split_natural(whole_outer, plan, n))
        sum_2 = begin().add(*split_natural(whole_inner, plan, n))

    count = 2
    cols = count * LANES
    passed = gatt
    done, earlier = [], []
    sum_early, sum_late = begin(), begin()
    calls = HEADS // (2 * count)
    for call in range(calls):
        last = call == calls - 1
        wide = 3 * cols + LANES * (last and direct) + width * (call == 0)
        part = [((n // 2, rows_d, wide), BF16)] * 2 if direct else [((8, LANES), BF16), ((width, wide), BF16)]
        extra = [gvec2, gb_inner, bucket_rev] + [a for pair in earlier for a in pair] if last and direct else []
        send, keep, passed, gvec1, grow = run_kernel(
            order,
            functools.partial(
                attend_back_kernel, crossed=crossed, rows_d=rows_d, first=call * 2 * count, count=count
            ),
            "attend_back", [meta],
            [q, k, v, lse, ctx, gctx, bias_rev, nin, frames, gatt, passed, w1, vec] + extra,
            part + [((rows, width), BF16 if last else F32), ((8, width), F32), ((8, span), F32)],
            [
                base, base,
                pltpu.VMEM((HEADS, 1, rows), F32),
                pltpu.VMEM((LANES, rows), BF16),
                pltpu.VMEM((rows, 3 * cols), BF16),
                pltpu.VMEM((rows, LANES), F32),
                pltpu.VMEM((rows, LANES), F32),
                masks,
            ],
            spare=10,
        )
        earlier.append((gvec1, grow))
        start(send, keep, sum_late if call else sum_early)
        if call == 0:
            sum_2.step()
        if call == 1:
            sum_1.step()
            sum_early.step()
    for each_sum in (sum_2, sum_late, sum_early, sum_1, sum_2, sum_late, sum_early, sum_1, sum_2, sum_late, sum_early, sum_late):
        if each_sum.steps:
            each_sum.step()
    if direct:
        pass
    sum_1, sum_2, early, late = sum_1.finish(), sum_2.finish(), sum_early.finish(), sum_late.finish()
    if direct:
        both = jnp.concatenate([sum_1[:, : ff // 2], sum_2[:, : ff // 2]], axis=1)
        (grad_inner,) = run_kernel(
            Order(), functools.partial(move_kernel, moves=together), "together", [], [both], [((rows_d, ff), F32)]
        )
        folded = (sum_1[:, ff // 2 :], sum_2[:, ff // 2 : ff])
        grad_outer = jnp.concatenate([f[:, i * width : (i + 1) * width] for f in folded for i in range(2)], axis=0)
    else:
        grad_inner, grad_outer = sum_2[:, :ff], sum_1
    pieces = [early[:, : 3 * cols]] + [late[:, i * 3 * cols : (i + 1) * 3 * cols] for i in range(calls - 1)]
    if direct:
        sum_q, sum_k, sum_v = run_kernel(
            Order(), functools.partial(columns_kernel, count=cols), "columns", [], [early[:, : 3 * cols], late],
            [((rows_d, width), F32)] * 3, spare=4, pin_out=False,
        )
        small = late[:, 3 * cols * (calls - 1) :]
        vecs = small[:8, :rows_d]
        sum_b_inner = jnp.concatenate([small[8, :unit_half], small[16, :unit_half]])
        sum_table = small[9, :per_table]
    else:
        sum_q, sum_k, sum_v = (jnp.concatenate([p[:, i * cols : (i + 1) * cols] for p in pieces], axis=1) for i in range(3))
        hot_rev = (ids == index_rev[None]).astype(F32)
        grow = jnp.concatenate([g[: 2 * count] for _, g in earlier])
        gtable = lax.dot_general(
            hot_rev, grow, (((1,), (1,)), ((), ())), precision=lax.Precision.HIGHEST, preferred_element_type=F32
        )
        gbias = jnp.concatenate([g[2:4, :cols] for g, _ in earlier], axis=1)
        gsmall = jnp.concatenate([gvec1[0:2], gbias, gvec2[0:4]])
        gsmall = gsmall.reshape(8, n, rows_d).transpose(1, 0, 2).reshape(n, 8 * rows_d)
        gflat = jnp.concatenate([gsmall, gb_inner.reshape(n, rows_ff), gtable.reshape(n, -1)], axis=1)
        gflat = jnp.pad(gflat, ((0, 0), (0, -gflat.shape[1] % LANES))).astype(BF16)
        sum_flat = Scatter(n, order).add(*split_natural(gflat, plan, n)).finish()[0]
        vecs = sum_flat[: 8 * rows_d].reshape(8, rows_d)
        sum_b_inner = sum_flat[8 * rows_d : 8 * rows_d + rows_ff]
        sum_table = sum_flat[8 * rows_d + rows_ff : 8 * rows_d + rows_ff + per_table]
    return (
        mixed, passed, vecs[0], vecs[1], sum_q, vecs[2], sum_k, sum_v, vecs[3],
        early[:, 3 * cols :], vecs[4], vecs[5], vecs[6], grad_inner, sum_b_inner, grad_outer, vecs[7], sum_table,
    )


def solution(mesh):
    row, two = P("dp"), P("dp", None)
    in_specs = (two, row, row, two, row, two, two, row, two, row, row, row, two, row, two, row, row, row, two, P(), two)
    out_specs = (two, two, row, row, two, row, two, two, row, two, row, row, row, two, row, two, row, row)
    return jax.shard_map(
        functools.partial(on_device, n=mesh.shape["dp"]),
        mesh=mesh, in_specs=in_specs, out_specs=out_specs, check_vma=False,
    )
```

```python
import functools
import math

import jax
import jax.numpy as jnp
import numpy as np
from jax import lax
from jax.experimental import pallas as pl
from jax.experimental.pallas import tpu as pltpu
from jax.sharding import PartitionSpec as P

HEADS = 12
LANES = 128
UNITS = 4
MASKED = -1e30
F32 = jnp.float32
BF16 = jnp.bfloat16
SEGMENT = ((0, 0, 0, 1), (0, 0, 1, 1), (0, 0, 1, 2), (0, 1, 2, 3))
START = ((0, 0, 0, 3), (0, 0, 2, 2), (0, 0, 2, 3), (0, 1, 2, 3))
MIB = 1024 * 1024
COUNTS = (3, 3)


def bit_orders(n, kind):
    chip = [1 << k for k in range(1, n.bit_length() - 1)]
    low, high = chip[:2], chip[2:][::-1]
    if kind == "outer":
        return (low[:1] + high + low[1:], low[1:] + high + low[:1])
    return (high + low, high + low[::-1])


def gather_masks(bits):
    masks = [0]
    for bit in bits:
        masks = masks + [bit ^ m for m in masks]
    return masks


def scatter_masks(bits):
    masks = [0]
    for bit in bits:
        masks = [bit ^ m for m in masks] + masks
    return masks


def pairs(n, by_core):
    return [(i, i ^ by_core[i & 1]) for i in range(n)]


class Order:
    def __init__(self):
        self.last = None

    def after(self, *arrays):
        if self.last is None:
            return arrays
        return lax.optimization_barrier((*arrays, self.last))[:-1]

    def did(self, array):
        self.last = array


class Gather:
    def __init__(self, part, n, order, kind="inner"):
        self.n = n
        self.order = order
        self.steps = list(zip(*bit_orders(n, kind)))
        self.held = part if part.ndim == 3 else part[None]
        self.got = lax.ppermute(self.held, "dp", pairs(n, self.steps.pop(0)))

    def step(self):
        pair = self.order.after(self.held, self.got)
        self.held = jnp.concatenate(pair, axis=0)
        self.order.did(self.held)
        self.got = lax.ppermute(self.held, "dp", pairs(self.n, self.steps.pop(0)))
        return self

    def finish(self):
        while self.steps:
            self.step()
        (self.got,) = self.order.after(self.got)
        swap = pairs(self.n, (1, 1))
        return (self.held, self.got, lax.ppermute(self.held, "dp", swap), lax.ppermute(self.got, "dp", swap))


class Scatter:
    def __init__(self, n, order, kind="inner"):
        self.n = n
        self.order = order
        self.parts = []
        self.terms = []
        self.at = 0
        self.steps = list(reversed(list(zip(*bit_orders(n, kind)))))
        self.half = n // 4

    def add(self, send, keep):
        self.parts.append((keep, lax.ppermute(send, "dp", pairs(self.n, (1, 1)))))
        return self

    def total(self, count, dtype):
        at = self.at
        held = [(t, first) for t, first in self.terms if first <= at and at + count <= first + t.shape[0]]
        flat = [t for part in self.parts for t in part] + [t for t, _ in held]
        flat = list(self.order.after(*flat))
        cut = [lax.slice_in_dim(t, at, at + count).astype(F32) for t in flat[: 2 * len(self.parts)]]
        out = [cut[2 * i] + cut[2 * i + 1] for i in range(len(self.parts))]
        out = out[0] if len(out) == 1 else jnp.concatenate(out, axis=-1)
        for t, (_, first) in zip(flat[2 * len(self.parts) :], held):
            out = out + lax.slice_in_dim(t, at - first, at - first + count).astype(F32)
        out = out.astype(dtype)
        self.order.did(out)
        return out

    def step(self, transfers=1):
        by_core = self.steps.pop(0)
        count = self.half // transfers
        for _ in range(transfers):
            out = self.total(count, BF16)
            self.terms.append((lax.ppermute(out, "dp", pairs(self.n, by_core)), self.at + self.half))
            self.at += count
        self.half //= 2

    def finish(self):
        while self.steps:
            self.step()
        return self.total(1, F32)[0]


def plan_tables(n, kind="inner"):
    orders = bit_orders(n, kind)
    me = lax.axis_index("dp")
    core = me & 1
    g = np.array([gather_masks(o) for o in orders], np.int32)
    s = np.array([scatter_masks(o) for o in orders], np.int32)
    inverse = np.zeros((2, n), np.int32)
    for c in (0, 1):
        for i, m in enumerate(s[c]):
            inverse[c, m] = i
    devices = jnp.arange(n, dtype=jnp.int32)
    chips = (me ^ jnp.where(core == 0, jnp.asarray(g[0]), jnp.asarray(g[1]))) >> 1
    mask = (devices ^ me) & ~1
    place = jnp.sum(jnp.where(mask[:, None] == devices[None, :], jnp.asarray(inverse)[np.arange(n) % 2], 0), axis=1)
    return core, chips, place


def crossed_places(n, kind="inner"):
    first, second = (gather_masks(o) for o in bit_orders(n, kind))
    places = [second.index(m) for m in first]
    assert places == [first.index(m) for m in second]
    return places


def gathered(parts, plan, n):
    core, chips, _ = plan
    mine = jnp.concatenate(parts[:2])
    theirs = jnp.concatenate(parts[2:])[np.array(crossed_places(n))]
    both = jnp.where(core == 0, jnp.stack([mine, theirs], 1), jnp.stack([theirs, mine], 1))
    return both[jnp.argsort(chips)].reshape(n * mine.shape[1], mine.shape[2])


def split_natural(grad, plan, n):
    core, _, place = plan
    rows = grad.shape[0] // n
    blocks = grad.reshape(n // 2, 2, rows, grad.shape[1])
    mine = jnp.where(core == 0, blocks[:, 0], blocks[:, 1])
    theirs = jnp.where(core == 0, blocks[:, 1], blocks[:, 0])
    both = place.reshape(n // 2, 2)
    my_place = jnp.where(core == 0, both[:, 0], both[:, 1])
    their_place = jnp.where(core == 0, both[:, 1], both[:, 0])
    return theirs[jnp.argsort(their_place)], mine[jnp.argsort(my_place)]


def nn(a, b):
    return jnp.dot(a, b, preferred_element_type=F32)


def nt(a, b):
    return lax.dot_general(a, b, (((1,), (1,)), ((), ())), preferred_element_type=F32)


def tn(a, b):
    return lax.dot_general(a, b, (((0,), (0,)), ((), ())), preferred_element_type=F32)


def normalise(v):
    centred = v - jnp.mean(v, axis=-1, keepdims=True)
    r = lax.rsqrt(jnp.mean(centred * centred, axis=-1, keepdims=True) + 1e-05)
    return centred * r, r


def norm_backward(n, r, gain, e):
    eg = e * gain
    return r * (eg - jnp.mean(eg, axis=-1, keepdims=True) - n * jnp.mean(eg * n, axis=-1, keepdims=True))


def pick(table, code, u):
    out = jnp.int32(table[0][u])
    for c in range(1, 4):
        out = jnp.where(code == c, jnp.int32(table[c][u]), out)
    return out


def unit_range(meta, u, unit):
    code = meta[0]
    segment = pick(SEGMENT, code, u)
    start = pick(START, code, u)
    count = meta[1]
    for s in range(1, 4):
        count = jnp.where(segment == s, meta[1 + s], count)
    window = jnp.minimum(start, 1) * unit
    return start * unit, start * unit + count, window


def put_masks(meta, masks):
    units, window, unit = masks.shape
    row_at = lax.broadcasted_iota(jnp.int32, (window, unit), 0)
    starts = []
    for u in range(units):
        first, end, start = unit_range(meta, u, unit)
        masks[u] = jnp.where((row_at + start >= first) & (row_at + start < end), 0.0, MASKED)
        starts.append(start)
    return starts


def skewed(row, unit):
    wide = jnp.broadcast_to(row, (unit, row.shape[1]))
    return pltpu.roll(wide, row.shape[1] - (unit - 1), 1, stride=1, stride_axis=0)


def unskewed_sum(block, unit):
    width = block.shape[1]
    total = None
    for a in range(unit // 8):
        part = block[8 * a : 8 * a + 8]
        shift = (unit - 1 - 8 * a) % width
        part = pltpu.roll(part, shift, 1) if shift else part
        total = part if total is None else total + part
    out = total[0:1]
    for s in range(1, 8):
        out = out + pltpu.roll(total[s : s + 1], width - s, 1)
    return out


def unpack(core, chips, parts, crossed, out, columns):
    half = parts[0].shape[0]
    for i, j in enumerate(crossed):
        mine = parts[i // half][i % half, :, columns]
        theirs = parts[2 + j // half][j % half, :, columns]
        first = jnp.where(core == 0, mine, theirs)
        second = jnp.where(core == 0, theirs, mine)
        out[chips[i]] = jnp.concatenate([first, second], axis=0)


def weight(ref, columns):
    value = ref[..., columns]
    return value.reshape(-1, value.shape[-1])


def put_blocks(core, places, blocks, send, keep, columns):
    for plane in range(2):

        @pl.when(core == plane)
        def _(plane=plane):
            for at, (place, block) in enumerate(zip(places, blocks)):
                (keep if at % 2 == plane else send)[place, :, columns] = block.astype(BF16)


def row_blocks(value, rows):
    return [value[at : at + rows] for at in range(0, value.shape[0], rows)]


def project_body(meta, frames, w, vec, q_out, k_out, v_out, nin_out):
    width = frames.shape[1]
    head = width // HEADS
    n, _ = normalise(frames[...].astype(F32))
    nin = (n * vec[0:1, :] + vec[1:2, :]).astype(BF16)
    nin_out[...] = nin
    q_out[...] = ((nn(nin, weight(w, slice(0, width))) + vec[2:3, :]) * (head**-0.5)).astype(BF16)
    k_out[...] = nn(nin, weight(w, slice(width, 2 * width))).astype(BF16)
    v_out[...] = (nn(nin, weight(w, slice(2 * width, 3 * width))) + vec[3:4, :]).astype(BF16)


def apart_heads(rows, lane, head):
    zero = jnp.zeros_like(rows)
    return jnp.concatenate([jnp.where(lane < head, rows, zero), jnp.where(lane < head, zero, rows)], axis=0)


def attend_kernel(meta, q, k, v, bias_rev, ctx_out, lse_out, base, vt, masks):
    rows, width = q.shape
    unit = rows // UNITS
    window = rows - unit
    head = width // HEADS
    ranges = put_masks(meta, masks)
    lane = lax.broadcasted_iota(jnp.int32, (unit, LANES), 1)
    sub_lane = lax.broadcasted_iota(jnp.int32, (LANES, unit), 0)

    def pair(hp, carry):
        cols = pl.ds(pl.multiple_of(hp * LANES, LANES), LANES)
        vt[...] = jnp.transpose(v[:, cols])
        for sub in range(2):
            base[sub] = skewed(bias_rev[pl.ds(2 * hp + sub, 1), :], unit)
        for u in range(UNITS):
            ws = pl.multiple_of(ranges[u], LANES)
            win = pl.ds(ws, window)
            urows = slice(u * unit, (u + 1) * unit)
            kk = k[win, cols]
            qu = q[urows, cols]
            offsets = [
                pl.ds(pl.multiple_of((rows - unit) + u * unit - ws - jb * unit, LANES), unit) for jb in range(UNITS - 1)
            ]
            parts = []
            for sub in range(2):
                qs = jnp.where((lane >= head) == bool(sub), qu, jnp.zeros_like(qu))
                rel = jnp.concatenate([base[sub, :, o] for o in offsets], axis=0)
                s = nt(kk, qs) + rel + masks[u]
                top = jnp.max(s, axis=0, keepdims=True)
                e = jnp.exp(s - top)
                tot = jnp.sum(e, axis=0, keepdims=True)
                parts.append(nn(vt[:, win], e.astype(BF16)) * (1.0 / tot))
                lse_out[2 * hp + sub, :, urows] = top + jnp.log(tot)
            ctx_out[urows, cols] = jnp.transpose(jnp.where(sub_lane < head, parts[0], parts[1])).astype(BF16)
        return carry

    lax.fori_loop(0, HEADS // 2, pair, 0)


def small_vectors(core, chips, parts, crossed, at, rows_d, rows_ff, vec3, inner3, table):
    half = parts[0].shape[0]
    lane = lax.broadcasted_iota(jnp.int32, (8, LANES), 1)
    vec3[...] = jnp.zeros_like(vec3)
    inner3[...] = jnp.zeros_like(inner3)
    for i, j in enumerate(crossed):
        mine = parts[i // half][i % half, :, at : at + LANES].astype(F32)
        theirs = parts[2 + j // half][j % half, :, at : at + LANES].astype(F32)
        for plane in range(2):
            block = jnp.where(core == plane, mine, theirs)
            d = 2 * chips[i] + plane
            unit_half = rows_ff // 2
            half_at = 2 * half * rows_ff
            for first, rows, part, out in (
                (0, rows_d, block[0:8], vec3),
                (0, unit_half, block[8:16], inner3),
                (half_at, unit_half, block[16:24], inner3),
            ):
                start = first + d * rows
                tile = start >> 7
                shift = start & (LANES - 1)
                rolled = pltpu.roll(part, shift, 1)
                out[tile] += jnp.where(lane >= shift, rolled, 0.0)
                out[tile + 1] += jnp.where(lane < shift, rolled, 0.0)
            table[pl.ds(d, 1), :] = block[9:10]


def relative_rows(bucket, table, out):
    devices = lax.broadcasted_iota(jnp.int32, (table.shape[0], bucket.shape[1]), 0)
    hot = jnp.where(devices == bucket[0:1, :], 1.0, 0.0).astype(BF16)
    rows = tn(table[...].astype(BF16), hot)
    total = jnp.zeros((HEADS, bucket.shape[1]), F32)
    for m in range(LANES // HEADS):
        total = total + jnp.where(bucket[1:2, :] == m, rows[m * HEADS : (m + 1) * HEADS], 0.0)
    out[0:HEADS, :] = total
    out[HEADS:, :] = jnp.zeros_like(out[HEADS:, :])


def project_kernel(
    meta, frames, p0, p1, p2, p3, bucket_rev,
    q_out, k_out, v_out, nin_out, w, vec, b_inner, bias_rev,
    vec3, inner3, table, *, crossed, rows_d, rows_ff,
):
    width = frames.shape[1]
    core = meta[5]
    chips = [meta[6 + i] for i in range(len(crossed))]
    parts = (p0, p1, p2, p3)
    small_vectors(core, chips, parts, crossed, 3 * width, rows_d, rows_ff, vec3, inner3, table)
    for a in range(width // LANES):
        vec[:, a * LANES : (a + 1) * LANES] = vec3[a]
    for a in range(b_inner.shape[1] // LANES):
        b_inner[:, a * LANES : (a + 1) * LANES] = inner3[a, 0:1]
    relative_rows(bucket_rev, table, bias_rev)
    unpack(core, chips, parts, crossed, w, slice(0, 3 * width))
    project_body(meta, frames, w, vec, q_out, k_out, v_out, nin_out)


def unpack_folded(core, chips, parts, crossed, out, at, width):
    half = parts[0].shape[0]
    for i, j in enumerate(crossed):
        mine = parts[i // half][i % half, :, at : at + 2 * width]
        theirs = parts[2 + j // half][j % half, :, at : at + 2 * width]
        first = jnp.where(core == 0, mine, theirs)
        second = jnp.where(core == 0, theirs, mine)
        rows = [first[:, :width], first[:, width:], second[:, :width], second[:, width:]]
        out[chips[i]] = jnp.concatenate(rows, axis=0)


def feed_tiles(meta, kind, crossed, parts, natural, b_inner, cot, first, nmid, acc, gmid, gb_out, send, keep, w_tile, w_rows, rows_d):
    width = nmid.shape[1]
    tiles = b_inner.shape[1] // width // 2
    if crossed:
        half = len(crossed)
        core = meta[5]
        chips_at = 6 + half * (kind == "outer")
        chips = [meta[chips_at + i] for i in range(half)]
        place_at = 6 + 2 * half + 2 * half * (first == 0)
        place = [meta[place_at + i] for i in range(2 * half)]
        unpack_folded(core, chips, parts, crossed, w_rows, tiles * width, width)
        w_outer = w_rows.reshape(tiles * width, width)
    else:
        w, w_outer = natural

    def tile(t, carry):
        here = pl.multiple_of(t * width, LANES)
        cols = pl.ds(here, width)
        all_cols = pl.ds(pl.multiple_of(first + here, LANES), width)
        if crossed:
            unpack(core, chips, parts, crossed, w_tile, cols)
            wi = weight(w_tile, slice(None))
            wo = w_outer[cols, :]
        else:
            wi = w[:, all_cols]
            wo = w_outer[all_cols, :]
        v = nn(nmid[...], wi) + b_inner[:, all_cols]
        phi = 0.5 * (1.0 + lax.erf(v * (0.5**0.5)))
        act = (v * phi).astype(BF16)
        slope = phi + v * jnp.exp(-0.5 * v * v) * 0.3989422804014327
        acc[...] += nn(act, wo)
        gi = (slope * nt(cot[...], wo)).astype(BF16)
        gb_out[:, cols] = jnp.sum(gi.astype(F32), axis=0, keepdims=True)
        gmid[...] += nt(gi, wi)
        g_outer = tn(act, cot[...])
        g_inner = tn(nmid[...], gi)
        if crossed:
            put_blocks(core, place, row_blocks(g_inner, rows_d), send, keep, cols)
            per = width // (2 * rows_d)
            places = [meta[place_at + t * per + at] for at in range(per)]
            rows = row_blocks(g_outer, rows_d)
            blocks = [jnp.concatenate(rows[2 * at : 2 * at + 2], axis=1) for at in range(per)]
            put_blocks(core, places, blocks, send, keep, slice(tiles * width, (tiles + 2) * width))
        else:
            keep[0, :width, cols] = g_inner.astype(BF16)
            keep[1, cols, :width] = g_outer.astype(BF16)
        return carry

    lax.fori_loop(0, tiles, tile, 0)


def feed_first_kernel(meta, frames, ctx, vec, b_inner, cot, *refs, crossed, rows_d):
    rows, width = frames.shape
    ff = b_inner.shape[1]
    if crossed:
        parts, refs = refs[:4], refs[4:]
        att, nmid, acc, gmid, gb_out, send, keep, w_out, w_tile, w_rows = refs
        chips = [meta[6 + i] for i in range(len(crossed))]
        unpack(meta[5], chips, parts, crossed, w_out, slice(ff, ff + width))
        wo, natural = weight(w_out, slice(None)), None
    else:
        w, w_outer, att, nmid, acc, gmid, gb_out, send, keep = refs
        parts, natural, w_tile, w_rows = None, (w, w_outer), None, None
        wo = w[:, ff : ff + width]
    attended = frames[...].astype(F32) + nn(ctx[...], wo) + vec[4:5, :]
    att[...] = attended
    n, _ = normalise(attended)
    nmid[...] = (n * vec[5:6, :] + vec[6:7, :]).astype(BF16)
    acc[...] = attended + vec[7:8, :]
    gmid[...] = jnp.zeros_like(gmid)
    feed_tiles(
        meta, "inner", crossed, parts, natural, b_inner, cot, 0, nmid, acc, gmid, gb_out, send, keep, w_tile, w_rows, rows_d
    )


def feed_second_kernel(meta, att, nmid, acc_in, gmid_in, ctx, vec, b_inner, cot, *refs, crossed, rows_d):
    rows, width = att.shape
    ff = b_inner.shape[1]
    if crossed:
        w_out, parts, refs = refs[0], refs[1:5], refs[5:]
        mixed_out, gatt_out, gctx_out, send, keep, gb_out, gvec_out, acc, gmid, w_tile, w_rows = refs
        wo, natural = weight(w_out, slice(None)), None
    else:
        w, w_outer, mixed_out, gatt_out, gctx_out, send, keep, gb_out, gvec_out, acc, gmid = refs
        parts, natural, w_tile, w_rows = None, (w, w_outer), None, None
        wo = w[:, ff : ff + width]
    acc[...] = acc_in[...]
    gmid[...] = gmid_in[...]
    feed_tiles(
        meta, "outer", crossed, parts, natural, b_inner, cot, ff // 2, nmid, acc, gmid, gb_out, send, keep, w_tile, w_rows, rows_d
    )
    mixed_out[...] = acc[...].astype(BF16)
    n, r = normalise(att[...])
    e = gmid[...]
    c32 = cot[...].astype(F32)
    gatt = c32 + norm_backward(n, r, vec[5:6, :], e)
    gatt_out[...] = gatt
    gbr = gatt.astype(BF16)
    gctx_out[...] = nt(gbr, wo).astype(BF16)
    gvec_out[0:1, :] = jnp.sum(gbr.astype(F32), axis=0, keepdims=True)
    gvec_out[1:2, :] = jnp.sum(e * n, axis=0, keepdims=True)
    gvec_out[2:3, :] = jnp.sum(e, axis=0, keepdims=True)
    gvec_out[3:4, :] = jnp.sum(c32, axis=0, keepdims=True)
    gvec_out[4:8, :] = jnp.zeros_like(gvec_out[4:8, :])


def moved_lanes(value, moves):
    lane = lax.broadcasted_iota(jnp.int32, (value.shape[0], LANES), 1)
    out = [None] * (value.shape[1] // LANES)
    for source, target, count in moves:
        while count:
            step = min(count, LANES - source % LANES, LANES - target % LANES)
            piece = value[:, source - source % LANES : source - source % LANES + LANES]
            shift = (target - source) % LANES
            piece = pltpu.roll(piece, shift, 1) if shift else piece
            at = target % LANES
            old = out[target // LANES]
            inside = (lane >= at) & (lane < at + step)
            out[target // LANES] = piece if old is None else jnp.where(inside, piece, old)
            source, target, count = source + step, target + step, count - step
    return jnp.concatenate(out, axis=1)


def pack_first_kernel(*refs, rows_ff):
    w_query, w_key, w_value, *vectors, b_inner, table, out, small = refs
    rows, width = w_query.shape
    for i, part in enumerate((w_query, w_key, w_value)):
        out[0, :, i * width : (i + 1) * width] = part[...]
    half = rows_ff // 2
    small[...] = jnp.zeros_like(small)
    for i, vector in enumerate(vectors):
        small[i : i + 1, 0:rows] = vector[...].astype(F32)
    small[8:9, 0:half] = b_inner[:, 0:half].astype(F32)
    small[9:10, 0 : table.shape[1]] = table[...].astype(F32)
    small[16:17, 0:half] = b_inner[:, half:].astype(F32)
    out[0, :, 3 * width :] = small[...].astype(BF16)


def pack_feed_kernel(w_inner, w_outer, w_out, second, third, *, moves):
    rows, width = w_out.shape
    half = w_inner.shape[1] // 2
    inner = moved_lanes(w_inner[...].astype(F32), moves).astype(BF16)
    for part, out in enumerate((second, third)):
        out[0, :, 0:half] = inner[:, part * half : (part + 1) * half]
        for i in range(2):
            at = (2 * part + i) * rows
            out[0, :, half + i * width : half + (i + 1) * width] = w_outer[at : at + rows, :]
    second[0, :, 2 * half :] = w_out[...]


def columns_kernel(early, late, q_out, k_out, v_out, *, counts):
    at = first = 0
    for call, count in enumerate(counts):
        cols = count * LANES
        for i, out in enumerate((q_out, k_out, v_out)):
            out[:, at : at + cols] = (late if call else early)[:, first + i * cols : first + (i + 1) * cols]
        at += cols
        first = first + 3 * cols if call else 0


def move_kernel(value, out, *, moves):
    out[...] = moved_lanes(value[...].astype(F32), moves).astype(out.dtype)


def small_blocks(core, place, vecs, inner, grows, bucket_rev, send, keep, columns, rows_d, rows_ff):
    n = len(place)
    span = bucket_rev.shape[1]
    row = lax.broadcasted_iota(jnp.int32, (8, LANES), 0)
    lane = lax.broadcasted_iota(jnp.int32, (8, LANES), 1)
    each = LANES // HEADS
    big = [jnp.where(bucket_rev[1:2, :] == m, grows, 0.0) for m in range(each)]
    big = jnp.concatenate(big + [jnp.zeros((LANES - each * HEADS, span), F32)], axis=0)
    high = big.astype(BF16)
    low = (big - high.astype(F32)).astype(BF16)
    hot = jnp.where(lax.broadcasted_iota(jnp.int32, (n, span), 0) == bucket_rev[0:1, :], 1.0, 0.0).astype(BF16)
    table = nt(hot, high) + nt(hot, low)

    def cut(value, at, count):
        tile, shift = at // LANES, at % LANES
        out = value[:, tile * LANES : (tile + 1) * LANES]
        if shift:
            out = pltpu.roll(out, LANES - shift, 1)
            if shift + count > LANES:
                more = pltpu.roll(value[:, (tile + 1) * LANES : (tile + 2) * LANES], LANES - shift, 1)
                out = jnp.where(lane < LANES - shift, out, more)
        return jnp.where(lane < count, out, 0.0)

    half = rows_ff // 2
    blocks = []
    for d in range(n):
        low_rows = jnp.where(row == 0, cut(inner, d * half, half), 0.0)
        low_rows = jnp.where(row == 1, table[d : d + 1], low_rows)
        last_rows = jnp.where(row == 0, cut(inner, (n + d) * half, half), 0.0)
        block = [cut(vecs, d * rows_d, rows_d), low_rows, last_rows]
        block += [jnp.zeros((rows_d - 24, LANES), F32)] * (rows_d > 24)
        blocks.append(jnp.concatenate(block, axis=0))
    put_blocks(core, place, blocks, send, keep, columns)


def attend_back_kernel(
    meta, q, k, v, lse, ctx, gctx, bias_rev, nin, frames, gatt, gin, w, vec, *refs, crossed, rows_d, counts, count,
):
    first = 2 * sum(counts)
    last = first + 2 * count == HEADS
    if last and crossed:
        gvec2, gb_inner, bucket_rev, *refs = refs
        before = [(refs[2 * i], refs[2 * i + 1], c) for i, c in enumerate(counts)]
        refs = refs[2 * len(counts) :]
    send, keep, gin_out, gvec_out, grow_out, base, gbase, delta_t, kt, dqkv, gk, gv, masks = refs
    rows, width = frames.shape
    unit = rows // UNITS
    window = rows - unit
    head = width // HEADS
    core = meta[5]
    place = [meta[6 + 2 * len(crossed) + i] for i in range(2 * len(crossed))]
    prod = gctx[...].astype(F32) * ctx[...].astype(F32)
    sel_row = lax.broadcasted_iota(jnp.int32, (16, width), 0)
    sel_col = lax.broadcasted_iota(jnp.int32, (16, width), 1)
    sel = jnp.where((sel_col >= sel_row * head) & (sel_col < (sel_row + 1) * head), 1.0, 0.0).astype(BF16)
    high = prod.astype(BF16)
    low = (prod - high.astype(F32)).astype(BF16)
    deltas = nt(sel, high) + nt(sel, low)
    for h in range(HEADS):
        delta_t[h] = deltas[h : h + 1]
    ranges = put_masks(meta, masks)
    lane = lax.broadcasted_iota(jnp.int32, (unit, LANES), 1)
    sub_lane = lax.broadcasted_iota(jnp.int32, (LANES, unit), 0)
    span = count * LANES

    def pair(step, carry):
        hp = first // 2 + step
        cols = pl.ds(pl.multiple_of(hp * LANES, LANES), LANES)
        here = pl.multiple_of(step * LANES, LANES)
        kt[...] = jnp.transpose(k[:, cols])
        gk[...] = jnp.zeros_like(gk)
        gv[...] = jnp.zeros_like(gv)
        gbase[...] = jnp.zeros_like(gbase)
        for sub in range(2):
            base[sub] = skewed(bias_rev[pl.ds(2 * hp + sub, 1), :], unit)
        for u in range(UNITS):
            ws = pl.multiple_of(ranges[u], LANES)
            win = pl.ds(ws, window)
            urows = slice(u * unit, (u + 1) * unit)
            mask = jnp.concatenate([masks[u], masks[u]], axis=1)
            kk = k[win, cols]
            vv = v[win, cols]
            qu = q[urows, cols]
            gu = gctx[urows, cols]
            offsets = [
                pl.ds(pl.multiple_of((rows - unit) + u * unit - ws - jb * unit, LANES), unit) for jb in range(UNITS - 1)
            ]
            qs = apart_heads(qu, lane, head)
            gs = apart_heads(gu, lane, head)
            rel = jnp.concatenate([jnp.concatenate([base[sub, :, o] for o in offsets], axis=0) for sub in range(2)], axis=1)
            lses = jnp.concatenate([lse[2 * hp + sub, :, urows] for sub in range(2)], axis=1)
            deltas = jnp.concatenate([delta_t[2 * hp + sub, :, urows] for sub in range(2)], axis=1)
            p = jnp.exp(nt(kk, qs) + rel + mask - lses)
            ds = (p * (nt(vv, gs) - deltas)).astype(BF16)
            gv[win, :] += nn(p.astype(BF16), gs)
            gk[win, :] += nn(ds, qs)
            gq = nn(kt[:, win], ds)
            d32 = ds.astype(F32)
            for sub in range(2):
                for jb, o in enumerate(offsets):
                    gbase[sub, :, o] += d32[jb * unit : (jb + 1) * unit, sub * unit : (sub + 1) * unit]
            gq_t = jnp.where(sub_lane < head, gq[:, :unit], gq[:, unit:])
            dqkv[urows, pl.ds(here, LANES)] = jnp.transpose(gq_t).astype(BF16) * BF16(head**-0.5)
        dqkv[:, pl.ds(span + here, LANES)] = gk[...].astype(BF16)
        dqkv[:, pl.ds(2 * span + here, LANES)] = gv[...].astype(BF16)
        for sub in range(2):
            grow_out[pl.ds(2 * step + sub, 1), :] = unskewed_sum(gbase[sub], unit)
        return carry

    grow_out[...] = jnp.zeros_like(grow_out)
    lax.fori_loop(0, count, pair, 0)
    at_columns = first * head
    grad_in = gin[...] if first else jnp.zeros((rows, width), F32)
    for part in range(3):
        d = dqkv[:, part * span : (part + 1) * span]
        grad_in = grad_in + nt(d, weight(w, slice(part * width + at_columns, part * width + at_columns + span)))
    grads = [(tn(nin[...], dqkv[...]), slice(0, 3 * span))]
    if first == 0:
        grads.append((tn(ctx[...], gatt[...].astype(BF16)), slice(3 * span, 3 * span + width)))
    for g, columns in grads:
        if crossed:
            put_blocks(core, place, row_blocks(g, rows_d), send, keep, columns)
        else:
            keep[:, columns] = g.astype(BF16)
    sums = [jnp.sum(dqkv[:, at : at + span].astype(F32), axis=0, keepdims=True) for at in (0, 2 * span)]
    gvec_out[...] = jnp.zeros_like(gvec_out)
    gvec_out[2:4, 0:span] = jnp.concatenate(sums, axis=0)
    if not last:
        gin_out[...] = grad_in
        return
    n, r = normalise(frames[...].astype(F32))
    gin_out[...] = (gatt[...] + norm_backward(n, r, vec[0:1, :], grad_in)).astype(BF16)
    gvec_out[0:1, :] = jnp.sum(grad_in * n, axis=0, keepdims=True)
    gvec_out[1:2, :] = jnp.sum(grad_in, axis=0, keepdims=True)
    if crossed:
        at = 0
        for vectors, _, c in before:
            gvec_out[2:4, at : at + c * LANES] = vectors[2:4, 0 : c * LANES]
            at += c * LANES
        gvec_out[2:4, at_columns : at_columns + span] = jnp.concatenate(sums, axis=0)
        gvec_out[4:8, :] = gvec2[0:4, :]
        grows = jnp.concatenate([grow[0 : 2 * c, :] for _, grow, c in before] + [grow_out[0 : 2 * count, :]], axis=0)
        small_blocks(
            core, place, gvec_out[...], jnp.broadcast_to(gb_inner[...], (8, gb_inner.shape[1])), grows, bucket_rev,
            send, keep, slice(3 * span, 3 * span + LANES), rows_d, gb_inner.shape[1] // len(place),
        )


def run_kernel(order, kernel, name, scalars, arrays, outs, scratch=(), spare=10, us=100, pin_in=True, pin_out=True, hbm_in=(), hbm_out=()):
    spec = pl.BlockSpec(memory_space=pltpu.VMEM)
    smem = pl.BlockSpec(memory_space=pltpu.SMEM)
    arrays = order.after(*arrays)
    arrays = [
        pltpu.with_memory_space_constraint(a, pltpu.VMEM if pin_in and i not in hbm_in else pltpu.HBM)
        for i, a in enumerate(arrays)
    ]
    limit = spare * MIB + sum(math.prod(b.shape) * jnp.dtype(b.dtype).itemsize for b in scratch)
    out = pl.pallas_call(
        kernel,
        in_specs=[smem] * len(scalars) + [spec] * len(arrays),
        out_specs=[spec] * len(outs),
        out_shape=[
            (pltpu.VMEM if pin_out and i not in hbm_out else jax.ShapeDtypeStruct)(s, d) for i, (s, d) in enumerate(outs)
        ],
        scratch_shapes=list(scratch),
        compiler_params=pltpu.CompilerParams(vmem_limit_bytes=limit),
        cost_estimate=pl.CostEstimate(flops=us * 1_000_000_000, bytes_accessed=us * 1_000_000, transcendentals=0),
        name=name,
    )(*scalars, *arrays)
    order.did(out[0])
    return out


def on_device(
    frames, ln1_gain, ln1_shift, w_query, b_query, w_key, w_value, b_value, w_out, b_out, ln2_gain, ln2_shift,
    w_inner, b_inner, w_outer, b_outer, bias_table, layout, valid, rel_index, cotangent, *, n,
):
    rows, width = frames.shape
    rows_d = w_query.shape[0]
    rows_ff = w_outer.shape[0]
    ff = w_inner.shape[1]
    span = rel_index.shape[0] + 1
    unit = rows // UNITS
    per_table = bias_table.shape[0]
    plan = plan_tables(n)
    core, chips, place = plan
    order = Order()
    direct = (
        rows_d % 8 == 0 and rows_d >= 24 and rows_ff == 4 * rows_d and max(rows_d, rows_ff, per_table) <= LANES and per_table % HEADS == 0
    )
    crossed = tuple(crossed_places(n)) if direct else ()
    crossed_outer = tuple(crossed_places(n, "outer")) if direct else ()
    unit_half = rows_ff // 2
    apart = [(d * rows_ff + h * unit_half, h * ff // 2 + d * unit_half, unit_half) for h in range(2) for d in range(n)]
    together = [(b, a, c) for a, b, c in apart]
    meta = [layout, valid.reshape(-1), core[None]]
    if direct:
        _, chips_outer, place_outer = plan_tables(n, "outer")
        meta += [chips, chips_outer, place, place_outer]
    meta = jnp.concatenate(meta).astype(jnp.int32)
    small_d = jnp.stack([ln1_gain, ln1_shift, b_query, b_value, b_out, ln2_gain, ln2_shift, b_outer])

    base = pltpu.VMEM((2, unit, span), F32)
    masks = pltpu.VMEM((UNITS, rows - unit, unit), F32)
    if direct:
        vectors = (ln1_gain, ln1_shift, b_query, b_value, b_out, ln2_gain, ln2_shift, b_outer, b_inner, bias_table)
        (part1,) = run_kernel(
            Order(), functools.partial(pack_first_kernel, rows_ff=rows_ff), "pack_first", [],
            [w_query, w_key, w_value, *(v[None] for v in vectors)], [((1, rows_d, 3 * width + LANES), BF16)],
            [pltpu.VMEM((rows_d, LANES), F32)], spare=4, pin_in=False,
        )
        g1 = Gather(part1, n, order)
        part2, part3 = run_kernel(
            order, functools.partial(pack_feed_kernel, moves=apart), "pack_feed", [], [w_inner, w_outer, w_out],
            [((1, rows_d, ff + width), BF16), ((1, rows_d, ff), BF16)], spare=4, pin_in=False,
        )
        g3 = Gather(part3, n, order, "outer")
        (part2,) = lax.optimization_barrier((part2, g1.got))[:1]
        g2 = Gather(part2, n, order)
        (g2.got,) = lax.optimization_barrier((g2.got, g3.got))[:1]
        for g in (g1, g1, g2, g1, g2, g3):
            g.step()
        (g2.got,) = lax.optimization_barrier((g2.got, g1.got))[:1]
        for g in (g2, g3):
            g.step()
        first = g1.finish()
        each = per_table // HEADS
        index = jnp.stack([rel_index // each, rel_index % each])
        bucket_rev = jnp.pad(index[:, ::-1], ((0, 6), (0, 1)), constant_values=-1)
        q, k, v, nin, w1, vec, inner_bias, bias_rev = run_kernel(
            order, functools.partial(project_kernel, crossed=crossed, rows_d=rows_d, rows_ff=rows_ff), "project", [meta],
            [frames, *first, bucket_rev],
            [((rows, width), BF16)] * 4
            + [((n // 2, 2 * rows_d, 3 * width), BF16), ((8, width), F32), ((1, ff), F32), ((16, span), F32)],
            [
                pltpu.VMEM((width // LANES + 1, 8, LANES), F32),
                pltpu.VMEM((ff // LANES + 1, 8, LANES), F32),
                pltpu.VMEM((n, LANES), F32),
            ],
            us=1, hbm_in=(0,),
        )
        chunk = [[((n // 2, rows_d, c), BF16)] * 2 for c in (ff, ff)]
        w_out_whole = [((n // 2, 2 * rows_d, width), BF16)]
        unpacked = [pltpu.VMEM((n // 2, 2 * rows_d, width), BF16), pltpu.VMEM((n // 2, rows_ff, width), BF16)]
    else:
        flat = jnp.concatenate([small_d.reshape(-1), b_inner, bias_table])
        per = flat.shape[0] // rows_d
        small = jnp.pad(flat.reshape(rows_d, per), ((0, 0), (0, LANES - per)))
        w1 = gathered(Gather(jnp.concatenate([w_query, w_key, w_value, small], axis=1), n, order).finish(), plan, n)
        w2 = (gathered(Gather(jnp.concatenate([w_inner, w_out], axis=1), n, order).finish(), plan, n),)
        w2 += (gathered(Gather(w_outer, n, order).finish(), plan, n),)
        flats = w1[:, 3 * width : 3 * width + per].reshape(n, rows_d * per)
        vec = flats[:, : 8 * rows_d].reshape(n, 8, rows_d).transpose(1, 0, 2).reshape(8, width).astype(F32)
        inner_bias = flats[:, 8 * rows_d : 8 * rows_d + rows_ff].reshape(1, ff).astype(F32)
        table = jnp.pad(flats[:, 8 * rows_d + rows_ff :].reshape(-1, HEADS), ((0, 0), (0, 16 - HEADS)))
        index_rev = jnp.pad(rel_index[::-1], (0, 1), constant_values=-1)
        ids = jnp.arange(table.shape[0], dtype=jnp.int32)[:, None]
        bias_rev = tn(table, (ids == index_rev[None]).astype(BF16))
        q, k, v, nin = run_kernel(
            order, project_body, "project", [meta], [frames, w1, vec], [((rows, width), BF16)] * 4
        )
        chunk = [[((8, LANES), BF16), ((c, max(width, ff // 2), max(width, ff // 2)), BF16)] for c in (2, 2)]
        w_out_whole = []
        unpacked = []

    ctx, lse = run_kernel(
        order, attend_kernel, "attend", [meta], [q, k, v, bias_rev],
        [((rows, width), BF16), ((HEADS, 1, rows), F32)], [base, pltpu.VMEM((LANES, rows), BF16), masks], spare=4, us=1,
    )

    def start(send, keep, scatter):
        return scatter.add(*((send, keep) if direct else split_natural(keep, plan, n)))

    if direct:
        g3.step()
        w2 = g2.finish()
    att, nmid, acc, gmid, gb1, send1, keep1, *w_out_all = run_kernel(
        order, functools.partial(feed_first_kernel, crossed=crossed, rows_d=rows_d), "feed_first", [meta],
        [frames, ctx, vec, inner_bias, cotangent, *w2],
        [((rows, width), F32), ((rows, width), BF16), ((rows, width), F32), ((rows, width), F32), ((1, ff // 2), F32)]
        + chunk[0] + w_out_whole,
        unpacked, spare=12,
    )
    if direct:
        w3 = g3.finish()
        begin = functools.partial(Scatter, n, order)
        sum_1 = begin("outer").add(send1, keep1)
    else:
        w3 = w2
    mixed, gatt, gctx, send2, keep2, gb2, gvec2 = run_kernel(
        order, functools.partial(feed_second_kernel, crossed=crossed_outer, rows_d=rows_d), "feed_second", [meta],
        [att, nmid, acc, gmid, ctx, vec, inner_bias, cotangent, *w_out_all, *w3],
        [((rows, width), BF16), ((rows, width), F32), ((rows, width), BF16)] + chunk[1]
        + [((1, ff // 2), F32), ((8, width), F32)],
        [pltpu.VMEM((rows, width), F32)] * 2 + unpacked, spare=12, hbm_out=(0,),
    )
    gb_inner = jnp.concatenate([gb1, gb2], axis=1)
    if direct:
        sum_1.step(2)
        sum_2 = begin().add(send2, keep2)
    else:
        whole_inner = jnp.concatenate([keep1[0, :width, : ff // 2], keep2[0, :width, : ff // 2]], axis=1)
        whole_outer = jnp.concatenate([keep1[1, : ff // 2, :width], keep2[1, : ff // 2, :width]], axis=0)
        begin = functools.partial(Scatter, n, order)
        sum_1 = begin().add(*split_natural(whole_outer, plan, n))
        sum_2 = begin().add(*split_natural(whole_inner, plan, n))

    counts = COUNTS
    passed = gatt
    done, earlier = [], []
    sum_early, sum_late = begin(), begin()
    for call, count in enumerate(counts):
        cols = count * LANES
        last = call == len(counts) - 1
        wide = 3 * cols + LANES * (last and direct) + width * (call == 0)
        part = [((n // 2, rows_d, wide), BF16)] * 2 if direct else [((8, LANES), BF16), ((width, wide), BF16)]
        extra = [gvec2, gb_inner, bucket_rev] + [a for pair in earlier for a in pair] if last and direct else []
        send, keep, passed, gvec1, grow = run_kernel(
            order,
            functools.partial(
                attend_back_kernel, crossed=crossed, rows_d=rows_d, counts=counts[:call], count=count
            ),
            "attend_back", [meta],
            [q, k, v, lse, ctx, gctx, bias_rev, nin, frames, gatt, passed, w1, vec] + extra,
            part + [((rows, width), BF16 if last else F32), ((8, width), F32), ((8, span), F32)],
            [
                base, base,
                pltpu.VMEM((HEADS, 1, rows), F32),
                pltpu.VMEM((LANES, rows), BF16),
                pltpu.VMEM((rows, 3 * cols), BF16),
                pltpu.VMEM((rows, LANES), F32),
                pltpu.VMEM((rows, LANES), F32),
                masks,
            ],
            spare=10, hbm_out=(2,) if last else (),
        )
        earlier.append((gvec1, grow))
        start(send, keep, sum_late if call else sum_early)
        if call == 0:
            sum_1.step(2)
            sum_2.step()
    for each_sum in (sum_early, sum_1, sum_2, sum_late, sum_early, sum_1, sum_2, sum_late, sum_early, sum_2, sum_late, sum_early, sum_late):
        if each_sum.steps:
            each_sum.step()
    sum_1, sum_2, early, late = sum_1.finish(), sum_2.finish(), sum_early.finish(), sum_late.finish()
    if direct:
        both = jnp.concatenate([sum_1[:, : ff // 2], sum_2[:, : ff // 2]], axis=1)
        (grad_inner,) = run_kernel(
            Order(), functools.partial(move_kernel, moves=together), "together", [], [both], [((rows_d, ff), F32)]
        )
        folded = (sum_1[:, ff // 2 :], sum_2[:, ff // 2 : ff])
        grad_outer = jnp.concatenate([f[:, i * width : (i + 1) * width] for f in folded for i in range(2)], axis=0)
    else:
        grad_inner, grad_outer = sum_2[:, :ff], sum_1
    if direct:
        sum_q, sum_k, sum_v = run_kernel(
            Order(), functools.partial(columns_kernel, counts=counts), "columns", [], [early, late],
            [((rows_d, width), F32)] * 3, spare=4, pin_out=False,
        )
        small = late[:, 3 * LANES * sum(counts[1:]) :]
        vecs = small[:8, :rows_d]
        sum_b_inner = jnp.concatenate([small[8, :unit_half], small[16, :unit_half]])
        sum_table = small[9, :per_table]
    else:
        places = [3 * LANES * sum(counts[1:call]) for call in range(len(counts))]
        calls = list(zip([early] + [late] * len(counts[1:]), places, [c * LANES for c in counts]))
        sum_q, sum_k, sum_v = (
            jnp.concatenate([p[:, at + i * cols : at + (i + 1) * cols] for p, at, cols in calls], axis=1) for i in range(3)
        )
        hot_rev = (ids == index_rev[None]).astype(F32)
        grow = jnp.concatenate([g[: 2 * c] for (_, g), c in zip(earlier, counts)])
        gtable = lax.dot_general(
            hot_rev, grow, (((1,), (1,)), ((), ())), precision=lax.Precision.HIGHEST, preferred_element_type=F32
        )
        gbias = jnp.concatenate([g[2:4, : c * LANES] for (g, _), c in zip(earlier, counts)], axis=1)
        gsmall = jnp.concatenate([gvec1[0:2], gbias, gvec2[0:4]])
        gsmall = gsmall.reshape(8, n, rows_d).transpose(1, 0, 2).reshape(n, 8 * rows_d)
        gflat = jnp.concatenate([gsmall, gb_inner.reshape(n, rows_ff), gtable.reshape(n, -1)], axis=1)
        gflat = jnp.pad(gflat, ((0, 0), (0, -gflat.shape[1] % LANES))).astype(BF16)
        sum_flat = Scatter(n, order).add(*split_natural(gflat, plan, n)).finish()[0]
        vecs = sum_flat[: 8 * rows_d].reshape(8, rows_d)
        sum_b_inner = sum_flat[8 * rows_d : 8 * rows_d + rows_ff]
        sum_table = sum_flat[8 * rows_d + rows_ff : 8 * rows_d + rows_ff + per_table]
    return (
        mixed, passed, vecs[0], vecs[1], sum_q, vecs[2], sum_k, sum_v, vecs[3],
        early[:, 3 * LANES * counts[0] :], vecs[4], vecs[5], vecs[6], grad_inner, sum_b_inner, grad_outer, vecs[7], sum_table,
    )


def solution(mesh):
    row, two = P("dp"), P("dp", None)
    in_specs = (two, row, row, two, row, two, two, row, two, row, row, row, two, row, two, row, row, row, two, P(), two)
    out_specs = (two, two, row, row, two, row, two, two, row, two, row, row, row, two, row, two, row, row)
    return jax.shard_map(
        functools.partial(on_device, n=mesh.shape["dp"]),
        mesh=mesh, in_specs=in_specs, out_specs=out_specs, check_vma=False,
    )
```

```python
import functools
import math

import jax
import jax.numpy as jnp
import numpy as np
from jax import lax
from jax.experimental import pallas as pl
from jax.experimental.pallas import tpu as pltpu
from jax.sharding import PartitionSpec as P

HEADS = 12
LANES = 128
UNITS = 4
MASKED = -1e30
F32 = jnp.float32
BF16 = jnp.bfloat16
SEGMENT = ((0, 0, 0, 1), (0, 0, 1, 1), (0, 0, 1, 2), (0, 1, 2, 3))
START = ((0, 0, 0, 3), (0, 0, 2, 2), (0, 0, 2, 3), (0, 1, 2, 3))
MIB = 1024 * 1024
COUNTS = (3, 3)


def bit_orders(n, kind):
    chip = [1 << k for k in range(1, n.bit_length() - 1)]
    low, high = chip[:2], chip[2:][::-1]
    if kind == "outer":
        return (low[:1] + high + low[1:], low[1:] + high + low[:1])
    return (high + low, high + low[::-1])


def gather_masks(bits):
    masks = [0]
    for bit in bits:
        masks = masks + [bit ^ m for m in masks]
    return masks


def scatter_masks(bits):
    masks = [0]
    for bit in bits:
        masks = [bit ^ m for m in masks] + masks
    return masks


def pairs(n, by_core):
    return [(i, i ^ by_core[i & 1]) for i in range(n)]


class Order:
    def __init__(self):
        self.last = None

    def after(self, *arrays):
        if self.last is None:
            return arrays
        return lax.optimization_barrier((*arrays, self.last))[:-1]

    def did(self, array):
        self.last = array


class Gather:
    def __init__(self, part, n, order, kind="inner"):
        self.n = n
        self.order = order
        self.steps = list(zip(*bit_orders(n, kind)))
        self.held = part if part.ndim == 3 else part[None]
        self.got = lax.ppermute(self.held, "dp", pairs(n, self.steps.pop(0)))

    def step(self):
        pair = self.order.after(self.held, self.got)
        self.held = jnp.concatenate(pair, axis=0)
        self.order.did(self.held)
        self.got = lax.ppermute(self.held, "dp", pairs(self.n, self.steps.pop(0)))
        return self

    def finish(self):
        while self.steps:
            self.step()
        (self.got,) = self.order.after(self.got)
        swap = pairs(self.n, (1, 1))
        return (self.held, self.got, lax.ppermute(self.held, "dp", swap), lax.ppermute(self.got, "dp", swap))


class Scatter:
    def __init__(self, n, order, kind="inner"):
        self.n = n
        self.order = order
        self.parts = []
        self.terms = []
        self.at = 0
        self.steps = list(reversed(list(zip(*bit_orders(n, kind)))))
        self.half = n // 4

    def add(self, send, keep):
        self.parts.append((keep, lax.ppermute(send, "dp", pairs(self.n, (1, 1)))))
        return self

    def total(self, count, dtype):
        at = self.at
        held = [(t, first) for t, first in self.terms if first <= at and at + count <= first + t.shape[0]]
        flat = [t for part in self.parts for t in part] + [t for t, _ in held]
        flat = list(self.order.after(*flat))
        cut = [lax.slice_in_dim(t, at, at + count).astype(F32) for t in flat[: 2 * len(self.parts)]]
        out = [cut[2 * i] + cut[2 * i + 1] for i in range(len(self.parts))]
        out = out[0] if len(out) == 1 else jnp.concatenate(out, axis=-1)
        for t, (_, first) in zip(flat[2 * len(self.parts) :], held):
            out = out + lax.slice_in_dim(t, at - first, at - first + count).astype(F32)
        out = out.astype(dtype)
        self.order.did(out)
        return out

    def step(self, transfers=1):
        by_core = self.steps.pop(0)
        count = self.half // transfers
        for _ in range(transfers):
            out = self.total(count, BF16)
            self.terms.append((lax.ppermute(out, "dp", pairs(self.n, by_core)), self.at + self.half))
            self.at += count
        self.half //= 2

    def finish(self):
        while self.steps:
            self.step()
        return self.total(1, F32)[0]


def plan_tables(n, kind="inner"):
    orders = bit_orders(n, kind)
    me = lax.axis_index("dp")
    core = me & 1
    g = np.array([gather_masks(o) for o in orders], np.int32)
    s = np.array([scatter_masks(o) for o in orders], np.int32)
    inverse = np.zeros((2, n), np.int32)
    for c in (0, 1):
        for i, m in enumerate(s[c]):
            inverse[c, m] = i
    devices = jnp.arange(n, dtype=jnp.int32)
    chips = (me ^ jnp.where(core == 0, jnp.asarray(g[0]), jnp.asarray(g[1]))) >> 1
    mask = (devices ^ me) & ~1
    place = jnp.sum(jnp.where(mask[:, None] == devices[None, :], jnp.asarray(inverse)[np.arange(n) % 2], 0), axis=1)
    return core, chips, place


def crossed_places(n, kind="inner"):
    first, second = (gather_masks(o) for o in bit_orders(n, kind))
    places = [second.index(m) for m in first]
    assert places == [first.index(m) for m in second]
    return places


def gathered(parts, plan, n):
    core, chips, _ = plan
    mine = jnp.concatenate(parts[:2])
    theirs = jnp.concatenate(parts[2:])[np.array(crossed_places(n))]
    both = jnp.where(core == 0, jnp.stack([mine, theirs], 1), jnp.stack([theirs, mine], 1))
    return both[jnp.argsort(chips)].reshape(n * mine.shape[1], mine.shape[2])


def split_natural(grad, plan, n):
    core, _, place = plan
    rows = grad.shape[0] // n
    blocks = grad.reshape(n // 2, 2, rows, grad.shape[1])
    mine = jnp.where(core == 0, blocks[:, 0], blocks[:, 1])
    theirs = jnp.where(core == 0, blocks[:, 1], blocks[:, 0])
    both = place.reshape(n // 2, 2)
    my_place = jnp.where(core == 0, both[:, 0], both[:, 1])
    their_place = jnp.where(core == 0, both[:, 1], both[:, 0])
    return theirs[jnp.argsort(their_place)], mine[jnp.argsort(my_place)]


def nn(a, b):
    return jnp.dot(a, b, preferred_element_type=F32)


def nt(a, b):
    return lax.dot_general(a, b, (((1,), (1,)), ((), ())), preferred_element_type=F32)


def tn(a, b):
    return lax.dot_general(a, b, (((0,), (0,)), ((), ())), preferred_element_type=F32)


def normalise(v):
    centred = v - jnp.mean(v, axis=-1, keepdims=True)
    r = lax.rsqrt(jnp.mean(centred * centred, axis=-1, keepdims=True) + 1e-05)
    return centred * r, r


def norm_backward(n, r, gain, e):
    eg = e * gain
    return r * (eg - jnp.mean(eg, axis=-1, keepdims=True) - n * jnp.mean(eg * n, axis=-1, keepdims=True))


def pick(table, code, u):
    out = jnp.int32(table[0][u])
    for c in range(1, 4):
        out = jnp.where(code == c, jnp.int32(table[c][u]), out)
    return out


def unit_range(meta, u, unit):
    code = meta[0]
    segment = pick(SEGMENT, code, u)
    start = pick(START, code, u)
    count = meta[1]
    for s in range(1, 4):
        count = jnp.where(segment == s, meta[1 + s], count)
    window = jnp.minimum(start, 1) * unit
    return start * unit, start * unit + count, window


def put_masks(meta, masks):
    units, window, unit = masks.shape
    row_at = lax.broadcasted_iota(jnp.int32, (window, unit), 0)
    starts = []
    for u in range(units):
        first, end, start = unit_range(meta, u, unit)
        masks[u] = jnp.where((row_at + start >= first) & (row_at + start < end), 0.0, MASKED)
        starts.append(start)
    return starts


def skewed(row, unit):
    wide = jnp.broadcast_to(row, (unit, row.shape[1]))
    return pltpu.roll(wide, row.shape[1] - (unit - 1), 1, stride=1, stride_axis=0)


def unskewed_sum(block, unit):
    width = block.shape[1]
    total = None
    for a in range(unit // 8):
        part = block[8 * a : 8 * a + 8]
        shift = (unit - 1 - 8 * a) % width
        part = pltpu.roll(part, shift, 1) if shift else part
        total = part if total is None else total + part
    out = total[0:1]
    for s in range(1, 8):
        out = out + pltpu.roll(total[s : s + 1], width - s, 1)
    return out


def unpack(core, chips, parts, crossed, out, columns):
    half = parts[0].shape[0]
    for i, j in enumerate(crossed):
        mine = parts[i // half][i % half, :, columns]
        theirs = parts[2 + j // half][j % half, :, columns]
        first = jnp.where(core == 0, mine, theirs)
        second = jnp.where(core == 0, theirs, mine)
        out[chips[i]] = jnp.concatenate([first, second], axis=0)


def weight(ref, columns):
    value = ref[..., columns]
    return value.reshape(-1, value.shape[-1])


def put_blocks(core, places, blocks, send, keep, columns):
    for plane in range(2):

        @pl.when(core == plane)
        def _(plane=plane):
            for at, (place, block) in enumerate(zip(places, blocks)):
                (keep if at % 2 == plane else send)[place, :, columns] = block.astype(BF16)


def row_blocks(value, rows):
    return [value[at : at + rows] for at in range(0, value.shape[0], rows)]


def project_body(meta, frames, w, vec, q_out, k_out, v_out, nin_out):
    width = frames.shape[1]
    head = width // HEADS
    n, _ = normalise(frames[...].astype(F32))
    nin = (n * vec[0:1, :] + vec[1:2, :]).astype(BF16)
    nin_out[...] = nin
    q_out[...] = ((nn(nin, weight(w, slice(0, width))) + vec[2:3, :]) * (head**-0.5)).astype(BF16)
    k_out[...] = nn(nin, weight(w, slice(width, 2 * width))).astype(BF16)
    v_out[...] = (nn(nin, weight(w, slice(2 * width, 3 * width))) + vec[3:4, :]).astype(BF16)


def apart_heads(rows, lane, head):
    zero = jnp.zeros_like(rows)
    return jnp.concatenate([jnp.where(lane < head, rows, zero), jnp.where(lane < head, zero, rows)], axis=0)


def attend_kernel(meta, q, k, v, bias_rev, ctx_out, lse_out, base, vt, masks):
    rows, width = q.shape
    unit = rows // UNITS
    window = rows - unit
    head = width // HEADS
    ranges = put_masks(meta, masks)
    lane = lax.broadcasted_iota(jnp.int32, (unit, LANES), 1)
    sub_lane = lax.broadcasted_iota(jnp.int32, (LANES, unit), 0)

    def pair(hp, carry):
        cols = pl.ds(pl.multiple_of(hp * LANES, LANES), LANES)
        vt[...] = jnp.transpose(v[:, cols])
        for sub in range(2):
            base[sub] = skewed(bias_rev[pl.ds(2 * hp + sub, 1), :], unit)
        for u in range(UNITS):
            ws = pl.multiple_of(ranges[u], LANES)
            win = pl.ds(ws, window)
            urows = slice(u * unit, (u + 1) * unit)
            kk = k[win, cols]
            qu = q[urows, cols]
            offsets = [
                pl.ds(pl.multiple_of((rows - unit) + u * unit - ws - jb * unit, LANES), unit) for jb in range(UNITS - 1)
            ]
            parts = []
            for sub in range(2):
                qs = jnp.where((lane >= head) == bool(sub), qu, jnp.zeros_like(qu))
                rel = jnp.concatenate([base[sub, :, o] for o in offsets], axis=0)
                s = nt(kk, qs) + rel + masks[u]
                top = jnp.max(s, axis=0, keepdims=True)
                e = jnp.exp(s - top)
                tot = jnp.sum(e, axis=0, keepdims=True)
                parts.append(nn(vt[:, win], e.astype(BF16)) * (1.0 / tot))
                lse_out[2 * hp + sub, :, urows] = top + jnp.log(tot)
            ctx_out[urows, cols] = jnp.transpose(jnp.where(sub_lane < head, parts[0], parts[1])).astype(BF16)
        return carry

    lax.fori_loop(0, HEADS // 2, pair, 0)


def small_vectors(core, chips, parts, crossed, at, rows_d, rows_ff, vec3, inner3, table):
    half = parts[0].shape[0]
    lane = lax.broadcasted_iota(jnp.int32, (8, LANES), 1)
    vec3[...] = jnp.zeros_like(vec3)
    inner3[...] = jnp.zeros_like(inner3)
    for i, j in enumerate(crossed):
        mine = parts[i // half][i % half, :, at : at + LANES].astype(F32)
        theirs = parts[2 + j // half][j % half, :, at : at + LANES].astype(F32)
        for plane in range(2):
            block = jnp.where(core == plane, mine, theirs)
            d = 2 * chips[i] + plane
            unit_half = rows_ff // 2
            half_at = 2 * half * rows_ff
            for first, rows, part, out in (
                (0, rows_d, block[0:8], vec3),
                (0, unit_half, block[8:16], inner3),
                (half_at, unit_half, block[16:24], inner3),
            ):
                start = first + d * rows
                tile = start >> 7
                shift = start & (LANES - 1)
                rolled = pltpu.roll(part, shift, 1)
                out[tile] += jnp.where(lane >= shift, rolled, 0.0)
                out[tile + 1] += jnp.where(lane < shift, rolled, 0.0)
            table[pl.ds(d, 1), :] = block[9:10]


def relative_rows(bucket, table, out):
    devices = lax.broadcasted_iota(jnp.int32, (table.shape[0], bucket.shape[1]), 0)
    hot = jnp.where(devices == bucket[0:1, :], 1.0, 0.0).astype(BF16)
    rows = tn(table[...].astype(BF16), hot)
    total = jnp.zeros((HEADS, bucket.shape[1]), F32)
    for m in range(LANES // HEADS):
        total = total + jnp.where(bucket[1:2, :] == m, rows[m * HEADS : (m + 1) * HEADS], 0.0)
    out[0:HEADS, :] = total
    out[HEADS:, :] = jnp.zeros_like(out[HEADS:, :])


def project_kernel(
    meta, frames, p0, p1, p2, p3, bucket_rev,
    q_out, k_out, v_out, nin_out, w, vec, b_inner, bias_rev,
    vec3, inner3, table, *, crossed, rows_d, rows_ff,
):
    width = frames.shape[1]
    core = meta[5]
    chips = [meta[6 + i] for i in range(len(crossed))]
    parts = (p0, p1, p2, p3)
    small_vectors(core, chips, parts, crossed, 3 * width, rows_d, rows_ff, vec3, inner3, table)
    for a in range(width // LANES):
        vec[:, a * LANES : (a + 1) * LANES] = vec3[a]
    for a in range(b_inner.shape[1] // LANES):
        b_inner[:, a * LANES : (a + 1) * LANES] = inner3[a, 0:1]
    relative_rows(bucket_rev, table, bias_rev)
    unpack(core, chips, parts, crossed, w, slice(0, 3 * width))
    project_body(meta, frames, w, vec, q_out, k_out, v_out, nin_out)


def unpack_folded(core, chips, parts, crossed, out, at, width):
    half = parts[0].shape[0]
    for i, j in enumerate(crossed):
        mine = parts[i // half][i % half, :, at : at + 2 * width]
        theirs = parts[2 + j // half][j % half, :, at : at + 2 * width]
        first = jnp.where(core == 0, mine, theirs)
        second = jnp.where(core == 0, theirs, mine)
        rows = [first[:, :width], first[:, width:], second[:, :width], second[:, width:]]
        out[chips[i]] = jnp.concatenate(rows, axis=0)


def feed_tiles(meta, kind, crossed, parts, natural, b_inner, cot, first, nmid, acc, gmid, gb_out, send, keep, w_tile, w_rows, rows_d):
    width = nmid.shape[1]
    tiles = b_inner.shape[1] // width // 2
    if crossed:
        half = len(crossed)
        core = meta[5]
        chips_at = 6 + half * (kind == "outer")
        chips = [meta[chips_at + i] for i in range(half)]
        place_at = 6 + 2 * half + 2 * half * (first == 0)
        place = [meta[place_at + i] for i in range(2 * half)]
        unpack_folded(core, chips, parts, crossed, w_rows, tiles * width, width)
        w_outer = w_rows.reshape(tiles * width, width)
    else:
        w, w_outer = natural

    def tile(t, carry):
        here = pl.multiple_of(t * width, LANES)
        cols = pl.ds(here, width)
        all_cols = pl.ds(pl.multiple_of(first + here, LANES), width)
        if crossed:
            unpack(core, chips, parts, crossed, w_tile, cols)
            wi = weight(w_tile, slice(None))
            wo = w_outer[cols, :]
        else:
            wi = w[:, all_cols]
            wo = w_outer[all_cols, :]
        v = nn(nmid[...], wi) + b_inner[:, all_cols]
        phi = 0.5 * (1.0 + lax.erf(v * (0.5**0.5)))
        act = (v * phi).astype(BF16)
        slope = phi + v * jnp.exp(-0.5 * v * v) * 0.3989422804014327
        acc[...] += nn(act, wo)
        gi = (slope * nt(cot[...], wo)).astype(BF16)
        gb_out[:, cols] = jnp.sum(gi.astype(F32), axis=0, keepdims=True)
        gmid[...] += nt(gi, wi)
        g_outer = tn(act, cot[...])
        g_inner = tn(nmid[...], gi)
        if crossed:
            put_blocks(core, place, row_blocks(g_inner, rows_d), send, keep, cols)
            per = width // (2 * rows_d)
            places = [meta[place_at + t * per + at] for at in range(per)]
            rows = row_blocks(g_outer, rows_d)
            blocks = [jnp.concatenate(rows[2 * at : 2 * at + 2], axis=1) for at in range(per)]
            put_blocks(core, places, blocks, send, keep, slice(tiles * width, (tiles + 2) * width))
        else:
            keep[0, :width, cols] = g_inner.astype(BF16)
            keep[1, cols, :width] = g_outer.astype(BF16)
        return carry

    lax.fori_loop(0, tiles, tile, 0)


def feed_first_kernel(meta, frames, ctx, vec, b_inner, cot, *refs, crossed, rows_d):
    rows, width = frames.shape
    ff = b_inner.shape[1]
    if crossed:
        parts, refs = refs[:4], refs[4:]
        att, nmid, acc, gmid, gb_out, send, keep, w_out, w_tile, w_rows = refs
        chips = [meta[6 + i] for i in range(len(crossed))]
        unpack(meta[5], chips, parts, crossed, w_out, slice(ff, ff + width))
        wo, natural = weight(w_out, slice(None)), None
    else:
        w, w_outer, att, nmid, acc, gmid, gb_out, send, keep = refs
        parts, natural, w_tile, w_rows = None, (w, w_outer), None, None
        wo = w[:, ff : ff + width]
    attended = frames[...].astype(F32) + nn(ctx[...], wo) + vec[4:5, :]
    att[...] = attended
    n, _ = normalise(attended)
    nmid[...] = (n * vec[5:6, :] + vec[6:7, :]).astype(BF16)
    acc[...] = attended + vec[7:8, :]
    gmid[...] = jnp.zeros_like(gmid)
    feed_tiles(
        meta, "inner", crossed, parts, natural, b_inner, cot, 0, nmid, acc, gmid, gb_out, send, keep, w_tile, w_rows, rows_d
    )


def feed_second_kernel(meta, att, nmid, acc_in, gmid_in, ctx, vec, b_inner, cot, *refs, crossed, rows_d):
    rows, width = att.shape
    ff = b_inner.shape[1]
    if crossed:
        w_out, parts, refs = refs[0], refs[1:5], refs[5:]
        mixed_out, gatt_out, gctx_out, send, keep, gb_out, gvec_out, acc, gmid, w_tile, w_rows = refs
        wo, natural = weight(w_out, slice(None)), None
    else:
        w, w_outer, mixed_out, gatt_out, gctx_out, send, keep, gb_out, gvec_out, acc, gmid = refs
        parts, natural, w_tile, w_rows = None, (w, w_outer), None, None
        wo = w[:, ff : ff + width]
    acc[...] = acc_in[...]
    gmid[...] = gmid_in[...]
    feed_tiles(
        meta, "outer", crossed, parts, natural, b_inner, cot, ff // 2, nmid, acc, gmid, gb_out, send, keep, w_tile, w_rows, rows_d
    )
    mixed_out[...] = acc[...].astype(BF16)
    n, r = normalise(att[...])
    e = gmid[...]
    c32 = cot[...].astype(F32)
    gatt = c32 + norm_backward(n, r, vec[5:6, :], e)
    gatt_out[...] = gatt
    gbr = gatt.astype(BF16)
    gctx_out[...] = nt(gbr, wo).astype(BF16)
    gvec_out[0:1, :] = jnp.sum(gbr.astype(F32), axis=0, keepdims=True)
    gvec_out[1:2, :] = jnp.sum(e * n, axis=0, keepdims=True)
    gvec_out[2:3, :] = jnp.sum(e, axis=0, keepdims=True)
    gvec_out[3:4, :] = jnp.sum(c32, axis=0, keepdims=True)
    gvec_out[4:8, :] = jnp.zeros_like(gvec_out[4:8, :])


def moved_lanes(value, moves):
    lane = lax.broadcasted_iota(jnp.int32, (value.shape[0], LANES), 1)
    out = [None] * (value.shape[1] // LANES)
    for source, target, count in moves:
        while count:
            step = min(count, LANES - source % LANES, LANES - target % LANES)
            piece = value[:, source - source % LANES : source - source % LANES + LANES]
            shift = (target - source) % LANES
            piece = pltpu.roll(piece, shift, 1) if shift else piece
            at = target % LANES
            old = out[target // LANES]
            inside = (lane >= at) & (lane < at + step)
            out[target // LANES] = piece if old is None else jnp.where(inside, piece, old)
            source, target, count = source + step, target + step, count - step
    return jnp.concatenate(out, axis=1)


def pack_first_kernel(*refs, rows_ff):
    w_query, w_key, w_value, *vectors, b_inner, table, out, small = refs
    rows, width = w_query.shape
    for i, part in enumerate((w_query, w_key, w_value)):
        out[0, :, i * width : (i + 1) * width] = part[...]
    half = rows_ff // 2
    small[...] = jnp.zeros_like(small)
    for i, vector in enumerate(vectors):
        small[i : i + 1, 0:rows] = vector[...].astype(F32)
    small[8:9, 0:half] = b_inner[:, 0:half].astype(F32)
    small[9:10, 0 : table.shape[1]] = table[...].astype(F32)
    small[16:17, 0:half] = b_inner[:, half:].astype(F32)
    out[0, :, 3 * width :] = small[...].astype(BF16)


def pack_feed_kernel(w_inner, w_outer, w_out, second, third, *, moves):
    rows, width = w_out.shape
    half = w_inner.shape[1] // 2
    inner = moved_lanes(w_inner[...].astype(F32), moves).astype(BF16)
    for part, out in enumerate((second, third)):
        out[0, :, 0:half] = inner[:, part * half : (part + 1) * half]
        for i in range(2):
            at = (2 * part + i) * rows
            out[0, :, half + i * width : half + (i + 1) * width] = w_outer[at : at + rows, :]
    second[0, :, 2 * half :] = w_out[...]


def columns_kernel(early, late, q_out, k_out, v_out, inner_out, table_out, *vectors, counts):
    at = first = 0
    for call, count in enumerate(counts):
        cols = count * LANES
        for i, out in enumerate((q_out, k_out, v_out)):
            out[:, at : at + cols] = (late if call else early)[:, first + i * cols : first + (i + 1) * cols]
        at += cols
        first = first + 3 * cols if call else 0
    rows = vectors[0].shape[0]
    half = inner_out.shape[0] // 2
    for i, out in enumerate(vectors):
        out[...] = late[i, first : first + rows]
    inner_out[0:half] = late[8, first : first + half]
    inner_out[half:] = late[16, first : first + half]
    table_out[...] = late[9, first : first + table_out.shape[0]]


def feed_columns_kernel(first, second, early, inner_out, outer_out, w_out, *, moves):
    rows, width = w_out.shape
    half = inner_out.shape[1] // 2
    both = jnp.concatenate([first[:, 0:half], second[:, 0:half]], axis=1)
    inner_out[...] = moved_lanes(both, moves)
    for part, value in enumerate((first, second)):
        for i in range(2):
            at = (2 * part + i) * rows
            outer_out[at : at + rows, :] = value[:, half + i * width : half + (i + 1) * width]
    w_out[...] = early[:, early.shape[1] - width :]


def small_blocks(core, place, vecs, inner, grows, bucket_rev, send, keep, columns, rows_d, rows_ff):
    n = len(place)
    span = bucket_rev.shape[1]
    row = lax.broadcasted_iota(jnp.int32, (8, LANES), 0)
    lane = lax.broadcasted_iota(jnp.int32, (8, LANES), 1)
    each = LANES // HEADS
    big = [jnp.where(bucket_rev[1:2, :] == m, grows, 0.0) for m in range(each)]
    big = jnp.concatenate(big + [jnp.zeros((LANES - each * HEADS, span), F32)], axis=0)
    high = big.astype(BF16)
    low = (big - high.astype(F32)).astype(BF16)
    hot = jnp.where(lax.broadcasted_iota(jnp.int32, (n, span), 0) == bucket_rev[0:1, :], 1.0, 0.0).astype(BF16)
    table = nt(hot, high) + nt(hot, low)

    def cut(value, at, count):
        tile, shift = at // LANES, at % LANES
        out = value[:, tile * LANES : (tile + 1) * LANES]
        if shift:
            out = pltpu.roll(out, LANES - shift, 1)
            if shift + count > LANES:
                more = pltpu.roll(value[:, (tile + 1) * LANES : (tile + 2) * LANES], LANES - shift, 1)
                out = jnp.where(lane < LANES - shift, out, more)
        return jnp.where(lane < count, out, 0.0)

    half = rows_ff // 2
    blocks = []
    for d in range(n):
        low_rows = jnp.where(row == 0, cut(inner, d * half, half), 0.0)
        low_rows = jnp.where(row == 1, table[d : d + 1], low_rows)
        last_rows = jnp.where(row == 0, cut(inner, (n + d) * half, half), 0.0)
        block = [cut(vecs, d * rows_d, rows_d), low_rows, last_rows]
        block += [jnp.zeros((rows_d - 24, LANES), F32)] * (rows_d > 24)
        blocks.append(jnp.concatenate(block, axis=0))
    put_blocks(core, place, blocks, send, keep, columns)


def attend_back_kernel(
    meta, q, k, v, lse, ctx, gctx, bias_rev, nin, frames, gatt, gin, w, vec, *refs, crossed, rows_d, counts, count,
):
    first = 2 * sum(counts)
    last = first + 2 * count == HEADS
    if last and crossed:
        gvec2, gb_inner, bucket_rev, *refs = refs
        before = [(refs[2 * i], refs[2 * i + 1], c) for i, c in enumerate(counts)]
        refs = refs[2 * len(counts) :]
    send, keep, gin_out, gvec_out, grow_out, base, gbase, delta_t, kt, dqkv, gk, gv, masks = refs
    rows, width = frames.shape
    unit = rows // UNITS
    window = rows - unit
    head = width // HEADS
    core = meta[5]
    place = [meta[6 + 2 * len(crossed) + i] for i in range(2 * len(crossed))]
    prod = gctx[...].astype(F32) * ctx[...].astype(F32)
    sel_row = lax.broadcasted_iota(jnp.int32, (16, width), 0)
    sel_col = lax.broadcasted_iota(jnp.int32, (16, width), 1)
    sel = jnp.where((sel_col >= sel_row * head) & (sel_col < (sel_row + 1) * head), 1.0, 0.0).astype(BF16)
    high = prod.astype(BF16)
    low = (prod - high.astype(F32)).astype(BF16)
    deltas = nt(sel, high) + nt(sel, low)
    for h in range(HEADS):
        delta_t[h] = deltas[h : h + 1]
    ranges = put_masks(meta, masks)
    lane = lax.broadcasted_iota(jnp.int32, (unit, LANES), 1)
    sub_lane = lax.broadcasted_iota(jnp.int32, (LANES, unit), 0)
    span = count * LANES

    def pair(step, carry):
        hp = first // 2 + step
        cols = pl.ds(pl.multiple_of(hp * LANES, LANES), LANES)
        here = pl.multiple_of(step * LANES, LANES)
        kt[...] = jnp.transpose(k[:, cols])
        gk[...] = jnp.zeros_like(gk)
        gv[...] = jnp.zeros_like(gv)
        gbase[...] = jnp.zeros_like(gbase)
        for sub in range(2):
            base[sub] = skewed(bias_rev[pl.ds(2 * hp + sub, 1), :], unit)
        for u in range(UNITS):
            ws = pl.multiple_of(ranges[u], LANES)
            win = pl.ds(ws, window)
            urows = slice(u * unit, (u + 1) * unit)
            mask = jnp.concatenate([masks[u], masks[u]], axis=1)
            kk = k[win, cols]
            vv = v[win, cols]
            qu = q[urows, cols]
            gu = gctx[urows, cols]
            offsets = [
                pl.ds(pl.multiple_of((rows - unit) + u * unit - ws - jb * unit, LANES), unit) for jb in range(UNITS - 1)
            ]
            qs = apart_heads(qu, lane, head)
            gs = apart_heads(gu, lane, head)
            rel = jnp.concatenate([jnp.concatenate([base[sub, :, o] for o in offsets], axis=0) for sub in range(2)], axis=1)
            lses = jnp.concatenate([lse[2 * hp + sub, :, urows] for sub in range(2)], axis=1)
            deltas = jnp.concatenate([delta_t[2 * hp + sub, :, urows] for sub in range(2)], axis=1)
            p = jnp.exp(nt(kk, qs) + rel + mask - lses)
            ds = (p * (nt(vv, gs) - deltas)).astype(BF16)
            gv[win, :] += nn(p.astype(BF16), gs)
            gk[win, :] += nn(ds, qs)
            gq = nn(kt[:, win], ds)
            d32 = ds.astype(F32)
            for sub in range(2):
                for jb, o in enumerate(offsets):
                    gbase[sub, :, o] += d32[jb * unit : (jb + 1) * unit, sub * unit : (sub + 1) * unit]
            gq_t = jnp.where(sub_lane < head, gq[:, :unit], gq[:, unit:])
            dqkv[urows, pl.ds(here, LANES)] = jnp.transpose(gq_t).astype(BF16) * BF16(head**-0.5)
        dqkv[:, pl.ds(span + here, LANES)] = gk[...].astype(BF16)
        dqkv[:, pl.ds(2 * span + here, LANES)] = gv[...].astype(BF16)
        for sub in range(2):
            grow_out[pl.ds(2 * step + sub, 1), :] = unskewed_sum(gbase[sub], unit)
        return carry

    grow_out[...] = jnp.zeros_like(grow_out)
    lax.fori_loop(0, count, pair, 0)
    at_columns = first * head
    grad_in = gin[...] if first else jnp.zeros((rows, width), F32)
    for part in range(3):
        d = dqkv[:, part * span : (part + 1) * span]
        grad_in = grad_in + nt(d, weight(w, slice(part * width + at_columns, part * width + at_columns + span)))
    grads = [(tn(nin[...], dqkv[...]), slice(0, 3 * span))]
    if first == 0:
        grads.append((tn(ctx[...], gatt[...].astype(BF16)), slice(3 * span, 3 * span + width)))
    for g, columns in grads:
        if crossed:
            put_blocks(core, place, row_blocks(g, rows_d), send, keep, columns)
        else:
            keep[:, columns] = g.astype(BF16)
    sums = [jnp.sum(dqkv[:, at : at + span].astype(F32), axis=0, keepdims=True) for at in (0, 2 * span)]
    gvec_out[...] = jnp.zeros_like(gvec_out)
    gvec_out[2:4, 0:span] = jnp.concatenate(sums, axis=0)
    if not last:
        gin_out[...] = grad_in
        return
    n, r = normalise(frames[...].astype(F32))
    gin_out[...] = (gatt[...] + norm_backward(n, r, vec[0:1, :], grad_in)).astype(BF16)
    gvec_out[0:1, :] = jnp.sum(grad_in * n, axis=0, keepdims=True)
    gvec_out[1:2, :] = jnp.sum(grad_in, axis=0, keepdims=True)
    if crossed:
        at = 0
        for vectors, _, c in before:
            gvec_out[2:4, at : at + c * LANES] = vectors[2:4, 0 : c * LANES]
            at += c * LANES
        gvec_out[2:4, at_columns : at_columns + span] = jnp.concatenate(sums, axis=0)
        gvec_out[4:8, :] = gvec2[0:4, :]
        grows = jnp.concatenate([grow[0 : 2 * c, :] for _, grow, c in before] + [grow_out[0 : 2 * count, :]], axis=0)
        small_blocks(
            core, place, gvec_out[...], jnp.broadcast_to(gb_inner[...], (8, gb_inner.shape[1])), grows, bucket_rev,
            send, keep, slice(3 * span, 3 * span + LANES), rows_d, gb_inner.shape[1] // len(place),
        )


def run_kernel(order, kernel, name, scalars, arrays, outs, scratch=(), spare=10, us=100, pin_in=True, pin_out=True, hbm_in=(), hbm_out=()):
    spec = pl.BlockSpec(memory_space=pltpu.VMEM)
    smem = pl.BlockSpec(memory_space=pltpu.SMEM)
    arrays = order.after(*arrays)
    arrays = [
        pltpu.with_memory_space_constraint(a, pltpu.VMEM if pin_in and i not in hbm_in else pltpu.HBM)
        for i, a in enumerate(arrays)
    ]
    limit = spare * MIB + sum(math.prod(b.shape) * jnp.dtype(b.dtype).itemsize for b in scratch)
    out = pl.pallas_call(
        kernel,
        in_specs=[smem] * len(scalars) + [spec] * len(arrays),
        out_specs=[spec] * len(outs),
        out_shape=[
            (pltpu.VMEM if pin_out and i not in hbm_out else jax.ShapeDtypeStruct)(s, d) for i, (s, d) in enumerate(outs)
        ],
        scratch_shapes=list(scratch),
        compiler_params=pltpu.CompilerParams(vmem_limit_bytes=limit),
        cost_estimate=pl.CostEstimate(flops=us * 1_000_000_000, bytes_accessed=us * 1_000_000, transcendentals=0),
        name=name,
    )(*scalars, *arrays)
    order.did(out[0])
    return out


def on_device(
    frames, ln1_gain, ln1_shift, w_query, b_query, w_key, w_value, b_value, w_out, b_out, ln2_gain, ln2_shift,
    w_inner, b_inner, w_outer, b_outer, bias_table, layout, valid, rel_index, cotangent, *, n,
):
    rows, width = frames.shape
    rows_d = w_query.shape[0]
    rows_ff = w_outer.shape[0]
    ff = w_inner.shape[1]
    span = rel_index.shape[0] + 1
    unit = rows // UNITS
    per_table = bias_table.shape[0]
    plan = plan_tables(n)
    core, chips, place = plan
    order = Order()
    direct = (
        rows_d % 8 == 0 and rows_d >= 24 and rows_ff == 4 * rows_d and max(rows_d, rows_ff, per_table) <= LANES and per_table % HEADS == 0
    )
    crossed = tuple(crossed_places(n)) if direct else ()
    crossed_outer = tuple(crossed_places(n, "outer")) if direct else ()
    unit_half = rows_ff // 2
    apart = [(d * rows_ff + h * unit_half, h * ff // 2 + d * unit_half, unit_half) for h in range(2) for d in range(n)]
    together = [(b, a, c) for a, b, c in apart]
    meta = [layout, valid.reshape(-1), core[None]]
    if direct:
        _, chips_outer, place_outer = plan_tables(n, "outer")
        meta += [chips, chips_outer, place, place_outer]
    meta = jnp.concatenate(meta).astype(jnp.int32)
    small_d = jnp.stack([ln1_gain, ln1_shift, b_query, b_value, b_out, ln2_gain, ln2_shift, b_outer])

    base = pltpu.VMEM((2, unit, span), F32)
    masks = pltpu.VMEM((UNITS, rows - unit, unit), F32)
    if direct:
        vectors = (ln1_gain, ln1_shift, b_query, b_value, b_out, ln2_gain, ln2_shift, b_outer, b_inner, bias_table)
        (part1,) = run_kernel(
            Order(), functools.partial(pack_first_kernel, rows_ff=rows_ff), "pack_first", [],
            [w_query, w_key, w_value, *(v[None] for v in vectors)], [((1, rows_d, 3 * width + LANES), BF16)],
            [pltpu.VMEM((rows_d, LANES), F32)], spare=4, pin_in=False,
        )
        g1 = Gather(part1, n, order)
        part2, part3 = run_kernel(
            order, functools.partial(pack_feed_kernel, moves=apart), "pack_feed", [], [w_inner, w_outer, w_out],
            [((1, rows_d, ff + width), BF16), ((1, rows_d, ff), BF16)], spare=4, pin_in=False,
        )
        g3 = Gather(part3, n, order, "outer")
        (part2,) = lax.optimization_barrier((part2, g1.got))[:1]
        g2 = Gather(part2, n, order)
        (g2.got,) = lax.optimization_barrier((g2.got, g3.got))[:1]
        for g in (g1, g1, g2, g1, g2, g3):
            g.step()
        (g2.got,) = lax.optimization_barrier((g2.got, g1.got))[:1]
        for g in (g2, g3):
            g.step()
        first = g1.finish()
        each = per_table // HEADS
        index = jnp.stack([rel_index // each, rel_index % each])
        bucket_rev = jnp.pad(index[:, ::-1], ((0, 6), (0, 1)), constant_values=-1)
        q, k, v, nin, w1, vec, inner_bias, bias_rev = run_kernel(
            order, functools.partial(project_kernel, crossed=crossed, rows_d=rows_d, rows_ff=rows_ff), "project", [meta],
            [frames, *first, bucket_rev],
            [((rows, width), BF16)] * 4
            + [((n // 2, 2 * rows_d, 3 * width), BF16), ((8, width), F32), ((1, ff), F32), ((16, span), F32)],
            [
                pltpu.VMEM((width // LANES + 1, 8, LANES), F32),
                pltpu.VMEM((ff // LANES + 1, 8, LANES), F32),
                pltpu.VMEM((n, LANES), F32),
            ],
            us=1, hbm_in=(0,),
        )
        chunk = [[((n // 2, rows_d, c), BF16)] * 2 for c in (ff, ff)]
        w_out_whole = [((n // 2, 2 * rows_d, width), BF16)]
        unpacked = [pltpu.VMEM((n // 2, 2 * rows_d, width), BF16), pltpu.VMEM((n // 2, rows_ff, width), BF16)]
    else:
        flat = jnp.concatenate([small_d.reshape(-1), b_inner, bias_table])
        per = flat.shape[0] // rows_d
        small = jnp.pad(flat.reshape(rows_d, per), ((0, 0), (0, LANES - per)))
        w1 = gathered(Gather(jnp.concatenate([w_query, w_key, w_value, small], axis=1), n, order).finish(), plan, n)
        w2 = (gathered(Gather(jnp.concatenate([w_inner, w_out], axis=1), n, order).finish(), plan, n),)
        w2 += (gathered(Gather(w_outer, n, order).finish(), plan, n),)
        flats = w1[:, 3 * width : 3 * width + per].reshape(n, rows_d * per)
        vec = flats[:, : 8 * rows_d].reshape(n, 8, rows_d).transpose(1, 0, 2).reshape(8, width).astype(F32)
        inner_bias = flats[:, 8 * rows_d : 8 * rows_d + rows_ff].reshape(1, ff).astype(F32)
        table = jnp.pad(flats[:, 8 * rows_d + rows_ff :].reshape(-1, HEADS), ((0, 0), (0, 16 - HEADS)))
        index_rev = jnp.pad(rel_index[::-1], (0, 1), constant_values=-1)
        ids = jnp.arange(table.shape[0], dtype=jnp.int32)[:, None]
        bias_rev = tn(table, (ids == index_rev[None]).astype(BF16))
        q, k, v, nin = run_kernel(
            order, project_body, "project", [meta], [frames, w1, vec], [((rows, width), BF16)] * 4
        )
        chunk = [[((8, LANES), BF16), ((c, max(width, ff // 2), max(width, ff // 2)), BF16)] for c in (2, 2)]
        w_out_whole = []
        unpacked = []

    ctx, lse = run_kernel(
        order, attend_kernel, "attend", [meta], [q, k, v, bias_rev],
        [((rows, width), BF16), ((HEADS, 1, rows), F32)], [base, pltpu.VMEM((LANES, rows), BF16), masks], spare=4, us=1,
    )

    def start(send, keep, scatter):
        return scatter.add(*((send, keep) if direct else split_natural(keep, plan, n)))

    if direct:
        g3.step()
        w2 = g2.finish()
    att, nmid, acc, gmid, gb1, send1, keep1, *w_out_all = run_kernel(
        order, functools.partial(feed_first_kernel, crossed=crossed, rows_d=rows_d), "feed_first", [meta],
        [frames, ctx, vec, inner_bias, cotangent, *w2],
        [((rows, width), F32), ((rows, width), BF16), ((rows, width), F32), ((rows, width), F32), ((1, ff // 2), F32)]
        + chunk[0] + w_out_whole,
        unpacked, spare=12,
    )
    if direct:
        w3 = g3.finish()
        begin = functools.partial(Scatter, n, order)
        sum_1 = begin("outer").add(send1, keep1)
    else:
        w3 = w2
    mixed, gatt, gctx, send2, keep2, gb2, gvec2 = run_kernel(
        order, functools.partial(feed_second_kernel, crossed=crossed_outer, rows_d=rows_d), "feed_second", [meta],
        [att, nmid, acc, gmid, ctx, vec, inner_bias, cotangent, *w_out_all, *w3],
        [((rows, width), BF16), ((rows, width), F32), ((rows, width), BF16)] + chunk[1]
        + [((1, ff // 2), F32), ((8, width), F32)],
        [pltpu.VMEM((rows, width), F32)] * 2 + unpacked, spare=12, hbm_out=(0,),
    )
    gb_inner = jnp.concatenate([gb1, gb2], axis=1)
    if direct:
        sum_1.step(2)
        sum_2 = begin().add(send2, keep2)
    else:
        whole_inner = jnp.concatenate([keep1[0, :width, : ff // 2], keep2[0, :width, : ff // 2]], axis=1)
        whole_outer = jnp.concatenate([keep1[1, : ff // 2, :width], keep2[1, : ff // 2, :width]], axis=0)
        begin = functools.partial(Scatter, n, order)
        sum_1 = begin().add(*split_natural(whole_outer, plan, n))
        sum_2 = begin().add(*split_natural(whole_inner, plan, n))

    counts = COUNTS
    passed = gatt
    done, earlier = [], []
    sum_early, sum_late = begin(), begin()
    for call, count in enumerate(counts):
        cols = count * LANES
        last = call == len(counts) - 1
        wide = 3 * cols + LANES * (last and direct) + width * (call == 0)
        part = [((n // 2, rows_d, wide), BF16)] * 2 if direct else [((8, LANES), BF16), ((width, wide), BF16)]
        extra = [gvec2, gb_inner, bucket_rev] + [a for pair in earlier for a in pair] if last and direct else []
        send, keep, passed, gvec1, grow = run_kernel(
            order,
            functools.partial(
                attend_back_kernel, crossed=crossed, rows_d=rows_d, counts=counts[:call], count=count
            ),
            "attend_back", [meta],
            [q, k, v, lse, ctx, gctx, bias_rev, nin, frames, gatt, passed, w1, vec] + extra,
            part + [((rows, width), BF16 if last else F32), ((8, width), F32), ((8, span), F32)],
            [
                base, base,
                pltpu.VMEM((HEADS, 1, rows), F32),
                pltpu.VMEM((LANES, rows), BF16),
                pltpu.VMEM((rows, 3 * cols), BF16),
                pltpu.VMEM((rows, LANES), F32),
                pltpu.VMEM((rows, LANES), F32),
                masks,
            ],
            spare=10, hbm_out=(2,) if last else (),
        )
        earlier.append((gvec1, grow))
        start(send, keep, sum_late if call else sum_early)
        if call == 0:
            sum_1.step(2)
            sum_2.step()
    for each_sum in (sum_early, sum_1, sum_2, sum_late, sum_early, sum_1, sum_2, sum_late, sum_early, sum_2, sum_late, sum_early, sum_late):
        if each_sum.steps:
            each_sum.step()
    sum_1, sum_2, early, late = sum_1.finish(), sum_2.finish(), sum_early.finish(), sum_late.finish()
    if direct:
        grad_inner, grad_outer, grad_w_out = run_kernel(
            Order(), functools.partial(feed_columns_kernel, moves=together), "feed_columns", [], [sum_1, sum_2, early],
            [((rows_d, ff), F32), ((rows_ff, width), F32), ((rows_d, width), F32)], spare=4, pin_out=False,
        )
    else:
        grad_inner, grad_outer = sum_2[:, :ff], sum_1
        grad_w_out = early[:, 3 * LANES * counts[0] :]
    if direct:
        sum_q, sum_k, sum_v, sum_b_inner, sum_table, *vecs = run_kernel(
            Order(), functools.partial(columns_kernel, counts=counts), "columns", [], [early, late],
            [((rows_d, width), F32)] * 3 + [((rows_ff,), F32), ((per_table,), F32)] + [((rows_d,), F32)] * 8,
            spare=4, pin_out=False,
        )
    else:
        places = [3 * LANES * sum(counts[1:call]) for call in range(len(counts))]
        calls = list(zip([early] + [late] * len(counts[1:]), places, [c * LANES for c in counts]))
        sum_q, sum_k, sum_v = (
            jnp.concatenate([p[:, at + i * cols : at + (i + 1) * cols] for p, at, cols in calls], axis=1) for i in range(3)
        )
        hot_rev = (ids == index_rev[None]).astype(F32)
        grow = jnp.concatenate([g[: 2 * c] for (_, g), c in zip(earlier, counts)])
        gtable = lax.dot_general(
            hot_rev, grow, (((1,), (1,)), ((), ())), precision=lax.Precision.HIGHEST, preferred_element_type=F32
        )
        gbias = jnp.concatenate([g[2:4, : c * LANES] for (g, _), c in zip(earlier, counts)], axis=1)
        gsmall = jnp.concatenate([gvec1[0:2], gbias, gvec2[0:4]])
        gsmall = gsmall.reshape(8, n, rows_d).transpose(1, 0, 2).reshape(n, 8 * rows_d)
        gflat = jnp.concatenate([gsmall, gb_inner.reshape(n, rows_ff), gtable.reshape(n, -1)], axis=1)
        gflat = jnp.pad(gflat, ((0, 0), (0, -gflat.shape[1] % LANES))).astype(BF16)
        sum_flat = Scatter(n, order).add(*split_natural(gflat, plan, n)).finish()[0]
        vecs = sum_flat[: 8 * rows_d].reshape(8, rows_d)
        sum_b_inner = sum_flat[8 * rows_d : 8 * rows_d + rows_ff]
        sum_table = sum_flat[8 * rows_d + rows_ff : 8 * rows_d + rows_ff + per_table]
    return (
        mixed, passed, vecs[0], vecs[1], sum_q, vecs[2], sum_k, sum_v, vecs[3],
        grad_w_out, vecs[4], vecs[5], vecs[6], grad_inner, sum_b_inner, grad_outer, vecs[7], sum_table,
    )


def solution(mesh):
    row, two = P("dp"), P("dp", None)
    in_specs = (two, row, row, two, row, two, two, row, two, row, row, row, two, row, two, row, row, row, two, P(), two)
    out_specs = (two, two, row, row, two, row, two, two, row, two, row, row, row, two, row, two, row, row)
    return jax.shard_map(
        functools.partial(on_device, n=mesh.shape["dp"]),
        mesh=mesh, in_specs=in_specs, out_specs=out_specs, check_vma=False,
    )
```

```python
import functools
import math

import jax
import jax.numpy as jnp
import numpy as np
from jax import lax
from jax.experimental import pallas as pl
from jax.experimental.pallas import tpu as pltpu
from jax.sharding import PartitionSpec as P

HEADS = 12
LANES = 128
UNITS = 4
MASKED = -1e30
F32 = jnp.float32
BF16 = jnp.bfloat16
SEGMENT = ((0, 0, 0, 1), (0, 0, 1, 1), (0, 0, 1, 2), (0, 1, 2, 3))
START = ((0, 0, 0, 3), (0, 0, 2, 2), (0, 0, 2, 3), (0, 1, 2, 3))
MIB = 1024 * 1024
COUNTS = (3, 3)


def bit_orders(n, kind):
    chip = [1 << k for k in range(1, n.bit_length() - 1)]
    low, high = chip[:2], chip[2:][::-1]
    if kind == "outer":
        return (low[:1] + high + low[1:], low[1:] + high + low[:1])
    return (high + low, high + low[::-1])


def gather_masks(bits):
    masks = [0]
    for bit in bits:
        masks = masks + [bit ^ m for m in masks]
    return masks


def scatter_masks(bits):
    masks = [0]
    for bit in bits:
        masks = [bit ^ m for m in masks] + masks
    return masks


def pairs(n, by_core):
    return [(i, i ^ by_core[i & 1]) for i in range(n)]


class Order:
    def __init__(self):
        self.last = None

    def after(self, *arrays):
        if self.last is None:
            return arrays
        return lax.optimization_barrier((*arrays, self.last))[:-1]

    def did(self, array):
        self.last = array


class Gather:
    def __init__(self, part, n, order, kind="inner"):
        self.n = n
        self.order = order
        self.steps = list(zip(*bit_orders(n, kind)))
        self.held = part if part.ndim == 3 else part[None]
        self.got = lax.ppermute(self.held, "dp", pairs(n, self.steps.pop(0)))

    def step(self):
        pair = self.order.after(self.held, self.got)
        self.held = jnp.concatenate(pair, axis=0)
        self.order.did(self.held)
        self.got = lax.ppermute(self.held, "dp", pairs(self.n, self.steps.pop(0)))
        return self

    def finish(self):
        while self.steps:
            self.step()
        (self.got,) = self.order.after(self.got)
        swap = pairs(self.n, (1, 1))
        return (self.held, self.got, lax.ppermute(self.held, "dp", swap), lax.ppermute(self.got, "dp", swap))


class Scatter:
    def __init__(self, n, order, kind="inner"):
        self.n = n
        self.order = order
        self.parts = []
        self.terms = []
        self.at = 0
        self.steps = list(reversed(list(zip(*bit_orders(n, kind)))))
        self.half = n // 4

    def add(self, send, keep):
        self.parts.append((keep, lax.ppermute(send, "dp", pairs(self.n, (1, 1)))))
        return self

    def total(self, count, dtype):
        at = self.at
        held = [(t, first) for t, first in self.terms if first <= at and at + count <= first + t.shape[0]]
        flat = [t for part in self.parts for t in part] + [t for t, _ in held]
        flat = list(self.order.after(*flat))
        cut = [lax.slice_in_dim(t, at, at + count).astype(F32) for t in flat[: 2 * len(self.parts)]]
        out = [cut[2 * i] + cut[2 * i + 1] for i in range(len(self.parts))]
        out = out[0] if len(out) == 1 else jnp.concatenate(out, axis=-1)
        for t, (_, first) in zip(flat[2 * len(self.parts) :], held):
            out = out + lax.slice_in_dim(t, at - first, at - first + count).astype(F32)
        out = out.astype(dtype)
        self.order.did(out)
        return out

    def step(self, transfers=1):
        by_core = self.steps.pop(0)
        count = self.half // transfers
        for _ in range(transfers):
            out = self.total(count, BF16)
            self.terms.append((lax.ppermute(out, "dp", pairs(self.n, by_core)), self.at + self.half))
            self.at += count
        self.half //= 2

    def finish(self):
        while self.steps:
            self.step()
        return self.total(1, F32)[0]


def plan_tables(n, kind="inner"):
    orders = bit_orders(n, kind)
    me = lax.axis_index("dp")
    core = me & 1
    g = np.array([gather_masks(o) for o in orders], np.int32)
    s = np.array([scatter_masks(o) for o in orders], np.int32)
    inverse = np.zeros((2, n), np.int32)
    for c in (0, 1):
        for i, m in enumerate(s[c]):
            inverse[c, m] = i
    devices = jnp.arange(n, dtype=jnp.int32)
    chips = (me ^ jnp.where(core == 0, jnp.asarray(g[0]), jnp.asarray(g[1]))) >> 1
    mask = (devices ^ me) & ~1
    place = jnp.sum(jnp.where(mask[:, None] == devices[None, :], jnp.asarray(inverse)[np.arange(n) % 2], 0), axis=1)
    return core, chips, place


def crossed_places(n, kind="inner"):
    first, second = (gather_masks(o) for o in bit_orders(n, kind))
    places = [second.index(m) for m in first]
    assert places == [first.index(m) for m in second]
    return places


def gathered(parts, plan, n):
    core, chips, _ = plan
    mine = jnp.concatenate(parts[:2])
    theirs = jnp.concatenate(parts[2:])[np.array(crossed_places(n))]
    both = jnp.where(core == 0, jnp.stack([mine, theirs], 1), jnp.stack([theirs, mine], 1))
    return both[jnp.argsort(chips)].reshape(n * mine.shape[1], mine.shape[2])


def split_natural(grad, plan, n):
    core, _, place = plan
    rows = grad.shape[0] // n
    blocks = grad.reshape(n // 2, 2, rows, grad.shape[1])
    mine = jnp.where(core == 0, blocks[:, 0], blocks[:, 1])
    theirs = jnp.where(core == 0, blocks[:, 1], blocks[:, 0])
    both = place.reshape(n // 2, 2)
    my_place = jnp.where(core == 0, both[:, 0], both[:, 1])
    their_place = jnp.where(core == 0, both[:, 1], both[:, 0])
    return theirs[jnp.argsort(their_place)], mine[jnp.argsort(my_place)]


def nn(a, b):
    return jnp.dot(a, b, preferred_element_type=F32)


def nt(a, b):
    return lax.dot_general(a, b, (((1,), (1,)), ((), ())), preferred_element_type=F32)


def tn(a, b):
    return lax.dot_general(a, b, (((0,), (0,)), ((), ())), preferred_element_type=F32)


def normalise(v):
    centred = v - jnp.mean(v, axis=-1, keepdims=True)
    r = lax.rsqrt(jnp.mean(centred * centred, axis=-1, keepdims=True) + 1e-05)
    return centred * r, r


def norm_backward(n, r, gain, e):
    eg = e * gain
    return r * (eg - jnp.mean(eg, axis=-1, keepdims=True) - n * jnp.mean(eg * n, axis=-1, keepdims=True))


def pick(table, code, u):
    out = jnp.int32(table[0][u])
    for c in range(1, 4):
        out = jnp.where(code == c, jnp.int32(table[c][u]), out)
    return out


def unit_range(meta, u, unit):
    code = meta[0]
    segment = pick(SEGMENT, code, u)
    start = pick(START, code, u)
    count = meta[1]
    for s in range(1, 4):
        count = jnp.where(segment == s, meta[1 + s], count)
    window = jnp.minimum(start, 1) * unit
    return start * unit, start * unit + count, window


def put_masks(meta, masks):
    units, window, unit = masks.shape
    row_at = lax.broadcasted_iota(jnp.int32, (window, unit), 0)
    starts = []
    for u in range(units):
        first, end, start = unit_range(meta, u, unit)
        masks[u] = jnp.where((row_at + start >= first) & (row_at + start < end), 0.0, MASKED)
        starts.append(start)
    return starts


def skewed(row, unit):
    wide = jnp.broadcast_to(row, (unit, row.shape[1]))
    return pltpu.roll(wide, row.shape[1] - (unit - 1), 1, stride=1, stride_axis=0)


def unskewed_sum(block, unit):
    width = block.shape[1]
    total = None
    for a in range(unit // 8):
        part = block[8 * a : 8 * a + 8]
        shift = (unit - 1 - 8 * a) % width
        part = pltpu.roll(part, shift, 1) if shift else part
        total = part if total is None else total + part
    out = total[0:1]
    for s in range(1, 8):
        out = out + pltpu.roll(total[s : s + 1], width - s, 1)
    return out


def unpack(core, chips, parts, crossed, out, columns):
    half = parts[0].shape[0]
    for i, j in enumerate(crossed):
        mine = parts[i // half][i % half, :, columns]
        theirs = parts[2 + j // half][j % half, :, columns]
        first = jnp.where(core == 0, mine, theirs)
        second = jnp.where(core == 0, theirs, mine)
        out[chips[i]] = jnp.concatenate([first, second], axis=0)


def weight(ref, columns):
    value = ref[..., columns]
    return value.reshape(-1, value.shape[-1])


def put_blocks(core, places, blocks, send, keep, columns):
    for plane in range(2):

        @pl.when(core == plane)
        def _(plane=plane):
            for at, (place, block) in enumerate(zip(places, blocks)):
                (keep if at % 2 == plane else send)[place, :, columns] = block.astype(BF16)


def row_blocks(value, rows):
    return [value[at : at + rows] for at in range(0, value.shape[0], rows)]


def project_body(meta, frames, w, vec, q_out, k_out, v_out, nin_out):
    width = frames.shape[1]
    head = width // HEADS
    n, _ = normalise(frames[...].astype(F32))
    nin = (n * vec[0:1, :] + vec[1:2, :]).astype(BF16)
    nin_out[...] = nin
    q_out[...] = ((nn(nin, weight(w, slice(0, width))) + vec[2:3, :]) * (head**-0.5)).astype(BF16)
    k_out[...] = nn(nin, weight(w, slice(width, 2 * width))).astype(BF16)
    v_out[...] = (nn(nin, weight(w, slice(2 * width, 3 * width))) + vec[3:4, :]).astype(BF16)


def apart_heads(rows, lane, head):
    zero = jnp.zeros_like(rows)
    return jnp.concatenate([jnp.where(lane < head, rows, zero), jnp.where(lane < head, zero, rows)], axis=0)


def attend_kernel(meta, q, k, v, bias_rev, ctx_out, lse_out, base, vt, masks):
    rows, width = q.shape
    unit = rows // UNITS
    window = rows - unit
    head = width // HEADS
    ranges = put_masks(meta, masks)
    lane = lax.broadcasted_iota(jnp.int32, (unit, LANES), 1)
    sub_lane = lax.broadcasted_iota(jnp.int32, (LANES, unit), 0)

    def pair(hp, carry):
        cols = pl.ds(pl.multiple_of(hp * LANES, LANES), LANES)
        vt[...] = jnp.transpose(v[:, cols])
        for sub in range(2):
            base[sub] = skewed(bias_rev[pl.ds(2 * hp + sub, 1), :], unit)
        for u in range(UNITS):
            ws = pl.multiple_of(ranges[u], LANES)
            win = pl.ds(ws, window)
            urows = slice(u * unit, (u + 1) * unit)
            kk = k[win, cols]
            qu = q[urows, cols]
            offsets = [
                pl.ds(pl.multiple_of((rows - unit) + u * unit - ws - jb * unit, LANES), unit) for jb in range(UNITS - 1)
            ]
            parts = []
            for sub in range(2):
                qs = jnp.where((lane >= head) == bool(sub), qu, jnp.zeros_like(qu))
                rel = jnp.concatenate([base[sub, :, o] for o in offsets], axis=0)
                s = nt(kk, qs) + rel + masks[u]
                top = jnp.max(s, axis=0, keepdims=True)
                e = jnp.exp(s - top)
                tot = jnp.sum(e, axis=0, keepdims=True)
                parts.append(nn(vt[:, win], e.astype(BF16)) * (1.0 / tot))
                lse_out[2 * hp + sub, :, urows] = top + jnp.log(tot)
            ctx_out[urows, cols] = jnp.transpose(jnp.where(sub_lane < head, parts[0], parts[1])).astype(BF16)
        return carry

    lax.fori_loop(0, HEADS // 2, pair, 0)


def small_vectors(core, chips, parts, crossed, at, rows_d, rows_ff, vec3, inner3, table):
    half = parts[0].shape[0]
    lane = lax.broadcasted_iota(jnp.int32, (8, LANES), 1)
    vec3[...] = jnp.zeros_like(vec3)
    inner3[...] = jnp.zeros_like(inner3)
    for i, j in enumerate(crossed):
        mine = parts[i // half][i % half, :, at : at + LANES].astype(F32)
        theirs = parts[2 + j // half][j % half, :, at : at + LANES].astype(F32)
        for plane in range(2):
            block = jnp.where(core == plane, mine, theirs)
            d = 2 * chips[i] + plane
            unit_half = rows_ff // 2
            half_at = 2 * half * rows_ff
            for first, rows, part, out in (
                (0, rows_d, block[0:8], vec3),
                (0, unit_half, block[8:16], inner3),
                (half_at, unit_half, block[16:24], inner3),
            ):
                start = first + d * rows
                tile = start >> 7
                shift = start & (LANES - 1)
                rolled = pltpu.roll(part, shift, 1)
                out[tile] += jnp.where(lane >= shift, rolled, 0.0)
                out[tile + 1] += jnp.where(lane < shift, rolled, 0.0)
            table[pl.ds(d, 1), :] = block[9:10]


def relative_rows(bucket, table, out):
    devices = lax.broadcasted_iota(jnp.int32, (table.shape[0], bucket.shape[1]), 0)
    hot = jnp.where(devices == bucket[0:1, :], 1.0, 0.0).astype(BF16)
    rows = tn(table[...].astype(BF16), hot)
    total = jnp.zeros((HEADS, bucket.shape[1]), F32)
    for m in range(LANES // HEADS):
        total = total + jnp.where(bucket[1:2, :] == m, rows[m * HEADS : (m + 1) * HEADS], 0.0)
    out[0:HEADS, :] = total
    out[HEADS:, :] = jnp.zeros_like(out[HEADS:, :])


def project_kernel(
    meta, frames, p0, p1, p2, p3, bucket_rev,
    q_out, k_out, v_out, nin_out, w, vec, b_inner, bias_rev,
    vec3, inner3, table, *, crossed, rows_d, rows_ff,
):
    width = frames.shape[1]
    core = meta[5]
    chips = [meta[6 + i] for i in range(len(crossed))]
    parts = (p0, p1, p2, p3)
    small_vectors(core, chips, parts, crossed, 3 * width, rows_d, rows_ff, vec3, inner3, table)
    for a in range(width // LANES):
        vec[:, a * LANES : (a + 1) * LANES] = vec3[a]
    for a in range(b_inner.shape[1] // LANES):
        b_inner[:, a * LANES : (a + 1) * LANES] = inner3[a, 0:1]
    relative_rows(bucket_rev, table, bias_rev)
    unpack(core, chips, parts, crossed, w, slice(0, 3 * width))
    project_body(meta, frames, w, vec, q_out, k_out, v_out, nin_out)


def unpack_folded(core, chips, parts, crossed, out, at, width):
    half = parts[0].shape[0]
    for i, j in enumerate(crossed):
        mine = parts[i // half][i % half, :, at : at + 2 * width]
        theirs = parts[2 + j // half][j % half, :, at : at + 2 * width]
        first = jnp.where(core == 0, mine, theirs)
        second = jnp.where(core == 0, theirs, mine)
        rows = [first[:, :width], first[:, width:], second[:, :width], second[:, width:]]
        out[chips[i]] = jnp.concatenate(rows, axis=0)


def feed_tiles(meta, kind, crossed, parts, natural, b_inner, cot, first, nmid, acc, gmid, gb_out, send, keep, w_tile, w_rows, rows_d):
    width = nmid.shape[1]
    tiles = b_inner.shape[1] // width // 2
    if crossed:
        half = len(crossed)
        core = meta[5]
        chips_at = 6 + half * (kind == "outer")
        chips = [meta[chips_at + i] for i in range(half)]
        place_at = 6 + 2 * half + 2 * half * (first == 0)
        place = [meta[place_at + i] for i in range(2 * half)]
        unpack_folded(core, chips, parts, crossed, w_rows, tiles * width, width)
        w_outer = w_rows.reshape(tiles * width, width)
    else:
        w, w_outer = natural

    def tile(t, carry):
        here = pl.multiple_of(t * width, LANES)
        cols = pl.ds(here, width)
        all_cols = pl.ds(pl.multiple_of(first + here, LANES), width)
        if crossed:
            unpack(core, chips, parts, crossed, w_tile, cols)
            wi = weight(w_tile, slice(None))
            wo = w_outer[cols, :]
        else:
            wi = w[:, all_cols]
            wo = w_outer[all_cols, :]
        v = nn(nmid[...], wi) + b_inner[:, all_cols]
        phi = 0.5 * (1.0 + lax.erf(v * (0.5**0.5)))
        act = (v * phi).astype(BF16)
        slope = phi + v * jnp.exp(-0.5 * v * v) * 0.3989422804014327
        acc[...] += nn(act, wo)
        gi = (slope * nt(cot[...], wo)).astype(BF16)
        gb_out[:, cols] = jnp.sum(gi.astype(F32), axis=0, keepdims=True)
        gmid[...] += nt(gi, wi)
        g_outer = tn(act, cot[...])
        g_inner = tn(nmid[...], gi)
        if crossed:
            put_blocks(core, place, row_blocks(g_inner, rows_d), send, keep, cols)
            per = width // (2 * rows_d)
            places = [meta[place_at + t * per + at] for at in range(per)]
            rows = row_blocks(g_outer, rows_d)
            blocks = [jnp.concatenate(rows[2 * at : 2 * at + 2], axis=1) for at in range(per)]
            put_blocks(core, places, blocks, send, keep, slice(tiles * width, (tiles + 2) * width))
        else:
            keep[0, :width, cols] = g_inner.astype(BF16)
            keep[1, cols, :width] = g_outer.astype(BF16)
        return carry

    lax.fori_loop(0, tiles, tile, 0)


def feed_first_kernel(meta, frames, ctx, vec, b_inner, cot, *refs, crossed, rows_d):
    rows, width = frames.shape
    ff = b_inner.shape[1]
    if crossed:
        parts, refs = refs[:4], refs[4:]
        att, nmid, acc, gmid, gb_out, send, keep, w_out, w_tile, w_rows = refs
        chips = [meta[6 + i] for i in range(len(crossed))]
        unpack(meta[5], chips, parts, crossed, w_out, slice(ff, ff + width))
        wo, natural = weight(w_out, slice(None)), None
    else:
        w, w_outer, att, nmid, acc, gmid, gb_out, send, keep = refs
        parts, natural, w_tile, w_rows = None, (w, w_outer), None, None
        wo = w[:, ff : ff + width]
    attended = frames[...].astype(F32) + nn(ctx[...], wo) + vec[4:5, :]
    att[...] = attended
    n, _ = normalise(attended)
    nmid[...] = (n * vec[5:6, :] + vec[6:7, :]).astype(BF16)
    acc[...] = attended + vec[7:8, :]
    gmid[...] = jnp.zeros_like(gmid)
    feed_tiles(
        meta, "inner", crossed, parts, natural, b_inner, cot, 0, nmid, acc, gmid, gb_out, send, keep, w_tile, w_rows, rows_d
    )


def feed_second_kernel(meta, att, nmid, acc_in, gmid_in, ctx, vec, b_inner, cot, *refs, crossed, rows_d):
    rows, width = att.shape
    ff = b_inner.shape[1]
    if crossed:
        w_out, parts, refs = refs[0], refs[1:5], refs[5:]
        mixed_out, gatt_out, gctx_out, send, keep, gb_out, gvec_out, acc, gmid, w_tile, w_rows = refs
        wo, natural = weight(w_out, slice(None)), None
    else:
        w, w_outer, mixed_out, gatt_out, gctx_out, send, keep, gb_out, gvec_out, acc, gmid = refs
        parts, natural, w_tile, w_rows = None, (w, w_outer), None, None
        wo = w[:, ff : ff + width]
    acc[...] = acc_in[...]
    gmid[...] = gmid_in[...]
    feed_tiles(
        meta, "outer", crossed, parts, natural, b_inner, cot, ff // 2, nmid, acc, gmid, gb_out, send, keep, w_tile, w_rows, rows_d
    )
    mixed_out[...] = acc[...].astype(BF16)
    n, r = normalise(att[...])
    e = gmid[...]
    c32 = cot[...].astype(F32)
    gatt = c32 + norm_backward(n, r, vec[5:6, :], e)
    gatt_out[...] = gatt
    gbr = gatt.astype(BF16)
    gctx_out[...] = nt(gbr, wo).astype(BF16)
    gvec_out[0:1, :] = jnp.sum(gbr.astype(F32), axis=0, keepdims=True)
    gvec_out[1:2, :] = jnp.sum(e * n, axis=0, keepdims=True)
    gvec_out[2:3, :] = jnp.sum(e, axis=0, keepdims=True)
    gvec_out[3:4, :] = jnp.sum(c32, axis=0, keepdims=True)
    gvec_out[4:8, :] = jnp.zeros_like(gvec_out[4:8, :])


def moved_lanes(value, moves):
    lane = lax.broadcasted_iota(jnp.int32, (value.shape[0], LANES), 1)
    out = [None] * (value.shape[1] // LANES)
    for source, target, count in moves:
        while count:
            step = min(count, LANES - source % LANES, LANES - target % LANES)
            piece = value[:, source - source % LANES : source - source % LANES + LANES]
            shift = (target - source) % LANES
            piece = pltpu.roll(piece, shift, 1) if shift else piece
            at = target % LANES
            old = out[target // LANES]
            inside = (lane >= at) & (lane < at + step)
            out[target // LANES] = piece if old is None else jnp.where(inside, piece, old)
            source, target, count = source + step, target + step, count - step
    return jnp.concatenate(out, axis=1)


def pack_first_kernel(*refs, rows_ff):
    w_query, w_key, w_value, *vectors, b_inner, table, out, small = refs
    rows, width = w_query.shape
    for i, part in enumerate((w_query, w_key, w_value)):
        out[0, :, i * width : (i + 1) * width] = part[...]
    half = rows_ff // 2
    small[...] = jnp.zeros_like(small)
    for i, vector in enumerate(vectors):
        small[i : i + 1, 0:rows] = vector[...].astype(F32)
    small[8:9, 0:half] = b_inner[:, 0:half].astype(F32)
    small[9:10, 0 : table.shape[1]] = table[...].astype(F32)
    small[16:17, 0:half] = b_inner[:, half:].astype(F32)
    out[0, :, 3 * width :] = small[...].astype(BF16)


def pack_feed_kernel(w_inner, w_outer, w_out, second, third, *, moves):
    rows, width = w_out.shape
    half = w_inner.shape[1] // 2
    inner = moved_lanes(w_inner[...].astype(F32), moves).astype(BF16)
    for part, out in enumerate((second, third)):
        out[0, :, 0:half] = inner[:, part * half : (part + 1) * half]
        for i in range(2):
            at = (2 * part + i) * rows
            out[0, :, half + i * width : half + (i + 1) * width] = w_outer[at : at + rows, :]
    second[0, :, 2 * half :] = w_out[...]


def columns_kernel(early, late, q_out, k_out, v_out, inner_out, table_out, *vectors, counts):
    at = first = 0
    for call, count in enumerate(counts):
        cols = count * LANES
        for i, out in enumerate((q_out, k_out, v_out)):
            out[:, at : at + cols] = (late if call else early)[:, first + i * cols : first + (i + 1) * cols]
        at += cols
        first = first + 3 * cols if call else 0
    rows = vectors[0].shape[0]
    half = inner_out.shape[0] // 2
    for i, out in enumerate(vectors):
        out[...] = late[i, first : first + rows]
    inner_out[0:half] = late[8, first : first + half]
    inner_out[half:] = late[16, first : first + half]
    table_out[...] = late[9, first : first + table_out.shape[0]]


def feed_columns_kernel(first, second, early, inner_out, outer_out, w_out, *, moves):
    rows, width = w_out.shape
    half = inner_out.shape[1] // 2
    both = jnp.concatenate([first[:, 0:half], second[:, 0:half]], axis=1)
    inner_out[...] = moved_lanes(both, moves)
    for part, value in enumerate((first, second)):
        for i in range(2):
            at = (2 * part + i) * rows
            outer_out[at : at + rows, :] = value[:, half + i * width : half + (i + 1) * width]
    w_out[...] = early[:, early.shape[1] - width :]


def small_blocks(core, place, vecs, inner, grows, bucket_rev, send, keep, columns, rows_d, rows_ff):
    n = len(place)
    span = bucket_rev.shape[1]
    row = lax.broadcasted_iota(jnp.int32, (8, LANES), 0)
    lane = lax.broadcasted_iota(jnp.int32, (8, LANES), 1)
    each = LANES // HEADS
    big = [jnp.where(bucket_rev[1:2, :] == m, grows, 0.0) for m in range(each)]
    big = jnp.concatenate(big + [jnp.zeros((LANES - each * HEADS, span), F32)], axis=0)
    high = big.astype(BF16)
    low = (big - high.astype(F32)).astype(BF16)
    hot = jnp.where(lax.broadcasted_iota(jnp.int32, (n, span), 0) == bucket_rev[0:1, :], 1.0, 0.0).astype(BF16)
    table = nt(hot, high) + nt(hot, low)

    def cut(value, at, count):
        tile, shift = at // LANES, at % LANES
        out = value[:, tile * LANES : (tile + 1) * LANES]
        if shift:
            out = pltpu.roll(out, LANES - shift, 1)
            if shift + count > LANES:
                more = pltpu.roll(value[:, (tile + 1) * LANES : (tile + 2) * LANES], LANES - shift, 1)
                out = jnp.where(lane < LANES - shift, out, more)
        return jnp.where(lane < count, out, 0.0)

    half = rows_ff // 2
    blocks = []
    for d in range(n):
        low_rows = jnp.where(row == 0, cut(inner, d * half, half), 0.0)
        low_rows = jnp.where(row == 1, table[d : d + 1], low_rows)
        last_rows = jnp.where(row == 0, cut(inner, (n + d) * half, half), 0.0)
        block = [cut(vecs, d * rows_d, rows_d), low_rows, last_rows]
        block += [jnp.zeros((rows_d - 24, LANES), F32)] * (rows_d > 24)
        blocks.append(jnp.concatenate(block, axis=0))
    put_blocks(core, place, blocks, send, keep, columns)


def attend_back_kernel(
    meta, q, k, v, lse, ctx, gctx, bias_rev, nin, frames, gatt, gin, w, vec, *refs, crossed, rows_d, counts, count,
):
    first = 2 * sum(counts)
    last = first + 2 * count == HEADS
    if last and crossed:
        gvec2, gb_inner, bucket_rev, *refs = refs
        before = [(refs[2 * i], refs[2 * i + 1], c) for i, c in enumerate(counts)]
        refs = refs[2 * len(counts) :]
    send, keep, gin_out, gvec_out, grow_out, base, gbase, delta_t, kt, dqkv, gk, gv, masks = refs
    rows, width = frames.shape
    unit = rows // UNITS
    window = rows - unit
    head = width // HEADS
    core = meta[5]
    place = [meta[6 + 2 * len(crossed) + i] for i in range(2 * len(crossed))]
    prod = gctx[...].astype(F32) * ctx[...].astype(F32)
    sel_row = lax.broadcasted_iota(jnp.int32, (16, width), 0)
    sel_col = lax.broadcasted_iota(jnp.int32, (16, width), 1)
    sel = jnp.where((sel_col >= sel_row * head) & (sel_col < (sel_row + 1) * head), 1.0, 0.0).astype(BF16)
    high = prod.astype(BF16)
    low = (prod - high.astype(F32)).astype(BF16)
    deltas = nt(sel, high) + nt(sel, low)
    for h in range(HEADS):
        delta_t[h] = deltas[h : h + 1]
    ranges = put_masks(meta, masks)
    lane = lax.broadcasted_iota(jnp.int32, (unit, LANES), 1)
    sub_lane = lax.broadcasted_iota(jnp.int32, (LANES, unit), 0)
    span = count * LANES

    def pair(step, carry):
        hp = first // 2 + step
        cols = pl.ds(pl.multiple_of(hp * LANES, LANES), LANES)
        here = pl.multiple_of(step * LANES, LANES)
        kt[...] = jnp.transpose(k[:, cols])
        gk[...] = jnp.zeros_like(gk)
        gv[...] = jnp.zeros_like(gv)
        gbase[...] = jnp.zeros_like(gbase)
        for sub in range(2):
            base[sub] = skewed(bias_rev[pl.ds(2 * hp + sub, 1), :], unit)
        for u in range(UNITS):
            ws = pl.multiple_of(ranges[u], LANES)
            win = pl.ds(ws, window)
            urows = slice(u * unit, (u + 1) * unit)
            mask = jnp.concatenate([masks[u], masks[u]], axis=1)
            kk = k[win, cols]
            vv = v[win, cols]
            qu = q[urows, cols]
            gu = gctx[urows, cols]
            offsets = [
                pl.ds(pl.multiple_of((rows - unit) + u * unit - ws - jb * unit, LANES), unit) for jb in range(UNITS - 1)
            ]
            qs = apart_heads(qu, lane, head)
            gs = apart_heads(gu, lane, head)
            rel = jnp.concatenate([jnp.concatenate([base[sub, :, o] for o in offsets], axis=0) for sub in range(2)], axis=1)
            lses = jnp.concatenate([lse[2 * hp + sub, :, urows] for sub in range(2)], axis=1)
            deltas = jnp.concatenate([delta_t[2 * hp + sub, :, urows] for sub in range(2)], axis=1)
            p = jnp.exp(nt(kk, qs) + rel + mask - lses)
            ds = (p * (nt(vv, gs) - deltas)).astype(BF16)
            gv[win, :] += nn(p.astype(BF16), gs)
            gk[win, :] += nn(ds, qs)
            gq = nn(kt[:, win], ds)
            d32 = ds.astype(F32)
            for sub in range(2):
                for jb, o in enumerate(offsets):
                    gbase[sub, :, o] += d32[jb * unit : (jb + 1) * unit, sub * unit : (sub + 1) * unit]
            gq_t = jnp.where(sub_lane < head, gq[:, :unit], gq[:, unit:])
            dqkv[urows, pl.ds(here, LANES)] = jnp.transpose(gq_t).astype(BF16) * BF16(head**-0.5)
        dqkv[:, pl.ds(span + here, LANES)] = gk[...].astype(BF16)
        dqkv[:, pl.ds(2 * span + here, LANES)] = gv[...].astype(BF16)
        for sub in range(2):
            grow_out[pl.ds(2 * step + sub, 1), :] = unskewed_sum(gbase[sub], unit)
        return carry

    grow_out[...] = jnp.zeros_like(grow_out)
    lax.fori_loop(0, count, pair, 0)
    at_columns = first * head
    grad_in = gin[...] if first else jnp.zeros((rows, width), F32)
    for part in range(3):
        d = dqkv[:, part * span : (part + 1) * span]
        grad_in = grad_in + nt(d, weight(w, slice(part * width + at_columns, part * width + at_columns + span)))
    grads = [(tn(nin[...], dqkv[...]), slice(0, 3 * span))]
    if first == 0:
        grads.append((tn(ctx[...], gatt[...].astype(BF16)), slice(3 * span, 3 * span + width)))
    for g, columns in grads:
        if crossed:
            put_blocks(core, place, row_blocks(g, rows_d), send, keep, columns)
        else:
            keep[:, columns] = g.astype(BF16)
    sums = [jnp.sum(dqkv[:, at : at + span].astype(F32), axis=0, keepdims=True) for at in (0, 2 * span)]
    gvec_out[...] = jnp.zeros_like(gvec_out)
    gvec_out[2:4, 0:span] = jnp.concatenate(sums, axis=0)
    if not last:
        gin_out[...] = grad_in
        return
    n, r = normalise(frames[...].astype(F32))
    gin_out[...] = (gatt[...] + norm_backward(n, r, vec[0:1, :], grad_in)).astype(BF16)
    gvec_out[0:1, :] = jnp.sum(grad_in * n, axis=0, keepdims=True)
    gvec_out[1:2, :] = jnp.sum(grad_in, axis=0, keepdims=True)
    if crossed:
        at = 0
        for vectors, _, c in before:
            gvec_out[2:4, at : at + c * LANES] = vectors[2:4, 0 : c * LANES]
            at += c * LANES
        gvec_out[2:4, at_columns : at_columns + span] = jnp.concatenate(sums, axis=0)
        gvec_out[4:8, :] = gvec2[0:4, :]
        grows = jnp.concatenate([grow[0 : 2 * c, :] for _, grow, c in before] + [grow_out[0 : 2 * count, :]], axis=0)
        small_blocks(
            core, place, gvec_out[...], jnp.broadcast_to(gb_inner[...], (8, gb_inner.shape[1])), grows, bucket_rev,
            send, keep, slice(3 * span, 3 * span + LANES), rows_d, gb_inner.shape[1] // len(place),
        )


def run_kernel(order, kernel, name, scalars, arrays, outs, scratch=(), spare=10, us=100, pin_in=True, pin_out=True, hbm_in=(), hbm_out=()):
    spec = pl.BlockSpec(memory_space=pltpu.VMEM)
    smem = pl.BlockSpec(memory_space=pltpu.SMEM)
    arrays = order.after(*arrays)
    arrays = [
        pltpu.with_memory_space_constraint(a, pltpu.VMEM if pin_in and i not in hbm_in else pltpu.HBM)
        for i, a in enumerate(arrays)
    ]
    limit = spare * MIB + sum(math.prod(b.shape) * jnp.dtype(b.dtype).itemsize for b in scratch)
    out = pl.pallas_call(
        kernel,
        in_specs=[smem] * len(scalars) + [spec] * len(arrays),
        out_specs=[spec] * len(outs),
        out_shape=[
            (pltpu.VMEM if pin_out and i not in hbm_out else jax.ShapeDtypeStruct)(s, d) for i, (s, d) in enumerate(outs)
        ],
        scratch_shapes=list(scratch),
        compiler_params=pltpu.CompilerParams(vmem_limit_bytes=limit),
        cost_estimate=pl.CostEstimate(flops=us * 1_000_000_000, bytes_accessed=us * 1_000_000, transcendentals=0),
        name=name,
    )(*scalars, *arrays)
    order.did(out[0])
    return out


def on_device(
    frames, ln1_gain, ln1_shift, w_query, b_query, w_key, w_value, b_value, w_out, b_out, ln2_gain, ln2_shift,
    w_inner, b_inner, w_outer, b_outer, bias_table, layout, valid, rel_index, cotangent, *, n,
):
    rows, width = frames.shape
    rows_d = w_query.shape[0]
    rows_ff = w_outer.shape[0]
    ff = w_inner.shape[1]
    span = rel_index.shape[0] + 1
    unit = rows // UNITS
    per_table = bias_table.shape[0]
    plan = plan_tables(n)
    core, chips, place = plan
    order = Order()
    direct = (
        rows_d % 8 == 0 and rows_d >= 24 and rows_ff == 4 * rows_d and max(rows_d, rows_ff, per_table) <= LANES and per_table % HEADS == 0
    )
    crossed = tuple(crossed_places(n)) if direct else ()
    crossed_outer = tuple(crossed_places(n, "outer")) if direct else ()
    unit_half = rows_ff // 2
    apart = [(d * rows_ff + h * unit_half, h * ff // 2 + d * unit_half, unit_half) for h in range(2) for d in range(n)]
    together = [(b, a, c) for a, b, c in apart]
    meta = [layout, valid.reshape(-1), core[None]]
    if direct:
        _, chips_outer, place_outer = plan_tables(n, "outer")
        meta += [chips, chips_outer, place, place_outer]
    meta = jnp.concatenate(meta).astype(jnp.int32)
    small_d = jnp.stack([ln1_gain, ln1_shift, b_query, b_value, b_out, ln2_gain, ln2_shift, b_outer])

    base = pltpu.VMEM((2, unit, span), F32)
    masks = pltpu.VMEM((UNITS, rows - unit, unit), F32)
    if direct:
        vectors = (ln1_gain, ln1_shift, b_query, b_value, b_out, ln2_gain, ln2_shift, b_outer, b_inner, bias_table)
        (part1,) = run_kernel(
            Order(), functools.partial(pack_first_kernel, rows_ff=rows_ff), "pack_first", [],
            [w_query, w_key, w_value, *(v[None] for v in vectors)], [((1, rows_d, 3 * width + LANES), BF16)],
            [pltpu.VMEM((rows_d, LANES), F32)], spare=4, pin_in=False,
        )
        g1 = Gather(part1, n, order)
        part2, part3 = run_kernel(
            order, functools.partial(pack_feed_kernel, moves=apart), "pack_feed", [], [w_inner, w_outer, w_out],
            [((1, rows_d, ff + width), BF16), ((1, rows_d, ff), BF16)], spare=4, pin_in=False,
        )
        g3 = Gather(part3, n, order, "outer")
        (part2,) = lax.optimization_barrier((part2, g1.got))[:1]
        g2 = Gather(part2, n, order)
        (g2.got,) = lax.optimization_barrier((g2.got, g3.got))[:1]
        for g in (g1, g1, g2, g1, g2, g3):
            g.step()
        (g2.got,) = lax.optimization_barrier((g2.got, g1.got))[:1]
        for g in (g2, g3):
            g.step()
        first = g1.finish()
        each = per_table // HEADS
        index = jnp.stack([rel_index // each, rel_index % each])
        bucket_rev = jnp.pad(index[:, ::-1], ((0, 6), (0, 1)), constant_values=-1)
        q, k, v, nin, w1, vec, inner_bias, bias_rev = run_kernel(
            order, functools.partial(project_kernel, crossed=crossed, rows_d=rows_d, rows_ff=rows_ff), "project", [meta],
            [frames, *first, bucket_rev],
            [((rows, width), BF16)] * 4
            + [((n // 2, 2 * rows_d, 3 * width), BF16), ((8, width), F32), ((1, ff), F32), ((16, span), F32)],
            [
                pltpu.VMEM((width // LANES + 1, 8, LANES), F32),
                pltpu.VMEM((ff // LANES + 1, 8, LANES), F32),
                pltpu.VMEM((n, LANES), F32),
            ],
            us=1, hbm_in=(0,),
        )
        chunk = [[((n // 2, rows_d, c), BF16)] * 2 for c in (ff, ff)]
        w_out_whole = [((n // 2, 2 * rows_d, width), BF16)]
        unpacked = [pltpu.VMEM((n // 2, 2 * rows_d, width), BF16), pltpu.VMEM((n // 2, rows_ff, width), BF16)]
    else:
        flat = jnp.concatenate([small_d.reshape(-1), b_inner, bias_table])
        per = flat.shape[0] // rows_d
        small = jnp.pad(flat.reshape(rows_d, per), ((0, 0), (0, LANES - per)))
        w1 = gathered(Gather(jnp.concatenate([w_query, w_key, w_value, small], axis=1), n, order).finish(), plan, n)
        w2 = (gathered(Gather(jnp.concatenate([w_inner, w_out], axis=1), n, order).finish(), plan, n),)
        w2 += (gathered(Gather(w_outer, n, order).finish(), plan, n),)
        flats = w1[:, 3 * width : 3 * width + per].reshape(n, rows_d * per)
        vec = flats[:, : 8 * rows_d].reshape(n, 8, rows_d).transpose(1, 0, 2).reshape(8, width).astype(F32)
        inner_bias = flats[:, 8 * rows_d : 8 * rows_d + rows_ff].reshape(1, ff).astype(F32)
        table = jnp.pad(flats[:, 8 * rows_d + rows_ff :].reshape(-1, HEADS), ((0, 0), (0, 16 - HEADS)))
        index_rev = jnp.pad(rel_index[::-1], (0, 1), constant_values=-1)
        ids = jnp.arange(table.shape[0], dtype=jnp.int32)[:, None]
        bias_rev = tn(table, (ids == index_rev[None]).astype(BF16))
        q, k, v, nin = run_kernel(
            order, project_body, "project", [meta], [frames, w1, vec], [((rows, width), BF16)] * 4
        )
        chunk = [[((8, LANES), BF16), ((c, max(width, ff // 2), max(width, ff // 2)), BF16)] for c in (2, 2)]
        w_out_whole = []
        unpacked = []

    ctx, lse = run_kernel(
        order, attend_kernel, "attend", [meta], [q, k, v, bias_rev],
        [((rows, width), BF16), ((HEADS, 1, rows), F32)], [base, pltpu.VMEM((LANES, rows), BF16), masks], spare=4, us=1,
    )

    def start(send, keep, scatter):
        return scatter.add(*((send, keep) if direct else split_natural(keep, plan, n)))

    if direct:
        g3.step()
        w2 = g2.finish()
    att, nmid, acc, gmid, gb1, send1, keep1, *w_out_all = run_kernel(
        order, functools.partial(feed_first_kernel, crossed=crossed, rows_d=rows_d), "feed_first", [meta],
        [frames, ctx, vec, inner_bias, cotangent, *w2],
        [((rows, width), F32), ((rows, width), BF16), ((rows, width), F32), ((rows, width), F32), ((1, ff // 2), F32)]
        + chunk[0] + w_out_whole,
        unpacked, spare=12,
    )
    if direct:
        w3 = g3.finish()
        begin = functools.partial(Scatter, n, order)
        sum_1 = begin("outer").add(send1, keep1)
    else:
        w3 = w2
    mixed, gatt, gctx, send2, keep2, gb2, gvec2 = run_kernel(
        order, functools.partial(feed_second_kernel, crossed=crossed_outer, rows_d=rows_d), "feed_second", [meta],
        [att, nmid, acc, gmid, ctx, vec, inner_bias, cotangent, *w_out_all, *w3],
        [((rows, width), BF16), ((rows, width), F32), ((rows, width), BF16)] + chunk[1]
        + [((1, ff // 2), F32), ((8, width), F32)],
        [pltpu.VMEM((rows, width), F32)] * 2 + unpacked, spare=12, hbm_out=(0,),
    )
    gb_inner = jnp.concatenate([gb1, gb2], axis=1)
    if direct:
        sum_1.step(2)
        sum_2 = begin().add(send2, keep2)
    else:
        whole_inner = jnp.concatenate([keep1[0, :width, : ff // 2], keep2[0, :width, : ff // 2]], axis=1)
        whole_outer = jnp.concatenate([keep1[1, : ff // 2, :width], keep2[1, : ff // 2, :width]], axis=0)
        begin = functools.partial(Scatter, n, order)
        sum_1 = begin().add(*split_natural(whole_outer, plan, n))
        sum_2 = begin().add(*split_natural(whole_inner, plan, n))

    counts = COUNTS
    passed = gatt
    done, earlier = [], []
    sum_early, sum_late = begin(), begin()
    for call, count in enumerate(counts):
        cols = count * LANES
        last = call == len(counts) - 1
        wide = 3 * cols + LANES * (last and direct) + width * (call == 0)
        part = [((n // 2, rows_d, wide), BF16)] * 2 if direct else [((8, LANES), BF16), ((width, wide), BF16)]
        extra = [gvec2, gb_inner, bucket_rev] + [a for pair in earlier for a in pair] if last and direct else []
        send, keep, passed, gvec1, grow = run_kernel(
            order,
            functools.partial(
                attend_back_kernel, crossed=crossed, rows_d=rows_d, counts=counts[:call], count=count
            ),
            "attend_back", [meta],
            [q, k, v, lse, ctx, gctx, bias_rev, nin, frames, gatt, passed, w1, vec] + extra,
            part + [((rows, width), BF16 if last else F32), ((8, width), F32), ((8, span), F32)],
            [
                base, base,
                pltpu.VMEM((HEADS, 1, rows), F32),
                pltpu.VMEM((LANES, rows), BF16),
                pltpu.VMEM((rows, 3 * cols), BF16),
                pltpu.VMEM((rows, LANES), F32),
                pltpu.VMEM((rows, LANES), F32),
                masks,
            ],
            spare=10, hbm_out=(2,) if last else (),
        )
        earlier.append((gvec1, grow))
        start(send, keep, sum_late if call else sum_early)
        if call == 0:
            sum_1.step()
            sum_2.step()
    for each_sum in (sum_early, sum_1, sum_2, sum_late, sum_early, sum_1, sum_2, sum_late, sum_early, sum_2, sum_late, sum_early, sum_late):
        if each_sum.steps:
            each_sum.step()
    sum_1, sum_2, early, late = sum_1.finish(), sum_2.finish(), sum_early.finish(), sum_late.finish()
    if direct:
        grad_inner, grad_outer, grad_w_out = run_kernel(
            Order(), functools.partial(feed_columns_kernel, moves=together), "feed_columns", [], [sum_1, sum_2, early],
            [((rows_d, ff), F32), ((rows_ff, width), F32), ((rows_d, width), F32)], spare=4, pin_out=False,
        )
    else:
        grad_inner, grad_outer = sum_2[:, :ff], sum_1
        grad_w_out = early[:, 3 * LANES * counts[0] :]
    if direct:
        sum_q, sum_k, sum_v, sum_b_inner, sum_table, *vecs = run_kernel(
            Order(), functools.partial(columns_kernel, counts=counts), "columns", [], [early, late],
            [((rows_d, width), F32)] * 3 + [((rows_ff,), F32), ((per_table,), F32)] + [((rows_d,), F32)] * 8,
            spare=4, pin_out=False,
        )
    else:
        places = [3 * LANES * sum(counts[1:call]) for call in range(len(counts))]
        calls = list(zip([early] + [late] * len(counts[1:]), places, [c * LANES for c in counts]))
        sum_q, sum_k, sum_v = (
            jnp.concatenate([p[:, at + i * cols : at + (i + 1) * cols] for p, at, cols in calls], axis=1) for i in range(3)
        )
        hot_rev = (ids == index_rev[None]).astype(F32)
        grow = jnp.concatenate([g[: 2 * c] for (_, g), c in zip(earlier, counts)])
        gtable = lax.dot_general(
            hot_rev, grow, (((1,), (1,)), ((), ())), precision=lax.Precision.HIGHEST, preferred_element_type=F32
        )
        gbias = jnp.concatenate([g[2:4, : c * LANES] for (g, _), c in zip(earlier, counts)], axis=1)
        gsmall = jnp.concatenate([gvec1[0:2], gbias, gvec2[0:4]])
        gsmall = gsmall.reshape(8, n, rows_d).transpose(1, 0, 2).reshape(n, 8 * rows_d)
        gflat = jnp.concatenate([gsmall, gb_inner.reshape(n, rows_ff), gtable.reshape(n, -1)], axis=1)
        gflat = jnp.pad(gflat, ((0, 0), (0, -gflat.shape[1] % LANES))).astype(BF16)
        sum_flat = Scatter(n, order).add(*split_natural(gflat, plan, n)).finish()[0]
        vecs = sum_flat[: 8 * rows_d].reshape(8, rows_d)
        sum_b_inner = sum_flat[8 * rows_d : 8 * rows_d + rows_ff]
        sum_table = sum_flat[8 * rows_d + rows_ff : 8 * rows_d + rows_ff + per_table]
    return (
        mixed, passed, vecs[0], vecs[1], sum_q, vecs[2], sum_k, sum_v, vecs[3],
        grad_w_out, vecs[4], vecs[5], vecs[6], grad_inner, sum_b_inner, grad_outer, vecs[7], sum_table,
    )


def solution(mesh):
    row, two = P("dp"), P("dp", None)
    in_specs = (two, row, row, two, row, two, two, row, two, row, row, row, two, row, two, row, row, row, two, P(), two)
    out_specs = (two, two, row, row, two, row, two, two, row, two, row, row, row, two, row, two, row, row)
    return jax.shard_map(
        functools.partial(on_device, n=mesh.shape["dp"]),
        mesh=mesh, in_specs=in_specs, out_specs=out_specs, check_vma=False,
    )
```
